32 devices in a mesh: depth: 4 (over y, x), rows: 8 (over z, core).
Axes of the slice: x: 2, y: 2, z: 4, core: 2. Of those that a mesh axis runs over, the one named last changes fastest.
Arguments:
- tokens: bfloat16 [16, 1024, 1152], P('depth', 'rows'), may hold values from -6 to 6
- cotangent: bfloat16 [16, 1024, 1152], P('depth', 'rows'), may hold values from -6 to 6
- exit_depth: int32 [16, 1024], P('depth', 'rows'), may hold values from 0 to 3
- lengths: int32 [16], replicated, may hold values from 256 to 1024, as said below
- loop_index: int32 [16], replicated, may hold values from 0 to 3, as said below
- attn_gain: bfloat16 [1152], P(('depth', 'rows')), may hold values from 0.099609375 to 1.8984375
- mlp_gain: bfloat16 [1152], P(('depth', 'rows')), may hold values from 0.099609375 to 1.8984375
- qkv_weight: bfloat16 [1152, 1536], P(('depth', 'rows')), may hold values from -0.1875 to 0.1875
- out_weight: bfloat16 [1024, 1152], P(('depth', 'rows')), may hold values from -0.5 to 0.5
- gateup_weight: bfloat16 [1152, 13824], P(('depth', 'rows')), may hold values from -0.1875 to 0.1875
- down_weight: bfloat16 [6912, 1152], P(('depth', 'rows')), may hold values from -0.078125 to 0.078125
- qkv_enter: bfloat16 [4, 1152, 768], P('depth', 'rows'), may hold values from -0.1875 to 0.1875
- query_leave: bfloat16 [4, 256, 1024], P('depth', 'rows'), may hold values from -0.375 to 0.375
- kv_leave: bfloat16 [4, 256, 512], P('depth', 'rows'), may hold values from -0.375 to 0.375
- out_enter: bfloat16 [4, 1024, 256], P('depth', 'rows'), may hold values from -0.5 to 0.5
- out_leave: bfloat16 [4, 256, 1152], P('depth', 'rows'), may hold values from -0.375 to 0.375
- gateup_enter: bfloat16 [4, 1152, 512], P('depth', 'rows'), may hold values from -0.1875 to 0.1875
- gateup_leave: bfloat16 [4, 256, 13824], P('depth', 'rows'), may hold values from -0.375 to 0.375
- down_enter: bfloat16 [4, 6912, 256], P('depth', 'rows'), may hold values from -0.078125 to 0.078125
- down_leave: bfloat16 [4, 256, 1152], P('depth', 'rows'), may hold values from -0.375 to 0.375
Outputs:
- activations: bfloat16 [16, 1024, 1152], P('depth', 'rows')
- grad_tokens: bfloat16 [16, 1024, 1152], P('depth', 'rows')
- exit_counts: int32 [4], replicated
- confidence: float32 [], replicated
- grad_attn_gain: float32 [1152], P(('depth', 'rows'))
- grad_mlp_gain: float32 [1152], P(('depth', 'rows'))
- grad_qkv_weight: float32 [1152, 1536], P(('depth', 'rows'))
- grad_out_weight: float32 [1024, 1152], P(('depth', 'rows'))
- grad_gateup_weight: float32 [1152, 13824], P(('depth', 'rows'))
- grad_down_weight: float32 [6912, 1152], P(('depth', 'rows'))
- grad_qkv_enter: float32 [4, 1152, 768], P('depth', 'rows')
- grad_query_leave: float32 [4, 256, 1024], P('depth', 'rows')
- grad_kv_leave: float32 [4, 256, 512], P('depth', 'rows')
- grad_out_enter: float32 [4, 1024, 256], P('depth', 'rows')
- grad_out_leave: float32 [4, 256, 1152], P('depth', 'rows')
- grad_gateup_enter: float32 [4, 1152, 512], P('depth', 'rows')
- grad_gateup_leave: float32 [4, 256, 13824], P('depth', 'rows')
- grad_down_enter: float32 [4, 6912, 256], P('depth', 'rows')
- grad_down_leave: float32 [4, 256, 1152], P('depth', 'rows')
The draws below stay inside these ranges and needn't reach their ends.
Inputs may be any that keep to these rules, and one draw needn't show every extreme that they name: `loop_index`: each aligned block of 4 entries is a permutation of the loops 0 to 3. `lengths`: for every loop, at least one of the sequence slots with that loop index has length 1024.
All inputs are finite; a program needn't handle non-finite values.
Results may differ from the reference program's by a relative error of at most 0.028.
Values may be sent and summed in bfloat16 or wider, within the bound.
No kernel may reach another device: no remote copies, remote signals or barrier semaphores. Data moves between devices by JAX's collectives and lax.ppermute only.
A program may use at most 240 MiB of HBM per device.

```python
import math
import jax
import jax.numpy as jnp
from jax import lax

D = 1152
HD = 256
FF = 6912
RANK = 256
LOOPS = 4
QW = 1024
QKV = 1536
SEQ = 1024
SLOTS = 16
N_DEPTH = 4


def route_draws(key):
    base = jax.random.fold_in(key, 11)
    perm_key, pick_key, size_key = jax.random.split(base, 3)
    orders = jnp.stack([jax.random.permutation(jax.random.fold_in(perm_key, index), LOOPS) for index in range(LOOPS)])
    orders = orders.astype(jnp.int32)
    chooser = jax.random.randint(pick_key, (LOOPS,), 0, LOOPS).astype(jnp.int32)
    sizes = jax.random.randint(size_key, (LOOPS, LOOPS), SEQ // 4, SEQ + 1).astype(jnp.int32)
    source = jnp.arange(LOOPS, dtype=jnp.int32)[:, None] * jnp.ones((1, LOOPS), jnp.int32)
    chosen = jnp.take(chooser, orders)
    sizes = jnp.where(source == chosen, SEQ, sizes)
    return (orders.reshape(-1).astype(jnp.int32), sizes.reshape(-1).astype(jnp.int32))


def draw_loop_index(key, part):
    orders, sizes = route_draws(key)
    return orders


def draw_lengths(key, part):
    orders, sizes = route_draws(key)
    return sizes


def set_ends(values, key, smallest, largest):
    spot = [jax.random.randint(jax.random.fold_in(key, axis), (), 0, length) for axis, length in enumerate(values.shape)]
    longest = values.shape.index(max(values.shape))
    neighbour = spot[:longest] + [(spot[longest] + 1) % values.shape[longest]] + spot[longest + 1:]
    return values.at[tuple(spot)].set(smallest).at[tuple(neighbour)].set(largest)


def block_scale(key, dims, shards, least, top_value):
    loudness, own = 1.0, jax.random.fold_in(key, 6)
    for dim, parts in shards:
        draws = jnp.exp(jax.random.uniform(jax.random.fold_in(own, dim), (parts,), jnp.float32, least / len(shards), top_value / len(shards)))
        loudness = loudness * jnp.repeat(draws, dims[dim] // parts).reshape([-1 if axis == dim else 1 for axis in range(len(dims))])
    return loudness


def normal_values(key, dims, scale, reach, cuts=(), kind=jnp.bfloat16):
    entries = scale * jax.random.normal(key, dims, jnp.float32)
    if cuts:
        entries = entries * block_scale(key, dims, cuts, -0.22, 0.18)
    return jnp.clip(entries, -reach, reach).astype(kind)


def setup_inputs(seed: int = 0) -> dict:
    seeds = jax.random.split(jax.random.key(seed), 21)
    tokens = normal_values(seeds[0], (SLOTS, SEQ, D), 1.0, 6.0, ((0, 4), (1, 8)))
    cotangent = normal_values(seeds[1], (SLOTS, SEQ, D), 1.0, 6.0, ((0, 4), (1, 8)))
    exit_depth = set_ends(jax.random.randint(seeds[2], (SLOTS, SEQ), 0, LOOPS), jax.random.fold_in(seeds[2], 1), 0, LOOPS - 1).astype(jnp.int32)
    lengths = draw_lengths(jax.random.fold_in(seeds[20], 71), 0)
    loop_index = draw_loop_index(jax.random.fold_in(seeds[20], 71), 0)
    attn_gain = jnp.clip(1.0 + 0.18 * jax.random.normal(seeds[5], (D,), jnp.float32), 0.099609375, 1.8984375).astype(jnp.bfloat16)
    mlp_gain = jnp.clip(1.0 + 0.18 * jax.random.normal(seeds[6], (D,), jnp.float32), 0.099609375, 1.8984375).astype(jnp.bfloat16)
    qkv_weight = normal_values(seeds[7], (D, QKV), D ** -0.5, 0.1875, ((0, 32),))
    out_weight = normal_values(seeds[8], (QW, D), (QW // 8) ** -0.5, 0.5, ((0, 32),))
    gateup_weight = normal_values(seeds[9], (D, 2 * FF), D ** -0.5, 0.1875, ((0, 32),))
    down_weight = normal_values(seeds[10], (FF, D), FF ** -0.5, 0.078125, ((0, 32),))
    qkv_enter = normal_values(seeds[11], (LOOPS, D, 3 * RANK), D ** -0.5, 0.1875, ((0, 4), (1, 8)))
    query_leave = normal_values(seeds[12], (LOOPS, RANK, QW), RANK ** -0.5, 0.375, ((0, 4), (1, 8)))
    kv_leave = normal_values(seeds[13], (LOOPS, RANK, 2 * HD), RANK ** -0.5, 0.375, ((0, 4), (1, 8)))
    out_enter = normal_values(seeds[14], (LOOPS, QW, RANK), (QW // 8) ** -0.5, 0.5, ((0, 4), (1, 8)))
    out_leave = normal_values(seeds[15], (LOOPS, RANK, D), RANK ** -0.5, 0.375, ((0, 4), (1, 8)))
    gateup_enter = normal_values(seeds[16], (LOOPS, D, 2 * RANK), D ** -0.5, 0.1875, ((0, 4), (1, 8)))
    gateup_leave = normal_values(seeds[17], (LOOPS, RANK, 2 * FF), RANK ** -0.5, 0.375, ((0, 4), (1, 8)))
    down_enter = normal_values(seeds[18], (LOOPS, FF, RANK), FF ** -0.5, 0.078125, ((0, 4), (1, 8)))
    down_leave = normal_values(seeds[19], (LOOPS, RANK, D), RANK ** -0.5, 0.375, ((0, 4), (1, 8)))
    return dict(tokens=tokens, cotangent=cotangent, exit_depth=exit_depth, lengths=lengths, loop_index=loop_index, attn_gain=attn_gain, mlp_gain=mlp_gain, qkv_weight=qkv_weight, out_weight=out_weight, gateup_weight=gateup_weight, down_weight=down_weight, qkv_enter=qkv_enter, query_leave=query_leave, kv_leave=kv_leave, out_enter=out_enter, out_leave=out_leave, gateup_enter=gateup_enter, gateup_leave=gateup_leave, down_enter=down_enter, down_leave=down_leave)


@jax.custom_vjp
def low(v):
    return lax.optimization_barrier(v.astype(jnp.bfloat16)).astype(jnp.float32)

@jax.custom_vjp
def low_back(v):
    return v

def low_keep(v):
    return (low(v), None)

def low_pass(kept, grad):
    return (grad,)

def back_keep(v):
    return (v, None)

def back_low(kept, grad):
    return (low(grad),)
low.defvjp(low_keep, low_pass)
low_back.defvjp(back_keep, back_low)

def product(left, right):
    return jnp.dot(left, right, precision=lax.Precision.HIGHEST)

def rms_scale(values, gain):
    return values * lax.rsqrt(lax.optimization_barrier(jnp.mean(values * values, axis=-1, keepdims=True)) + 1e-06) * gain

def angles(positions, size):
    freqs = jnp.exp(jnp.arange(size // 2, dtype=jnp.float32) * (-2.0 * math.log(10000.0) / size))
    phase = positions[:, None] * freqs[None, :]
    return (jnp.cos(phase), jnp.sin(phase))

def rotate(values, cosine, sine):
    half = values.shape[-1] // 2
    first = values[..., :half]
    second = values[..., half:]
    return jnp.concatenate([first * cosine - second * sine, second * cosine + first * sine], axis=-1)

def sequence_layer(inputs, length, params):
    gain_one, gain_two, qkv_weight, out_weight, gateup_weight, down_weight, qkv_enter, query_leave, kv_leave, out_enter, out_leave, gateup_enter, gateup_leave, down_enter, down_leave = params
    seq = inputs.shape[0]
    width_q = out_weight.shape[0]
    head = kv_leave.shape[1] // 2
    heads = width_q // head
    rank = query_leave.shape[0]
    hidden_units = down_weight.shape[0]
    normed_one = low(rms_scale(inputs, gain_one))
    joined = product(normed_one, qkv_weight)
    middle_one = low_back(low(product(normed_one, qkv_enter)))
    query_pre = low_back(joined[:, :width_q] + product(middle_one[:, :rank], query_leave))
    key_pre = low_back(joined[:, width_q:width_q + head] + product(middle_one[:, rank:2 * rank], kv_leave[:, :head]))
    value_pre = low_back(joined[:, width_q + head:] + product(middle_one[:, 2 * rank:], kv_leave[:, head:]))
    index = jnp.arange(seq, dtype=jnp.int32)
    cosine, sine = angles(index.astype(jnp.float32), head)
    queries = low(rotate(query_pre.reshape(seq, heads, head), cosine[:, None, :], sine[:, None, :]))
    keys = low(rotate(key_pre, cosine, sine))
    values = low(value_pre)
    scores = low_back(jnp.einsum('shd,td->hst', queries, keys, precision=lax.Precision.HIGHEST) * head ** (-0.5))
    allowed = (index[None, :] <= index[:, None]) & (index[None, :] < length)
    masked = jnp.where(allowed[None], scores, -1e+30)
    highest = lax.optimization_barrier(jnp.max(masked, axis=-1, keepdims=True))
    log_total = highest + jnp.log(lax.optimization_barrier(jnp.sum(jnp.exp(masked - highest), axis=-1, keepdims=True)))
    probs = jnp.exp(masked - log_total)
    attended = jnp.einsum('hst,td->shd', low(probs), values, precision=lax.Precision.HIGHEST)
    attended = low_back(low(attended.reshape(seq, width_q)))
    middle_two = low_back(low(product(attended, out_enter)))
    branch = low_back(product(attended, out_weight) + product(middle_two, out_leave))
    mixed = inputs + branch
    normed_two = low(rms_scale(mixed, gain_two))
    expanded = product(normed_two, gateup_weight)
    middle_three = low_back(low(product(normed_two, gateup_enter)))
    gate = low_back(expanded[:, :hidden_units] + product(middle_three[:, :rank], gateup_leave[:, :hidden_units]))
    upper = low_back(expanded[:, hidden_units:] + product(middle_three[:, rank:], gateup_leave[:, hidden_units:]))
    hidden = low(jax.nn.gelu(gate) * upper)
    middle_four = low_back(low(product(hidden, down_enter)))
    outcome = low_back(product(hidden, down_weight) + product(middle_four, down_leave))
    return mixed + outcome

def reference(tokens, cotangent, exit_depth, lengths, loop_index, attn_gain, mlp_gain, qkv_weight, out_weight, gateup_weight, down_weight, qkv_enter, query_leave, kv_leave, out_enter, out_leave, gateup_enter, gateup_leave, down_enter, down_leave):
    loops = N_DEPTH
    levels = jnp.arange(loops, dtype=jnp.int32)
    table = loop_index.reshape(loops, loops)
    marks = (table[None, :, :] == levels[:, None, None]).astype(jnp.int32)
    column = lax.optimization_barrier(jnp.sum(marks * levels[None, None, :], axis=2))
    route = (levels[None, :] * loops + column).reshape(-1).astype(jnp.int32)
    routed = tokens[route].astype(jnp.float32)
    routed_len = lengths[route]
    depth_of = jnp.repeat(levels, loops).astype(jnp.int32)
    shared = tuple((item.astype(jnp.float32) for item in (attn_gain, mlp_gain, qkv_weight, out_weight, gateup_weight, down_weight)))
    adapters = tuple((item.astype(jnp.float32) for item in (qkv_enter, query_leave, kv_leave, out_enter, out_leave, gateup_enter, gateup_leave, down_enter, down_leave)))

    def forward(routed_in, shared_in, adapters_in):

        def one_sequence(item):
            inputs, length, depth = item
            picked = tuple((lax.dynamic_index_in_dim(entry, depth, 0, keepdims=False) for entry in adapters_in))
            return sequence_layer(inputs, length, shared_in + picked)
        return lax.map(jax.checkpoint(one_sequence), (routed_in, routed_len, depth_of))
    outputs, pull = jax.vjp(forward, routed, shared, adapters)
    grad_routed, grad_shared, grad_adapters = pull(cotangent.astype(jnp.float32))
    grad_tokens = jnp.zeros_like(grad_routed).at[route].set(grad_routed).astype(jnp.bfloat16)
    valid = jnp.arange(SEQ, dtype=jnp.int32)[None, :] < routed_len[:, None]
    exit_counts = lax.optimization_barrier(jnp.sum(((exit_depth[None] == levels[:, None, None]) & valid[None]).astype(jnp.int32), axis=(1, 2))).astype(jnp.int32)
    cross = lax.optimization_barrier(jnp.sum(routed * outputs, axis=-1))
    own_sq = lax.optimization_barrier(jnp.sum(routed * routed, axis=-1))
    out_sq = lax.optimization_barrier(jnp.sum(outputs * outputs, axis=-1))
    cosines = cross * lax.rsqrt(own_sq * out_sq + 1e-06)
    confidence = jnp.sum(jnp.where(valid, cosines, 0.0)) / jnp.sum(lengths).astype(jnp.float32)
    return (outputs.astype(jnp.bfloat16), grad_tokens, exit_counts, confidence, grad_shared[0], grad_shared[1], grad_shared[2], grad_shared[3], grad_shared[4], grad_shared[5], grad_adapters[0], grad_adapters[1], grad_adapters[2], grad_adapters[3], grad_adapters[4], grad_adapters[5], grad_adapters[6], grad_adapters[7], grad_adapters[8])
```

```python
import math

import jax
import jax.numpy as jnp
from jax import lax
from jax.experimental import pallas as pl
from jax.experimental.pallas import tpu as pltpu
from jax.sharding import PartitionSpec as P

BF = jnp.bfloat16
F32 = jnp.float32
ROOT = math.sqrt(2.0 / math.pi)
CUBE = 0.044715


def angles(positions, size):
    freqs = jnp.exp(jnp.arange(size // 2, dtype=F32) * (-2.0 * math.log(10000.0) / size))
    phase = positions[:, None] * freqs[None, :]
    return (jnp.cos(phase), jnp.sin(phase))


def matmul(left, right):
    return jnp.dot(left, right, preferred_element_type=F32)


def outer_sum(left, right):
    return lax.dot_general(left, right, (((0,), (0,)), ((), ())), preferred_element_type=F32)


def through(left, right):
    return lax.dot_general(left, right, (((1,), (1,)), ((), ())), preferred_element_type=F32)


def swap(value, axis, flip):
    size = lax.axis_size(axis)
    return lax.ppermute(value, axis, [(i, i ^ flip) for i in range(size)])


def gather_flips(value, axis, bits):
    parts = {0: value}
    for bit in bits:
        parts.update({flip | bit: swap(part, axis, bit) for flip, part in list(parts.items())})
    return parts


def add_low(left, right):
    return (left.astype(F32) + right.astype(F32)).astype(BF)


def scatter_flips(parts, axis, bits):
    parts = dict(parts)
    for bit in bits:
        kept = {}
        for flip in [f for f in parts if not f & bit]:
            kept[flip] = add_low(parts[flip], swap(parts[flip | bit], axis, bit))
        parts = kept
    return parts[0]


def tie(*values):
    return lax.optimization_barrier(values)


def bits_of(size):
    return [1 << i for i in range(size.bit_length() - 1)]


LANES = 256


def even(height):
    return -(-height // 16) * 16


def segments(shapes):
    out, row = [], 0
    for which, (height, columns) in enumerate(shapes):
        for start in range(0, columns, LANES):
            out.append((which, row, start, min(LANES, columns - start)))
            row += even(height)
    return out, row


def put(out_ref, lead, row, height, value):
    short, narrow = even(height) - height, LANES - value.shape[1]
    if narrow:
        value = jnp.concatenate([value, jnp.zeros((height, narrow), value.dtype)], axis=1)
    if short:
        value = jnp.concatenate([value, jnp.zeros((short, LANES), value.dtype)], axis=0)
    out_ref[lead, row : row + even(height), :] = value


def pack_kernel(shapes, *refs):
    where, _ = segments(shapes)
    for which, row, start, size in where:
        put(refs[-1], 0, row, shapes[which][0], refs[which][:, start : start + size])


def pack_pass(arrays):
    shapes = [array.shape for array in arrays]
    return pl.pallas_call(
        lambda *refs: pack_kernel(shapes, *refs),
        out_shape=jax.ShapeDtypeStruct((1, segments(shapes)[1], LANES), BF),
        compiler_params=MEMORY,
        cost_estimate=FREE,
    )(*arrays)


def unpack_kernel(shapes, terms, *refs):
    where, _ = segments(shapes)
    for which, row, start, size in where:
        height = shapes[which][0]
        out_ref = refs[terms + which]
        for lead in range(refs[0].shape[0]):
            value = refs[0][lead, row : row + height, :size]
            if terms > 1:
                value = value.astype(F32) + refs[1][lead, row : row + height, :size].astype(F32)
            first = lead * height
            out_ref[first : first + height, start : start + size] = value.astype(out_ref.dtype)


def unpack_pass(terms, shapes, dtype):
    lead = terms[0].shape[0]
    return pl.pallas_call(
        lambda *refs: unpack_kernel(shapes, len(terms), *refs),
        out_shape=[jax.ShapeDtypeStruct((lead * h, c), dtype) for h, c in shapes],
        compiler_params=MEMORY,
        cost_estimate=FREE,
    )(*terms)


def spread_rows(pos_ref, out_ref, row, value, first, size):
    leads = out_ref.shape[0]
    height = value.shape[0] // leads
    for lead in range(leads):
        block = value[lead * height : (lead + 1) * height, first : first + size]
        put(out_ref, pos_ref[lead], row, height, block.astype(BF))


def total_of(refs):
    total = refs[0][...].astype(F32)
    for ref in refs[1:]:
        total = total + ref[...].astype(F32)
    return total


def place_all(pos_ref, out_ref, values):
    shapes = [(value.shape[0] // out_ref.shape[0], value.shape[1]) for value in values]
    for which, row, start, size in segments(shapes)[0]:
        spread_rows(pos_ref, out_ref, row, values[which], start, size)


def attn_grads_kernel(bands, pos_ref, *refs):
    grad_ref, enter_ref, leave_ref, out_ref = refs[-4:]
    rank = leave_ref.shape[0]
    values = [total_of(refs[:-4])]
    for start, size in bands:
        values.append(through(grad_ref[:, start : start + size], leave_ref[:, start : start + size]))
    for index, (start, size) in enumerate(bands):
        enter = enter_ref[:, index * rank : (index + 1) * rank]
        values.append(outer_sum(enter, grad_ref[:, start : start + size]))
    place_all(pos_ref, out_ref, values)


def attn_grads_shapes(rows, slab, grad, enter, leave, bands):
    rank = leave.shape[0]
    return (
        [(slab.shape[0] // rows, slab.shape[1])]
        + [(grad.shape[0] // rows, rank)] * len(bands)
        + [(rank // rows, size) for _, size in bands]
    )


def rest_grads_kernel(pos_ref, *refs):
    (
        grad_out_ref,
        out_enter_ref,
        out_leave_ref,
        grad_gateup_ref,
        leave_ref,
        grad_down_ref,
        down_enter_ref,
        out_ref,
    ) = refs[-8:]
    shard = leave_ref.shape[1] // 2
    values = [
        total_of(refs[:-8]),
        through(grad_out_ref[...], out_leave_ref[...]),
        outer_sum(out_enter_ref[...], grad_out_ref[...]),
        through(grad_gateup_ref[:, :shard], leave_ref[:, :shard]),
        through(grad_gateup_ref[:, shard:], leave_ref[:, shard:]),
        outer_sum(down_enter_ref[...], grad_down_ref[...]),
    ]
    place_all(pos_ref, out_ref, values)


def grads_pass(kernel, pos, rows, shapes, arrays):
    whole = [pl.BlockSpec(memory_space=pltpu.VMEM)] * len(arrays)
    shape = (rows, segments(shapes)[1], LANES)
    return pl.pallas_call(
        kernel,
        in_specs=[pl.BlockSpec(memory_space=pltpu.SMEM)] + whole,
        out_specs=pl.BlockSpec(memory_space=pltpu.VMEM),
        out_shape=jax.ShapeDtypeStruct(shape, BF),
        compiler_params=MEMORY,
        cost_estimate=FREE,
    )(pos, *arrays)


def leave_grads_kernel(order_ref, near_ref, far_ref, grad_ref, near_out, far_out):
    near_out[...] = outer_sum(near_ref[...], grad_ref[...]).astype(BF)
    far_out[...] = outer_sum(far_ref[...], grad_ref[...]).astype(BF)


def leave_grads_pass(order, enter, grad):
    width, shard = grad.shape[0], grad.shape[1] // 2
    half = enter.shape[1] // 4
    shape = jax.ShapeDtypeStruct((half, 2 * shard), BF)
    return pl.pallas_call(
        leave_grads_kernel,
        grid_spec=pltpu.PrefetchScalarGridSpec(
            num_scalar_prefetch=1,
            grid=(2,),
            in_specs=[
                pl.BlockSpec((width, half), lambda i, o: (0, 2 * i + o[0])),
                pl.BlockSpec((width, half), lambda i, o: (0, 2 * i + o[1])),
                pl.BlockSpec((width, shard), lambda i, o: (0, i)),
            ],
            out_specs=[pl.BlockSpec((half, shard), lambda i, o: (0, i))] * 2,
        ),
        out_shape=[shape, shape],
        compiler_params=MEMORY,
        cost_estimate=FREE,
    )(order, enter, enter, grad)


def enter_grads_kernel(order_ref, near_ref, far_ref, leave_ref, near_out, far_out):
    near_out[...] = through(near_ref[...], leave_ref[...]).astype(BF)
    far_out[...] = through(far_ref[...], leave_ref[...]).astype(BF)


def enter_grads_pass(order, grad, leave):
    half = grad.shape[0] // 2
    shape = jax.ShapeDtypeStruct((half, leave.shape[0]), BF)
    return pl.pallas_call(
        enter_grads_kernel,
        grid_spec=pltpu.PrefetchScalarGridSpec(
            num_scalar_prefetch=1,
            grid=(1,),
            in_specs=[
                pl.BlockSpec((half, grad.shape[1]), lambda i, o: (o[0], 0)),
                pl.BlockSpec((half, grad.shape[1]), lambda i, o: (o[1], 0)),
                held(leave),
            ],
            out_specs=[pl.BlockSpec(shape.shape, lambda i, o: (0, 0))] * 2,
        ),
        out_shape=[shape, shape],
        compiler_params=MEMORY,
        cost_estimate=FREE,
    )(order, grad, grad, leave)


def split_kernel(piece, padded, in_ref, out_ref):
    team, height, columns = out_ref.shape
    units, shard = in_ref.shape[1] // 2, columns // 2
    gap = jnp.zeros((height, padded - piece), in_ref.dtype)
    for half in range(2):
        for seat in range(team):
            parts = []
            for block in range(shard // padded):
                start = half * units + (block * team + seat) * piece
                parts += [in_ref[:, start : start + piece], gap]
            out_ref[seat, :, half * shard : (half + 1) * shard] = jnp.concatenate(parts, axis=1)


def split_pass(array, team, piece, padded):
    height, columns = array.shape
    shape = (team, height, columns // (team * piece) * padded)
    return pl.pallas_call(
        lambda *refs: split_kernel(piece, padded, *refs),
        out_shape=jax.ShapeDtypeStruct(shape, array.dtype),
        compiler_params=MEMORY,
        cost_estimate=FREE,
    )(array)


def join_kernel(piece, padded, in_ref, out_ref):
    team, height, columns = in_ref.shape
    units, shard = out_ref.shape[1] // 2, columns // 2
    for half in range(2):
        for block in range(shard // padded):
            first = half * shard + block * padded
            parts = [in_ref[seat, :, first : first + piece] for seat in range(team)]
            start = half * units + block * team * piece
            joined = jnp.concatenate(parts, axis=1).astype(F32)
            out_ref[:, start : start + team * piece] = joined


def join_pass(parts, piece, padded):
    team, height, columns = parts.shape
    return pl.pallas_call(
        lambda *refs: join_kernel(piece, padded, *refs),
        out_shape=jax.ShapeDtypeStruct((height, columns // padded * piece * team), F32),
        compiler_params=MEMORY,
        cost_estimate=FREE,
    )(parts)


FREE = pl.CostEstimate(flops=0, transcendentals=0, bytes_accessed=0)
MEMORY = pltpu.CompilerParams(vmem_limit_bytes=60 << 20)


def held(array):
    return pl.BlockSpec(
        array.shape, lambda *_: (0,) * len(array.shape), pipeline_mode=pl.Buffered(1)
    )


def strip(tile, columns):
    return pl.BlockSpec((tile, columns), lambda i: (i, 0))


def mean_scale(values):
    return lax.rsqrt(jnp.mean(values * values, axis=-1, keepdims=True) + 1e-06)


def turned(values, cosine, sine):
    half = values.shape[-1] // 2
    first, second = values[:, :half], values[:, half:]
    return jnp.concatenate(
        [first * cosine - second * sine, second * cosine + first * sine], axis=-1
    )


def enter_kernel(x_ref, gain_ref, weight_ref, cos_ref, sin_ref, n_ref, q_ref, kv_ref):
    head = kv_ref.shape[1] // 2
    width_q = q_ref.shape[1]
    values = x_ref[...].astype(F32)
    normed = (values * mean_scale(values) * gain_ref[...]).astype(BF)
    n_ref[...] = normed
    joined = matmul(normed, weight_ref[...])
    cosine, sine = cos_ref[...], sin_ref[...]
    scale = head ** (-0.5)
    for start in range(0, width_q, head):
        spun = turned(joined[:, start : start + head], cosine, sine)
        q_ref[:, start : start + head] = (spun * scale).astype(BF)
    kv_ref[:, :head] = turned(joined[:, width_q : width_q + head], cosine, sine).astype(BF)
    kv_ref[:, head:] = joined[:, width_q + head :].astype(BF)


def enter_pass(x, gain, weight, cosine, sine, width_q):
    count, width = x.shape
    tile = count // 2
    rest = weight.shape[1] - width_q
    return pl.pallas_call(
        enter_kernel,
        grid=(count // tile,),
        in_specs=[
            strip(tile, width),
            held(gain),
            held(weight),
            strip(tile, cosine.shape[1]),
            strip(tile, cosine.shape[1]),
        ],
        out_specs=[strip(tile, width), strip(tile, width_q), strip(tile, rest)],
        out_shape=[
            jax.ShapeDtypeStruct((count, width), BF),
            jax.ShapeDtypeStruct((count, width_q), BF),
            jax.ShapeDtypeStruct((count, rest), BF),
        ],
        compiler_params=MEMORY,
        cost_estimate=FREE,
    )(x, gain, weight, cosine, sine)


def stack_heads(ref, head):
    return jnp.concatenate(
        [ref[:, start : start + head] for start in range(0, ref.shape[1], head)], axis=0
    )


def allowed_keys(size_ref, pos_ref, key_ref, heads):
    fits = (key_ref[...] <= pos_ref[...]) & (key_ref[...] < size_ref[0])
    return jnp.concatenate([jnp.where(fits, 0.0, -1e30)] * heads, axis=0)


def attend_kernel(size_ref, q_ref, kv_ref, pos_ref, key_ref, o_ref, lse_ref):
    head = kv_ref.shape[1] // 2
    tile = q_ref.shape[0]
    heads = q_ref.shape[1] // head
    scores = through(stack_heads(q_ref, head), kv_ref[:, :head])
    scores = scores + allowed_keys(size_ref, pos_ref, key_ref, heads)
    highest = jnp.max(scores, axis=-1, keepdims=True)
    raised = jnp.exp(scores - highest)
    total = jnp.sum(raised, axis=-1, keepdims=True)
    probs = (raised * (1.0 / total)).astype(BF)
    lse_ref[...] = (highest + jnp.log(total)).reshape(1, heads * tile, 1)
    mixed = matmul(probs, kv_ref[:, head:]).astype(BF)
    for index in range(heads):
        o_ref[:, index * head : (index + 1) * head] = mixed[index * tile : (index + 1) * tile]


def attend_pass(size, q, kv, positions, key_positions, tile):
    count, width_q = q.shape
    heads = 2 * width_q // kv.shape[1]
    steps = count // tile

    def rows(columns):
        return pl.BlockSpec((tile, columns), lambda i, s: (i, 0))

    return pl.pallas_call(
        attend_kernel,
        grid_spec=pltpu.PrefetchScalarGridSpec(
            num_scalar_prefetch=1,
            grid=(steps,),
            in_specs=[rows(width_q), held(kv), rows(1), held(key_positions)],
            out_specs=[rows(width_q), pl.BlockSpec((1, heads * tile, 1), lambda i, s: (i, 0, 0))],
        ),
        out_shape=[
            jax.ShapeDtypeStruct((count, width_q), BF),
            jax.ShapeDtypeStruct((steps, heads * tile, 1), F32),
        ],
        compiler_params=MEMORY,
        cost_estimate=FREE,
    )(size, q, kv, positions, key_positions)


def attend_back_kernel(
    size_ref, q_ref, kv_ref, do_ref, lse_ref, pos_ref, key_ref, cos_ref, sin_ref, dq_ref, dkv_ref, acc
):
    head = kv_ref.shape[1] // 2
    tile = q_ref.shape[0]
    heads = q_ref.shape[1] // head
    step = pl.program_id(0)
    queries = stack_heads(q_ref, head)
    grads = stack_heads(do_ref, head)
    keys = kv_ref[:, :head]
    scores = through(queries, keys) + allowed_keys(size_ref, pos_ref, key_ref, heads)
    probs = jnp.exp(scores - lse_ref[0])
    grad_probs = through(grads, kv_ref[:, head:])
    centre = jnp.sum(probs * grad_probs, axis=-1, keepdims=True)
    grad_scores = (probs * (grad_probs - centre)).astype(BF)
    grad_q = matmul(grad_scores, keys) * (head ** (-0.5))
    cosine, sine = cos_ref[...], -sin_ref[...]
    for index in range(heads):
        spun = turned(grad_q[index * tile : (index + 1) * tile], cosine, sine)
        dq_ref[:, index * head : (index + 1) * head] = spun.astype(BF)
    grad_k = outer_sum(grad_scores, queries)
    grad_v = outer_sum(probs.astype(BF), grads)

    @pl.when(step == 0)
    def _():
        acc[:, :head] = grad_k
        acc[:, head:] = grad_v

    @pl.when(step > 0)
    def _():
        acc[:, :head] += grad_k
        acc[:, head:] += grad_v

    @pl.when(step == pl.num_programs(0) - 1)
    def _():
        dkv_ref[...] = acc[...].astype(BF)


def attend_back_pass(size, q, kv, do, lse, positions, key_positions, cosine, sine, tile):
    count, width_q = q.shape
    heads = 2 * width_q // kv.shape[1]

    def rows(columns):
        return pl.BlockSpec((tile, columns), lambda i, s: (i, 0))

    return pl.pallas_call(
        attend_back_kernel,
        grid_spec=pltpu.PrefetchScalarGridSpec(
            num_scalar_prefetch=1,
            grid=(count // tile,),
            in_specs=[
                rows(width_q),
                held(kv),
                rows(width_q),
                pl.BlockSpec((1, heads * tile, 1), lambda i, s: (i, 0, 0)),
                rows(1),
                held(key_positions),
                rows(cosine.shape[1]),
                rows(cosine.shape[1]),
            ],
            out_specs=[rows(width_q), pl.BlockSpec(kv.shape, lambda i, s: (0, 0))],
            scratch_shapes=[pltpu.VMEM(kv.shape, F32)],
        ),
        out_shape=[jax.ShapeDtypeStruct((count, width_q), BF), jax.ShapeDtypeStruct(kv.shape, BF)],
        compiler_params=MEMORY,
        cost_estimate=FREE,
    )(size, q, kv, do, lse, positions, key_positions, cosine, sine)


def leave_kernel(x_ref, o_ref, weight_ref, gain_ref, h_ref, n_ref):
    mixed = x_ref[...].astype(F32) + matmul(o_ref[...], weight_ref[...])
    h_ref[...] = mixed
    n_ref[...] = (mixed * mean_scale(mixed) * gain_ref[...]).astype(BF)


def leave_pass(x, o, weight, gain):
    count, width = x.shape
    tile = count // 2
    return pl.pallas_call(
        leave_kernel,
        grid=(count // tile,),
        in_specs=[strip(tile, width), strip(tile, o.shape[1]), held(weight), held(gain)],
        out_specs=[strip(tile, width)] * 2,
        out_shape=[jax.ShapeDtypeStruct((count, width), d) for d in (F32, BF)],
        compiler_params=MEMORY,
        cost_estimate=FREE,
    )(x, o, weight, gain)


def norm_grad(grad, values, gain):
    scaling = mean_scale(values)
    unit = values * scaling
    lifted = grad * gain
    back = scaling * (lifted - unit * jnp.mean(lifted * unit, axis=-1, keepdims=True))
    return back, jnp.sum(grad * unit, axis=0, keepdims=True)


def add_step(ref, value):
    @pl.when(pl.program_id(0) == 0)
    def _():
        ref[...] = value

    @pl.when(pl.program_id(0) > 0)
    def _():
        ref[...] += value


def leave_back_kernel(
    one_ref, two_ref, h_ref, gain_ref, dy_ref, weight_ref, dh_ref, dz_ref, do_ref, dgain_ref
):
    grad = one_ref[...].astype(F32) + two_ref[...].astype(F32)
    back, gain_sum = norm_grad(grad, h_ref[...], gain_ref[...])
    total = dy_ref[...].astype(F32) + back
    dh_ref[...] = total
    low = total.astype(BF)
    dz_ref[...] = low
    do_ref[...] = through(low, weight_ref[...]).astype(BF)
    add_step(dgain_ref, gain_sum)


def leave_back_pass(one, two, h, gain, dy, weight):
    count, width = h.shape
    tile = count // 2
    width_q = weight.shape[0]
    return pl.pallas_call(
        leave_back_kernel,
        grid=(count // tile,),
        in_specs=[strip(tile, width)] * 3 + [held(gain), strip(tile, width), held(weight)],
        out_specs=[strip(tile, width)] * 2
        + [strip(tile, width_q), pl.BlockSpec((1, width), lambda i: (0, 0))],
        out_shape=[
            jax.ShapeDtypeStruct((count, width), F32),
            jax.ShapeDtypeStruct((count, width), BF),
            jax.ShapeDtypeStruct((count, width_q), BF),
            jax.ShapeDtypeStruct((1, width), F32),
        ],
        compiler_params=MEMORY,
        cost_estimate=FREE,
    )(one, two, h, gain, dy, weight)


def enter_back_kernel(dq_ref, *refs):
    parts = refs[:-9]
    cos_ref, sin_ref, weight_ref, x_ref, gain_ref, dh_ref, joined_ref, dx_ref, dgain_ref = refs[-9:]
    head = parts[0].shape[1] // 2
    width_q = dq_ref.shape[1]
    pair = parts[0][...].astype(F32)
    for part in parts[1:]:
        pair = pair + part[...].astype(F32)
    joined_ref[:, :width_q] = dq_ref[...]
    spun = turned(pair[:, :head], cos_ref[...], -sin_ref[...])
    joined_ref[:, width_q : width_q + head] = spun.astype(BF)
    joined_ref[:, width_q + head :] = pair[:, head:].astype(BF)
    grad = through(joined_ref[...], weight_ref[...])
    back, gain_sum = norm_grad(grad, x_ref[...].astype(F32), gain_ref[...])
    dx_ref[...] = (dh_ref[...] + back).astype(BF)
    add_step(dgain_ref, gain_sum)


def enter_back_pass(dq, parts, cosine, sine, weight, x, gain, dh):
    count, width = x.shape
    tile = count // 2
    width_q = dq.shape[1]
    return pl.pallas_call(
        enter_back_kernel,
        grid=(count // tile,),
        in_specs=[strip(tile, width_q)]
        + [strip(tile, part.shape[1]) for part in parts]
        + [strip(tile, cosine.shape[1])] * 2
        + [held(weight), strip(tile, width), held(gain), strip(tile, width)],
        out_specs=[
            strip(tile, weight.shape[1]),
            strip(tile, width),
            pl.BlockSpec((1, width), lambda i: (0, 0)),
        ],
        out_shape=[
            jax.ShapeDtypeStruct((count, weight.shape[1]), BF),
            jax.ShapeDtypeStruct((count, width), BF),
            jax.ShapeDtypeStruct((1, width), F32),
        ],
        compiler_params=MEMORY,
        cost_estimate=FREE,
    )(dq, *parts, cosine, sine, weight, x, gain, dh)


def halving_order(bits):
    order = [0]
    for bit in reversed(bits):
        order = order + [flip | bit for flip in order]
    return order


def ff_kernel(n2_ref, df_ref, wg_ref, wd_ref, a_ref, dg_ref, dn_ref):
    hidden = wd_ref.shape[0]
    n2 = n2_ref[...]
    gate = matmul(n2, wg_ref[:, :hidden])
    upper = matmul(n2, wg_ref[:, hidden:])
    grad = through(df_ref[...], wd_ref[...])
    square = gate * gate
    bent = jnp.tanh(gate * (ROOT + ROOT * CUBE * square))
    half = 0.5 + 0.5 * bent
    act = gate * half
    a_ref[...] = (act * upper).astype(BF)
    slope = half + 0.5 * gate * (1.0 - bent * bent) * (ROOT + 3.0 * ROOT * CUBE * square)
    dg_ref[:, :hidden] = (grad * upper * slope).astype(BF)
    dg_ref[:, hidden:] = (grad * act).astype(BF)
    dn_ref[...] = through(dg_ref[...], wg_ref[...]).astype(BF)


def ff_pass(n2, df, wg, wd, tile):
    count, width = n2.shape
    hidden = wd.shape[0]

    return pl.pallas_call(
        ff_kernel,
        grid=(count // tile,),
        in_specs=[strip(tile, width), strip(tile, width), held(wg), held(wd)],
        out_specs=[strip(tile, hidden), strip(tile, 2 * hidden), strip(tile, width)],
        out_shape=[
            jax.ShapeDtypeStruct((count, hidden), BF),
            jax.ShapeDtypeStruct((count, 2 * hidden), BF),
            jax.ShapeDtypeStruct((count, width), BF),
        ],
        compiler_params=MEMORY,
        cost_estimate=FREE,
    )(n2, df, wg, wd)


def fold_kernel(bands, order_ref, *refs):
    slabs, enter_ref, leave_ref, out_ref = refs[:-3], refs[-3], refs[-2], refs[-1]
    rank = leave_ref.shape[0]
    step = pl.program_id(0)
    for index, (start, size) in enumerate(bands):
        lift = matmul(
            enter_ref[:, index * rank : (index + 1) * rank], leave_ref[:, start : start + size]
        )
        for which, slab_ref in enumerate(slabs):

            @pl.when(step == which)
            def _(slab_ref=slab_ref, lift=lift, start=start, size=size):
                part = slab_ref[:, start : start + size].astype(F32)
                out_ref[:, start : start + size] = (part + lift).astype(BF)


def fold(order, slabs, enter, leave, bands):
    height = slabs[0].shape[0]
    columns = leave.shape[1]

    return pl.pallas_call(
        lambda *refs: fold_kernel(bands, *refs),
        grid_spec=pltpu.PrefetchScalarGridSpec(
            num_scalar_prefetch=1,
            grid=(len(slabs),),
            in_specs=[held(slab) for slab in slabs]
            + [pl.BlockSpec((height, enter.shape[1]), lambda i, o: (o[i], 0)), held(leave)],
            out_specs=pl.BlockSpec((height, columns), lambda i, o: (o[i], 0)),
        ),
        out_shape=jax.ShapeDtypeStruct((len(slabs) * height, columns), BF),
        compiler_params=MEMORY,
        cost_estimate=FREE,
    )(order, *slabs, enter, leave)


def per_device(
    tokens,
    cotangent,
    exit_depth,
    lengths,
    loop_index,
    attn_gain,
    mlp_gain,
    qkv_weight,
    out_weight,
    gateup_weight,
    down_weight,
    qkv_enter,
    query_leave,
    kv_leave,
    out_enter,
    out_leave,
    gateup_enter,
    gateup_leave,
    down_enter,
    down_leave,
):
    loops = lax.axis_size("depth")
    rows = lax.axis_size("rows")
    group = lax.axis_index("depth")
    place = lax.axis_index("rows")
    slots, seq_dev, width = tokens.shape
    sub = rows // slots
    team = rows // 2
    count = slots * seq_dev
    across = [[q * sub + u for q in range(slots)] for u in range(sub)]
    teams = [[h * team + k for k in range(team)] for h in range(2)]
    seq_here, mate, core = place // sub, place % sub, place % 2
    side, seat = place // team, place % team
    levels = jnp.arange(loops, dtype=jnp.int32)

    head = kv_leave.shape[2] // 2
    width_q = query_leave.shape[2]
    rank = qkv_enter.shape[2] // 3
    hidden_units = gateup_weight.shape[1] // 2
    piece = down_weight.shape[0]
    padded = -(-piece // 16) * 16
    shard = 2 * loops * padded
    slab = width // (2 * loops)
    gain_size = attn_gain.shape[0]

    def turn(values):
        return jnp.stack(
            [values[0]] + [swap(values[f], "rows", f * sub) for f in range(1, slots)]
        )

    def deal(values):
        return lax.all_to_all(
            values, "rows", split_axis=0, concat_axis=0, axis_index_groups=teams, tiled=True
        )

    def pick(array, index):
        return array.at[index].get(mode="promise_in_bounds")

    def gather_rows(packed):
        return lax.all_gather(packed, "rows", axis=0, tiled=True)

    def band(array, index):
        return array[:, index * rank : (index + 1) * rank]

    depth_flips = [0, 1, 2, 3]
    halves_order = jnp.stack([(group ^ f) * 2 + (core ^ e) for f in depth_flips for e in (0, 1)])

    def half_of(array, which):
        height = array.shape[0] // 2
        return lax.dynamic_slice(array, (which * height, 0), (height, array.shape[1]))

    def fetch_halves(array):
        mine = half_of(array, core)
        return [mine, half_of(array, core ^ 1)] + [swap(mine, "depth", f) for f in depth_flips[1:]]

    def core_halves(parts):
        out = parts[:2]
        for got in parts[2:]:
            out = out + [got, swap(got, "rows", 1)]
        return out

    def split_columns(array):
        return split_pass(array, team, piece, padded)

    def join_columns(parts):
        return join_pass(parts, piece, padded)

    flips = [(d, f) for d in range(4) for f in range(2)]
    slab_order = jnp.stack([(group ^ d) * 2 + (side ^ f) for d, f in flips])

    def by_side(near, far):
        return jnp.where(
            side == 0, jnp.concatenate([near, far]), jnp.concatenate([far, near])
        )

    def positions_of(who):
        blocks = (seq_here ^ levels) * sub + who
        return (blocks[:, None] * seq_dev + jnp.arange(seq_dev, dtype=jnp.int32)[None, :]).reshape(
            count
        )

    table = loop_index.reshape(loops, loops)
    mine = lax.dynamic_index_in_dim(table, group, 0, keepdims=False)
    order = jnp.sum((mine[None, :] == levels[:, None]).astype(jnp.int32) * levels[None, :], axis=1)
    arrived = lax.all_to_all(
        pick(tokens, order), "depth", split_axis=0, concat_axis=0, tiled=True
    )
    sizes_here = jnp.sum(jnp.where(table == group, lengths.reshape(loops, loops), 0), axis=1)
    size_here = lax.dynamic_slice(sizes_here, (seq_here,), (1,))
    positions = positions_of(mate)
    cosine, sine = angles(positions.astype(F32), head)

    gains = jnp.concatenate([attn_gain, mlp_gain])[None]
    gains = jnp.concatenate([gains] + [swap(gains, "depth", f) for f in depth_flips[1:]])
    gains = pick(gains, group ^ levels)
    attn_own = [qkv_weight, qkv_enter[0], query_leave[0], kv_leave[0], gains]
    rest_own = [out_weight, out_enter[0], out_leave[0], gateup_enter[0], down_leave[0]]
    attn_shapes = [array.shape for array in attn_own]
    rest_shapes = [array.shape for array in rest_own]
    attn_packed = gather_rows(pack_pass(attn_own))
    gateup_near = split_columns(gateup_weight)
    down_near = jnp.pad(down_weight, ((0, padded - piece), (0, 0)))
    arrived, gateup_near, down_near = tie(arrived, gateup_near, down_near)
    inputs = turn(pick(arrived, seq_here ^ levels)).reshape(count, width)
    gateup_near = deal(gateup_near).reshape(slab, 2 * shard)
    downs = {(0, 0): down_near}
    downs[(1, 0)] = swap(down_near, "depth", 1)
    downs[(2, 0)] = swap(down_near, "depth", 2)
    rest_packed = pack_pass(rest_own)
    leave_near = split_columns(gateup_leave[0])
    bands = [(0, width_q), (width_q, head), (width_q + head, head)]
    inputs, gateup_near, attn_packed, downs, rest_packed, leave_near, cotangent, down_enter = tie(
        inputs, gateup_near, attn_packed, downs, rest_packed, leave_near, cotangent, down_enter
    )

    gateup_far = swap(gateup_near, "rows", team)
    qkv_slab, full_qkv_enter, full_query_leave, full_kv_leave, gain_slab = unpack_pass(
        [attn_packed], attn_shapes, BF
    )
    qkv_halves = fetch_halves(qkv_slab)
    downs[(3, 0)] = swap(downs[(1, 0)], "depth", 2)
    full_leave = jnp.concatenate([full_query_leave, full_kv_leave], axis=1)
    gain_slab = gain_slab.reshape(rows, loops, 2, -1)
    both_gains = gain_slab.transpose(2, 1, 0, 3).reshape(2, 1, width).astype(F32)
    gain_one, gain_two = both_gains[0], both_gains[1]
    leave_near = deal(leave_near).reshape(rank // 2, 2 * shard)
    if team == loops:
        enter_near = jnp.pad(
            down_enter[0].reshape(loops, piece, rank), ((0, 0), (0, padded - piece), (0, 0))
        )
        enter_near = deal(enter_near).reshape(loops * padded, rank)
    else:
        enter_near = down_enter
    qkv_halves, inputs, rest_packed, leave_near, enter_near, gateup_near, gateup_far, downs = tie(
        qkv_halves, inputs, rest_packed, leave_near, enter_near, gateup_near, gateup_far, downs
    )

    rest_packed = gather_rows(rest_packed)
    leave_far = swap(leave_near, "rows", team)
    slabs = {(0, 0): gateup_near}
    slabs[(1, 0)] = swap(gateup_near, "depth", 1)
    slabs[(2, 0)] = swap(gateup_near, "depth", 2)
    qkv_eff = fold(halves_order, core_halves(qkv_halves), full_qkv_enter, full_leave, bands)
    normed_one, queries, pairs_here = enter_pass(inputs, gain_one, qkv_eff, cosine, sine, width_q)
    pairs = gather_flips(pairs_here, "rows", bits_of(sub))
    mates = sorted(pairs)
    pairs_all = jnp.concatenate([pairs[f] for f in mates], axis=0)
    key_pos = jnp.concatenate([positions_of(mate ^ f) for f in mates])[None]
    attended, log_total = attend_pass(
        size_here, queries, pairs_all, positions[:, None], key_pos, seq_dev
    )
    attended, gateup_far, leave_far, slabs, rest_packed, downs, enter_near, cotangent = tie(
        attended, gateup_far, leave_far, slabs, rest_packed, downs, enter_near, cotangent
    )

    out_slab, full_out_enter, full_out_leave, full_gateup_enter, full_down_leave = unpack_pass(
        [rest_packed], rest_shapes, BF
    )
    out_halves = fetch_halves(out_slab)
    down_far = swap(downs[(0, 0)], "rows", team)
    enter_far = swap(enter_near, "rows", team) if team == loops else enter_near
    slabs[(0, 1)] = gateup_far
    slabs[(1, 1)] = swap(gateup_far, "depth", 1)
    slabs[(2, 1)] = swap(gateup_far, "depth", 2)
    slabs[(3, 0)] = swap(slabs[(1, 0)], "depth", 2)
    upstream_low = turn(pick(cotangent, seq_here ^ levels)).reshape(count, width)
    out_eff = fold(
        halves_order, core_halves(out_halves), full_out_enter, full_out_leave, [(0, width)]
    )
    mixed, normed_two = leave_pass(inputs, attended, out_eff, gain_two)
    normed_two, upstream_low, downs, down_far, enter_far, slabs = tie(
        normed_two, upstream_low, downs, down_far, enter_far, slabs
    )

    team_bits = bits_of(team)
    slabs[(3, 1)] = swap(slabs[(2, 1)], "depth", 1)
    normed_parts = gather_flips(normed_two, "rows", team_bits[::-1])
    cotan_parts = gather_flips(upstream_low, "rows", team_bits[::-1])
    seats = halving_order(team_bits)
    downs[(0, 1)] = down_far
    downs[(1, 1)] = swap(down_far, "depth", 1)
    downs[(2, 1)] = swap(down_far, "depth", 2)
    downs[(3, 1)] = swap(downs[(2, 1)], "depth", 1)
    leave_full = by_side(leave_near, leave_far)
    if team == loops:
        enter_full = by_side(enter_near, enter_far)
    else:
        enter_every = lax.all_gather(enter_far[0], "rows", axis=0, tiled=True)
        enter_every = enter_every.reshape(loops, 2, team, piece, rank)
        enter_full = lax.dynamic_index_in_dim(enter_every, seat, 2, keepdims=False)
        enter_full = jnp.pad(enter_full, ((0, 0), (0, 0), (0, padded - piece), (0, 0)))
        enter_full = enter_full.reshape(shard, rank)
    gate_enter, up_enter = band(full_gateup_enter, 0), band(full_gateup_enter, 1)
    gateup_eff = fold(
        slab_order,
        [slabs[f] for f in flips],
        full_gateup_enter,
        leave_full,
        [(0, shard), (shard, shard)],
    )
    down_eff = fold(
        slab_order, [downs[f] for f in flips], enter_full, full_down_leave, [(0, width)]
    )

    normed_team = jnp.concatenate([normed_parts[f] for f in seats], axis=0)
    cotan_team = jnp.concatenate([cotan_parts[f] for f in seats], axis=0)
    hidden, grad_expanded, grad_normed = ff_pass(
        normed_team, cotan_team, gateup_eff, down_eff, 256
    )

    def halve(array, bit):
        half = array.shape[0] // 2
        return array[:half], swap(array[half:], "rows", bit)

    def halve_but_last(array):
        for bit in team_bits[:-1]:
            array = add_low(*halve(array, bit))
        return array

    grad_normed = halve_but_last(grad_normed)
    grad_normed, hidden, grad_expanded = tie(grad_normed, hidden, grad_expanded)

    def slabs_of(array):
        height = array.shape[0] // (2 * loops)
        return {
            flips[i]: lax.dynamic_slice(
                array, (slab_order[i] * height, 0), (height, array.shape[1])
            )
            for i in range(len(flips))
        }

    def first_sums(array):
        parts = slabs_of(array)
        near = [add_low(parts[(d, 0)], swap(parts[(d | 2, 0)], "depth", 2)) for d in (0, 1)]
        far = [add_low(parts[(d, 1)], swap(parts[(d | 1, 1)], "depth", 1)) for d in (0, 2)]
        return near, far

    def second_sums(near, far):
        return (
            add_low(near[0], swap(near[1], "depth", 1)),
            add_low(far[0], swap(far[1], "depth", 2)),
        )

    sides = jnp.stack([side, side ^ 1])
    grad_terms = halve(grad_normed, team_bits[-1])
    grad_gateup = outer_sum(normed_team, grad_expanded).astype(BF)
    grad_terms, grad_gateup, hidden = tie(grad_terms, grad_gateup, hidden)

    leave_sides = list(leave_grads_pass(sides, full_gateup_enter, grad_gateup))
    leave_sides[1] = swap(leave_sides[1], "rows", team)
    gateup_sums = first_sums(grad_gateup)
    outcome = halve_but_last(matmul(hidden, down_eff).astype(BF))
    outcome = halve(outcome, team_bits[-1])
    grad_mixed, grad_branch, grad_attended, grad_gain_second = leave_back_pass(
        *grad_terms, mixed, gain_two, upstream_low, out_eff
    )
    grad_queries, key_terms = attend_back_pass(
        size_here,
        queries,
        pairs_all,
        grad_attended,
        log_total,
        positions[:, None],
        key_pos,
        cosine,
        sine,
        seq_dev,
    )
    grad_down = outer_sum(hidden, cotan_team).astype(BF)
    grad_queries, key_terms, leave_sides, gateup_sums, outcome, grad_down, grad_gateup = tie(
        grad_queries, key_terms, leave_sides, gateup_sums, outcome, grad_down, grad_gateup
    )

    sub_bits = bits_of(sub)
    mate_order = halving_order(sub_bits)
    key_terms = jnp.concatenate([key_terms[f * count : (f + 1) * count] for f in mate_order])
    for bit in sub_bits[:-1]:
        key_terms = add_low(*halve(key_terms, bit))
    pair_terms = halve(key_terms, sub_bits[-1])
    result = mixed + (outcome[0].astype(F32) + outcome[1].astype(F32))
    activations = turn(result.astype(BF).reshape(slots, seq_dev, width))
    gateup_sums = second_sums(*gateup_sums)
    down_sums = first_sums(grad_down)
    leave_sum = deal(add_low(*leave_sides).reshape(team, rank // (2 * team), 2 * shard))
    if team == loops:
        enter_sides = list(enter_grads_pass(sides, grad_down, full_down_leave))
        enter_sides[1] = swap(enter_sides[1], "rows", team)
    else:
        enter_sides = [through(grad_down, full_down_leave).astype(BF)]
    grad_joined, grad_inputs, grad_gain_first = enter_back_pass(
        grad_queries, pair_terms, cosine, sine, qkv_eff, inputs, gain_one, grad_mixed
    )
    grad_qkv = outer_sum(normed_one, grad_joined).astype(BF)
    grad_inputs, grad_qkv, enter_sides, gateup_sums, activations, down_sums, leave_sum = tie(
        grad_inputs, grad_qkv, enter_sides, gateup_sums, activations, down_sums, leave_sum
    )

    def loop_terms(array):
        height = array.shape[0] // loops
        terms = [
            lax.dynamic_slice(array, ((group ^ f) * height, 0), (height, array.shape[1]))
            for f in depth_flips
        ]
        return terms[:1] + [swap(terms[f], "depth", f) for f in depth_flips[1:]]

    returned = turn(grad_inputs.reshape(slots, seq_dev, width))
    gateup_sum = add_low(gateup_sums[0], swap(gateup_sums[1], "rows", team))
    qkv_terms = loop_terms(grad_qkv)
    down_sums = second_sums(*down_sums)
    if team == loops:
        enter_sum = deal(add_low(*enter_sides).reshape(team, padded, rank))
    grad_out = outer_sum(attended, grad_branch).astype(BF)
    returned, qkv_terms, gateup_sum, down_sums, grad_out = tie(
        returned, qkv_terms, gateup_sum, down_sums, grad_out
    )

    row_bits = bits_of(rows)
    row_order = jnp.array(halving_order(row_bits), jnp.int32)

    row_place = pick(jnp.argsort(row_order), place ^ jnp.arange(rows))

    def own_terms(packed):
        for bit in row_bits[:-1]:
            packed = add_low(*halve(packed, bit))
        return halve(packed, row_bits[-1])

    returned = pick(returned, seq_here ^ levels)
    returned = lax.all_to_all(returned, "depth", split_axis=0, concat_axis=0, tiled=True)
    attn_grads_of = attn_grads_shapes(
        rows, qkv_terms[0], grad_qkv, full_qkv_enter, full_leave, bands
    )
    attn_sum = own_terms(
        grads_pass(
            lambda *refs: attn_grads_kernel(bands, *refs),
            row_place,
            rows,
            attn_grads_of,
            [*qkv_terms, grad_qkv, full_qkv_enter, full_leave],
        )
    )
    down_sum = add_low(down_sums[0], swap(down_sums[1], "rows", team))
    out_terms = loop_terms(grad_out)
    gateup_sum = deal(gateup_sum.reshape(team, slab // team, 2 * shard))
    grad_gateup_leave = join_columns(leave_sum)
    returned, gateup_sum, attn_sum, out_terms, down_sum = tie(
        returned, gateup_sum, attn_sum, out_terms, down_sum
    )

    rest_grads_of = [
        (out_terms[0].shape[0] // rows, width),
        (grad_out.shape[0] // rows, rank),
        (rank // rows, width),
        (width // rows, rank),
        (width // rows, rank),
        (rank // rows, width),
    ]
    rest_sum = own_terms(
        grads_pass(
            rest_grads_kernel,
            row_place,
            rows,
            rest_grads_of,
            [
                *out_terms,
                grad_out,
                full_out_enter,
                full_out_leave,
                grad_gateup,
                leave_full,
                grad_down,
                enter_full,
            ],
        )
    )
    grad_tokens = pick(returned, mine)
    activations = pick(activations, seq_here ^ levels)
    grad_gateup_weight = join_columns(gateup_sum)
    grad_down_weight = down_sum[:piece].astype(F32)
    if team == loops:
        grad_down_enter = enter_sum[:, :piece].reshape(loops * piece, rank)
    else:
        grad_down_in = enter_sides[0].reshape(loops, 2, 1, padded, rank)[:, :, :, :piece]
        spaced = jnp.zeros((loops, 2, team, piece, rank), BF)
        spaced = lax.dynamic_update_slice(spaced, grad_down_in, (0, 0, seat, 0, 0))
        grad_down_enter = lax.psum_scatter(
            spaced.reshape(hidden_units, rank), "rows", scatter_dimension=0, tiled=True
        )
    own_wide, *attn_parts = unpack_pass(attn_sum, attn_grads_of, F32)
    own_out, *rest_parts = unpack_pass(rest_sum, rest_grads_of, F32)
    attn_grads = [
        jnp.concatenate(attn_parts[:3], axis=1),
        attn_parts[3],
        jnp.concatenate(attn_parts[4:], axis=1),
    ]
    rest_grads = rest_parts[:2] + [jnp.concatenate(rest_parts[2:4], axis=1), rest_parts[4]]

    block_pos = place * seq_dev + jnp.arange(seq_dev, dtype=jnp.int32)
    valid = block_pos[None, :] < sizes_here[:, None]
    counts_here = jnp.sum(
        ((exit_depth[None] == levels[:, None, None]) & valid[None]).astype(F32), axis=(1, 2)
    )
    given = inputs.astype(F32)
    cross = jnp.sum(given * result, axis=-1)
    own_sq = jnp.sum(given * given, axis=-1)
    out_sq = jnp.sum(result * result, axis=-1)
    cosines = cross * lax.rsqrt(own_sq * out_sq + 1e-06)
    cosine_here = jnp.sum(jnp.where(positions < size_here, cosines, 0.0))
    tallies = jnp.concatenate([counts_here, cosine_here[None]])
    gain_grads = jnp.concatenate([grad_gain_first, grad_gain_second])
    gain_grads = gain_grads.reshape(2, loops * rows, gain_size).transpose(1, 0, 2)
    small = jnp.concatenate(
        [
            jnp.broadcast_to(tallies[None], (loops * rows, loops + 1)),
            gain_grads.reshape(loops * rows, 2 * gain_size),
        ],
        axis=1,
    )
    small = jnp.pad(small, ((0, 0), (0, 127 - loops - 2 * gain_size)))
    small = lax.all_to_all(small, ("depth", "rows"), split_axis=0, concat_axis=0, tiled=True)
    small = jnp.sum(small, axis=0)
    tallies = small[: loops + 1]
    gain_grads = small[loops + 1 : loops + 1 + 2 * gain_size].reshape(2, gain_size)
    exit_counts = tallies[:loops].astype(jnp.int32)
    confidence = tallies[loops] / jnp.sum(lengths).astype(F32)

    return (
        activations,
        grad_tokens,
        exit_counts,
        confidence,
        gain_grads[0],
        gain_grads[1],
        own_wide,
        own_out,
        grad_gateup_weight,
        grad_down_weight,
        attn_grads[0][None],
        attn_grads[1][None],
        attn_grads[2][None],
        rest_grads[0][None],
        rest_grads[1][None],
        rest_grads[2][None],
        grad_gateup_leave[None],
        grad_down_enter[None].astype(F32),
        rest_grads[3][None],
    )


def solution(mesh):
    split = P("depth", "rows", None)
    flat = P(("depth", "rows"))
    tall = P(("depth", "rows"), None)
    return jax.shard_map(
        per_device,
        mesh=mesh,
        in_specs=(split, split, P("depth", "rows"), P(), P(), flat, flat)
        + (tall,) * 4
        + (split,) * 9,
        out_specs=(split, split, P(), P(), flat, flat) + (tall,) * 4 + (split,) * 9,
        check_vma=False,
    )
```

```python
import math

import jax
import jax.numpy as jnp
from jax import lax
from jax.experimental import pallas as pl
from jax.experimental.pallas import tpu as pltpu
from jax.sharding import PartitionSpec as P

BF = jnp.bfloat16
F32 = jnp.float32
ROOT = math.sqrt(2.0 / math.pi)
CUBE = 0.044715


def angles(positions, size):
    freqs = jnp.exp(jnp.arange(size // 2, dtype=F32) * (-2.0 * math.log(10000.0) / size))
    phase = positions[:, None] * freqs[None, :]
    return (jnp.cos(phase), jnp.sin(phase))


def matmul(left, right):
    return jnp.dot(left, right, preferred_element_type=F32)


def outer_sum(left, right):
    return lax.dot_general(left, right, (((0,), (0,)), ((), ())), preferred_element_type=F32)


def through(left, right):
    return lax.dot_general(left, right, (((1,), (1,)), ((), ())), preferred_element_type=F32)


def swap(value, axis, flip):
    size = lax.axis_size(axis)
    return lax.ppermute(value, axis, [(i, i ^ flip) for i in range(size)])


def add_low(left, right):
    return (left.astype(F32) + right.astype(F32)).astype(BF)


def tie(*values):
    return lax.optimization_barrier(values)


def bits_of(size):
    return [1 << i for i in range(size.bit_length() - 1)]


LANES = 256


def even(height):
    return -(-height // 16) * 16


def segments(shapes):
    out, row = [], 0
    for which, (height, columns) in enumerate(shapes):
        for start in range(0, columns, LANES):
            out.append((which, row, start, min(LANES, columns - start)))
            row += even(height)
    return out, row


def put(out_ref, lead, row, height, value):
    short, narrow = even(height) - height, LANES - value.shape[1]
    if narrow:
        value = jnp.concatenate([value, jnp.zeros((height, narrow), value.dtype)], axis=1)
    if short:
        value = jnp.concatenate([value, jnp.zeros((short, LANES), value.dtype)], axis=0)
    out_ref[lead, row : row + even(height), :] = value


def pack_kernel(shapes, *refs):
    where, _ = segments(shapes)
    for which, row, start, size in where:
        put(refs[-1], 0, row, shapes[which][0], refs[which][:, start : start + size])


def pack_pass(arrays):
    shapes = [array.shape for array in arrays]
    return pl.pallas_call(
        lambda *refs: pack_kernel(shapes, *refs),
        out_shape=jax.ShapeDtypeStruct((1, segments(shapes)[1], LANES), BF),
        compiler_params=MEMORY,
        cost_estimate=FREE,
    )(*arrays)


def unpack_kernel(shapes, terms, *refs):
    where, _ = segments(shapes)
    for which, row, start, size in where:
        height = shapes[which][0]
        out_ref = refs[terms + which]
        for lead in range(refs[0].shape[0]):
            value = refs[0][lead, row : row + height, :size]
            if terms > 1:
                value = value.astype(F32) + refs[1][lead, row : row + height, :size].astype(F32)
            first = lead * height
            out_ref[first : first + height, start : start + size] = value.astype(out_ref.dtype)


def unpack_pass(terms, shapes, dtype):
    lead = terms[0].shape[0]
    return pl.pallas_call(
        lambda *refs: unpack_kernel(shapes, len(terms), *refs),
        out_shape=[jax.ShapeDtypeStruct((lead * h, c), dtype) for h, c in shapes],
        compiler_params=MEMORY,
        cost_estimate=FREE,
    )(*terms)


def spread_rows(pos_ref, out_ref, row, value, first, size):
    leads = out_ref.shape[0]
    height = value.shape[0] // leads
    for lead in range(leads):
        block = value[lead * height : (lead + 1) * height, first : first + size]
        put(out_ref, pos_ref[lead], row, height, block.astype(BF))


def total_of(refs, rows, columns):
    total = refs[0][rows, :columns].astype(F32)
    for ref in refs[1:]:
        total = total + ref[rows, :columns].astype(F32)
    return total


def place_all(pos_ref, out_ref, values):
    shapes = [(value.shape[0] // out_ref.shape[0], value.shape[1]) for value in values]
    for which, row, start, size in segments(shapes)[0]:
        spread_rows(pos_ref, out_ref, row, values[which], start, size)


def attn_grads_kernel(height, bands, pos_ref, *refs):
    grad_ref, enter_ref, leave_ref, out_ref = refs[-4:]
    rank = leave_ref.shape[0]
    values = [total_of(refs[:-4], slice(0, height), grad_ref.shape[1])]
    for start, size in bands:
        values.append(through(grad_ref[:, start : start + size], leave_ref[:, start : start + size]))
    for index, (start, size) in enumerate(bands):
        enter = enter_ref[:, index * rank : (index + 1) * rank]
        values.append(outer_sum(enter, grad_ref[:, start : start + size]))
    place_all(pos_ref, out_ref, values)


def attn_grads_shapes(rows, height, grad, enter, leave, bands):
    rank = leave.shape[0]
    return (
        [(height // rows, grad.shape[1])]
        + [(grad.shape[0] // rows, rank)] * len(bands)
        + [(rank // rows, size) for _, size in bands]
    )


def rest_grads_kernel(first, pos_ref, *refs):
    (
        grad_out_ref,
        out_enter_ref,
        out_leave_ref,
        grad_gateup_ref,
        leave_ref,
        grad_down_ref,
        down_enter_ref,
        out_ref,
    ) = refs[-8:]
    shard = leave_ref.shape[1] // 2
    values = [
        total_of(refs[:-8], slice(first, refs[0].shape[0]), grad_out_ref.shape[1]),
        through(grad_out_ref[...], out_leave_ref[...]),
        outer_sum(out_enter_ref[...], grad_out_ref[...]),
        through(grad_gateup_ref[:, :shard], leave_ref[:, :shard]),
        through(grad_gateup_ref[:, shard:], leave_ref[:, shard:]),
        outer_sum(down_enter_ref[...], grad_down_ref[...]),
    ]
    place_all(pos_ref, out_ref, values)


def grads_pass(kernel, pos, rows, shapes, arrays):
    whole = [pl.BlockSpec(memory_space=pltpu.VMEM)] * len(arrays)
    shape = (rows, segments(shapes)[1], LANES)
    return pl.pallas_call(
        kernel,
        in_specs=[pl.BlockSpec(memory_space=pltpu.SMEM)] + whole,
        out_specs=pl.BlockSpec(memory_space=pltpu.VMEM),
        out_shape=jax.ShapeDtypeStruct(shape, BF),
        compiler_params=MEMORY,
        cost_estimate=FREE,
    )(pos, *arrays)


FREE = pl.CostEstimate(flops=0, transcendentals=0, bytes_accessed=0)
MEMORY = pltpu.CompilerParams(vmem_limit_bytes=60 << 20)


def held(array):
    return pl.BlockSpec(
        array.shape, lambda *_: (0,) * len(array.shape), pipeline_mode=pl.Buffered(1)
    )


def strip(tile, columns):
    return pl.BlockSpec((tile, columns), lambda i: (i, 0))


def mean_scale(values):
    return lax.rsqrt(jnp.mean(values * values, axis=-1, keepdims=True) + 1e-06)


def turned(values, cosine, sine):
    half = values.shape[-1] // 2
    first, second = values[:, :half], values[:, half:]
    return jnp.concatenate(
        [first * cosine - second * sine, second * cosine + first * sine], axis=-1
    )


def enter_kernel(x_ref, gain_ref, weight_ref, cos_ref, sin_ref, n_ref, q_ref, kv_ref):
    head = kv_ref.shape[1] // 2
    width_q = q_ref.shape[1]
    values = x_ref[...].astype(F32)
    normed = (values * mean_scale(values) * gain_ref[...]).astype(BF)
    n_ref[...] = normed
    joined = matmul(normed, weight_ref[...])
    cosine, sine = cos_ref[...], sin_ref[...]
    scale = head ** (-0.5)
    for start in range(0, width_q, head):
        spun = turned(joined[:, start : start + head], cosine, sine)
        q_ref[:, start : start + head] = (spun * scale).astype(BF)
    kv_ref[:, :head] = turned(joined[:, width_q : width_q + head], cosine, sine).astype(BF)
    kv_ref[:, head:] = joined[:, width_q + head :].astype(BF)


def enter_pass(x, gain, weight, cosine, sine, width_q):
    count, width = x.shape
    tile = count // 2
    rest = weight.shape[1] - width_q
    return pl.pallas_call(
        enter_kernel,
        grid=(count // tile,),
        in_specs=[
            strip(tile, width),
            held(gain),
            held(weight),
            strip(tile, cosine.shape[1]),
            strip(tile, cosine.shape[1]),
        ],
        out_specs=[strip(tile, width), strip(tile, width_q), strip(tile, rest)],
        out_shape=[
            jax.ShapeDtypeStruct((count, width), BF),
            jax.ShapeDtypeStruct((count, width_q), BF),
            jax.ShapeDtypeStruct((count, rest), BF),
        ],
        compiler_params=MEMORY,
        cost_estimate=FREE,
    )(x, gain, weight, cosine, sine)


def stack_heads(ref, head):
    return jnp.concatenate(
        [ref[:, start : start + head] for start in range(0, ref.shape[1], head)], axis=0
    )


def allowed_keys(size_ref, pos_ref, key_ref, heads):
    fits = (key_ref[...] <= pos_ref[...]) & (key_ref[...] < size_ref[0])
    return jnp.concatenate([jnp.where(fits, 0.0, -1e30)] * heads, axis=0)


def attend_kernel(size_ref, q_ref, kv_ref, pos_ref, key_ref, o_ref, lse_ref):
    head = kv_ref.shape[1] // 2
    tile = q_ref.shape[0]
    heads = q_ref.shape[1] // head
    scores = through(stack_heads(q_ref, head), kv_ref[:, :head])
    scores = scores + allowed_keys(size_ref, pos_ref, key_ref, heads)
    highest = jnp.max(scores, axis=-1, keepdims=True)
    raised = jnp.exp(scores - highest)
    total = jnp.sum(raised, axis=-1, keepdims=True)
    probs = (raised * (1.0 / total)).astype(BF)
    lse_ref[...] = (highest + jnp.log(total)).reshape(1, heads * tile, 1)
    mixed = matmul(probs, kv_ref[:, head:]).astype(BF)
    for index in range(heads):
        o_ref[:, index * head : (index + 1) * head] = mixed[index * tile : (index + 1) * tile]


def attend_pass(size, q, kv, positions, key_positions, tile):
    count, width_q = q.shape
    heads = 2 * width_q // kv.shape[1]
    steps = count // tile

    def rows(columns):
        return pl.BlockSpec((tile, columns), lambda i, s: (i, 0))

    return pl.pallas_call(
        attend_kernel,
        grid_spec=pltpu.PrefetchScalarGridSpec(
            num_scalar_prefetch=1,
            grid=(steps,),
            in_specs=[rows(width_q), held(kv), rows(1), held(key_positions)],
            out_specs=[rows(width_q), pl.BlockSpec((1, heads * tile, 1), lambda i, s: (i, 0, 0))],
        ),
        out_shape=[
            jax.ShapeDtypeStruct((count, width_q), BF),
            jax.ShapeDtypeStruct((steps, heads * tile, 1), F32),
        ],
        compiler_params=MEMORY,
        cost_estimate=FREE,
    )(size, q, kv, positions, key_positions)


def attend_back_kernel(
    size_ref, q_ref, kv_ref, do_ref, lse_ref, pos_ref, key_ref, cos_ref, sin_ref, dq_ref, dkv_ref, acc
):
    head = kv_ref.shape[1] // 2
    tile = q_ref.shape[0]
    heads = q_ref.shape[1] // head
    step = pl.program_id(0)
    queries = stack_heads(q_ref, head)
    grads = stack_heads(do_ref, head)
    keys = kv_ref[:, :head]
    scores = through(queries, keys) + allowed_keys(size_ref, pos_ref, key_ref, heads)
    probs = jnp.exp(scores - lse_ref[0])
    grad_probs = through(grads, kv_ref[:, head:])
    centre = jnp.sum(probs * grad_probs, axis=-1, keepdims=True)
    grad_scores = (probs * (grad_probs - centre)).astype(BF)
    grad_q = matmul(grad_scores, keys) * (head ** (-0.5))
    cosine, sine = cos_ref[...], -sin_ref[...]
    for index in range(heads):
        spun = turned(grad_q[index * tile : (index + 1) * tile], cosine, sine)
        dq_ref[:, index * head : (index + 1) * head] = spun.astype(BF)
    grad_k = outer_sum(grad_scores, queries)
    grad_v = outer_sum(probs.astype(BF), grads)

    @pl.when(step == 0)
    def _():
        acc[:, :head] = grad_k
        acc[:, head:] = grad_v

    @pl.when(step > 0)
    def _():
        acc[:, :head] += grad_k
        acc[:, head:] += grad_v

    @pl.when(step == pl.num_programs(0) - 1)
    def _():
        dkv_ref[...] = acc[...].astype(BF)


def attend_back_pass(size, q, kv, do, lse, positions, key_positions, cosine, sine, tile):
    count, width_q = q.shape
    heads = 2 * width_q // kv.shape[1]

    def rows(columns):
        return pl.BlockSpec((tile, columns), lambda i, s: (i, 0))

    return pl.pallas_call(
        attend_back_kernel,
        grid_spec=pltpu.PrefetchScalarGridSpec(
            num_scalar_prefetch=1,
            grid=(count // tile,),
            in_specs=[
                rows(width_q),
                held(kv),
                rows(width_q),
                pl.BlockSpec((1, heads * tile, 1), lambda i, s: (i, 0, 0)),
                rows(1),
                held(key_positions),
                rows(cosine.shape[1]),
                rows(cosine.shape[1]),
            ],
            out_specs=[rows(width_q), pl.BlockSpec(kv.shape, lambda i, s: (0, 0))],
            scratch_shapes=[pltpu.VMEM(kv.shape, F32)],
        ),
        out_shape=[jax.ShapeDtypeStruct((count, width_q), BF), jax.ShapeDtypeStruct(kv.shape, BF)],
        compiler_params=MEMORY,
        cost_estimate=FREE,
    )(size, q, kv, do, lse, positions, key_positions, cosine, sine)


def leave_kernel(x_ref, o_ref, weight_ref, gain_ref, h_ref, n_ref):
    mixed = x_ref[...].astype(F32) + matmul(o_ref[...], weight_ref[...])
    h_ref[...] = mixed
    n_ref[...] = (mixed * mean_scale(mixed) * gain_ref[...]).astype(BF)


def leave_pass(x, o, weight, gain):
    count, width = x.shape
    tile = count // 2
    return pl.pallas_call(
        leave_kernel,
        grid=(count // tile,),
        in_specs=[strip(tile, width), strip(tile, o.shape[1]), held(weight), held(gain)],
        out_specs=[strip(tile, width)] * 2,
        out_shape=[jax.ShapeDtypeStruct((count, width), d) for d in (F32, BF)],
        compiler_params=MEMORY,
        cost_estimate=FREE,
    )(x, o, weight, gain)


def norm_grad(grad, values, gain):
    scaling = mean_scale(values)
    unit = values * scaling
    lifted = grad * gain
    back = scaling * (lifted - unit * jnp.mean(lifted * unit, axis=-1, keepdims=True))
    return back, jnp.sum(grad * unit, axis=0, keepdims=True)


def add_step(ref, value):
    @pl.when(pl.program_id(0) == 0)
    def _():
        ref[...] = value

    @pl.when(pl.program_id(0) > 0)
    def _():
        ref[...] += value


def leave_back_kernel(
    one_ref, two_ref, h_ref, gain_ref, dy_ref, weight_ref, dh_ref, dz_ref, do_ref, dgain_ref
):
    grad = one_ref[...].astype(F32) + two_ref[...].astype(F32)
    back, gain_sum = norm_grad(grad, h_ref[...], gain_ref[...])
    total = dy_ref[...].astype(F32) + back
    dh_ref[...] = total
    low = total.astype(BF)
    dz_ref[...] = low
    do_ref[...] = through(low, weight_ref[...]).astype(BF)
    add_step(dgain_ref, gain_sum)


def leave_back_pass(one, two, h, gain, dy, weight):
    count, width = h.shape
    tile = count // 2
    width_q = weight.shape[0]
    return pl.pallas_call(
        leave_back_kernel,
        grid=(count // tile,),
        in_specs=[strip(tile, width)] * 3 + [held(gain), strip(tile, width), held(weight)],
        out_specs=[strip(tile, width)] * 2
        + [strip(tile, width_q), pl.BlockSpec((1, width), lambda i: (0, 0))],
        out_shape=[
            jax.ShapeDtypeStruct((count, width), F32),
            jax.ShapeDtypeStruct((count, width), BF),
            jax.ShapeDtypeStruct((count, width_q), BF),
            jax.ShapeDtypeStruct((1, width), F32),
        ],
        compiler_params=MEMORY,
        cost_estimate=FREE,
    )(one, two, h, gain, dy, weight)


def enter_back_kernel(dq_ref, *refs):
    parts = refs[:-9]
    cos_ref, sin_ref, weight_ref, x_ref, gain_ref, dh_ref, joined_ref, dx_ref, dgain_ref = refs[-9:]
    head = parts[0].shape[1] // 2
    width_q = dq_ref.shape[1]
    pair = parts[0][...].astype(F32)
    for part in parts[1:]:
        pair = pair + part[...].astype(F32)
    joined_ref[:, :width_q] = dq_ref[...]
    spun = turned(pair[:, :head], cos_ref[...], -sin_ref[...])
    joined_ref[:, width_q : width_q + head] = spun.astype(BF)
    joined_ref[:, width_q + head :] = pair[:, head:].astype(BF)
    grad = through(joined_ref[...], weight_ref[...])
    back, gain_sum = norm_grad(grad, x_ref[...].astype(F32), gain_ref[...])
    dx_ref[...] = (dh_ref[...] + back).astype(BF)
    add_step(dgain_ref, gain_sum)


def enter_back_pass(dq, parts, cosine, sine, weight, x, gain, dh):
    count, width = x.shape
    tile = count // 2
    width_q = dq.shape[1]
    return pl.pallas_call(
        enter_back_kernel,
        grid=(count // tile,),
        in_specs=[strip(tile, width_q)]
        + [strip(tile, part.shape[1]) for part in parts]
        + [strip(tile, cosine.shape[1])] * 2
        + [held(weight), strip(tile, width), held(gain), strip(tile, width)],
        out_specs=[
            strip(tile, weight.shape[1]),
            strip(tile, width),
            pl.BlockSpec((1, width), lambda i: (0, 0)),
        ],
        out_shape=[
            jax.ShapeDtypeStruct((count, weight.shape[1]), BF),
            jax.ShapeDtypeStruct((count, width), BF),
            jax.ShapeDtypeStruct((1, width), F32),
        ],
        compiler_params=MEMORY,
        cost_estimate=FREE,
    )(dq, *parts, cosine, sine, weight, x, gain, dh)


def halving_order(bits):
    order = [0]
    for bit in reversed(bits):
        order = order + [flip | bit for flip in order]
    return order


def ff_kernel(n2_ref, df_ref, wg_ref, wd_ref, a_ref, dg_ref, dn_ref):
    hidden = wd_ref.shape[0]
    n2 = n2_ref[...]
    gate = matmul(n2, wg_ref[:, :hidden])
    upper = matmul(n2, wg_ref[:, hidden:])
    grad = through(df_ref[...], wd_ref[...])
    square = gate * gate
    bent = jnp.tanh(gate * (ROOT + ROOT * CUBE * square))
    half = 0.5 + 0.5 * bent
    act = gate * half
    a_ref[...] = (act * upper).astype(BF)
    slope = half + 0.5 * gate * (1.0 - bent * bent) * (ROOT + 3.0 * ROOT * CUBE * square)
    dg_ref[:, :hidden] = (grad * upper * slope).astype(BF)
    dg_ref[:, hidden:] = (grad * act).astype(BF)
    dn_ref[...] = through(dg_ref[...], wg_ref[...]).astype(BF)


def ff_pass(n2, df, wg, wd, tile):
    count, width = n2.shape
    hidden = wd.shape[0]

    return pl.pallas_call(
        ff_kernel,
        grid=(count // tile,),
        in_specs=[strip(tile, width), strip(tile, width), held(wg), held(wd)],
        out_specs=[strip(tile, hidden), strip(tile, 2 * hidden), strip(tile, width)],
        out_shape=[
            jax.ShapeDtypeStruct((count, hidden), BF),
            jax.ShapeDtypeStruct((count, 2 * hidden), BF),
            jax.ShapeDtypeStruct((count, width), BF),
        ],
        compiler_params=MEMORY,
        cost_estimate=FREE,
    )(n2, df, wg, wd)


def blocks_of(padded, width, columns):
    across = columns // 128
    wide = width // 128
    out = []
    for r in range(padded // 16):
        for c in range(wide):
            out.append((16 * r, 128 * c, 16 * ((r * wide + c) // across), 128 * ((r * wide + c) % across)))
    return out, 16 * (-(-len(out) // across))


def tall(value, height):
    short = height - value.shape[0]
    if not short:
        return value
    return jnp.concatenate([value, jnp.zeros((short, value.shape[1]), value.dtype)], axis=0)


def deal_kernel(piece, padded, *refs):
    gateup_ref, leave_ref, out_ref = refs[0], refs[1], refs[-1]
    team, total, columns = out_ref.shape
    units, shard = gateup_ref.shape[1] // 2, columns // 2
    lines = leave_ref.shape[0]
    for in_ref, row in ((leave_ref, 0), (gateup_ref, total - gateup_ref.shape[0])):
        height = in_ref.shape[0]
        gap = jnp.zeros((height, padded - piece), in_ref.dtype)
        for half in range(2):
            for seat in range(team):
                parts = []
                for block in range(shard // padded):
                    start = half * units + (block * team + seat) * piece
                    parts += [in_ref[:, start : start + piece], gap]
                joined = jnp.concatenate(parts, axis=1)
                out_ref[seat, row : row + height, half * shard : (half + 1) * shard] = joined
    if len(refs) == 4:
        rank = refs[2].shape[1]
        for seat in range(team):
            for row in range(0, padded, 16):
                first = seat * piece + row
                value = tall(refs[2][first : first + min(16, piece - row), :], 16)
                start = row // 16 * rank
                out_ref[seat, lines : lines + 16, start : start + rank] = value


def deal_pass(arrays, team, piece, padded):
    lines = sum(array.shape[0] for array in arrays[:2]) + 16 * (len(arrays) == 3)
    columns = arrays[0].shape[1] // (team * piece) * padded
    return pl.pallas_call(
        lambda *refs: deal_kernel(piece, padded, *refs),
        out_shape=jax.ShapeDtypeStruct((team, lines, columns), BF),
        compiler_params=MEMORY,
        cost_estimate=FREE,
    )(*arrays)


def slab_kernel(padded, dealt_ref, down_ref, slab_ref, rest_ref):
    team, total, columns = dealt_ref.shape
    lines = rest_ref.shape[1]
    height = total - lines
    piece, width = down_ref.shape
    base = team * height
    for seat in range(team):
        slab_ref[seat * height : (seat + 1) * height, :] = dealt_ref[seat, lines:total, :]
        rest_ref[seat] = dealt_ref[seat, :lines, :]
    where, extra = blocks_of(padded, width, columns)
    slab_ref[base + extra - 16 : base + extra, :] = jnp.zeros((16, columns), BF)
    for r, c, row, lane in where:
        value = tall(down_ref[r : r + min(16, piece - r), c : c + 128], 16)
        slab_ref[base + row : base + row + 16, lane : lane + 128] = value


def slab_pass(dealt, down, lines, padded):
    team, total, columns = dealt.shape
    extra = blocks_of(padded, down.shape[1], columns)[1]
    return pl.pallas_call(
        lambda *refs: slab_kernel(padded, *refs),
        out_shape=[
            jax.ShapeDtypeStruct((team * (total - lines) + extra, columns), BF),
            jax.ShapeDtypeStruct((team, lines, columns), BF),
        ],
        compiler_params=MEMORY,
        cost_estimate=FREE,
    )(dealt, down)


def assemble_kernel(lines, side_ref, near_ref, far_ref, *outs):
    team = near_ref.shape[0]

    def fill(half, ref):
        for seat in range(team):
            first = (half * team + seat) * lines
            outs[0][first : first + lines, :] = ref[seat, :lines, :]
            if len(outs) == 2:
                rank = outs[1].shape[1]
                padded = outs[1].shape[0] // (2 * team)
                for row in range(0, padded, 16):
                    start = row // 16 * rank
                    first = (half * team + seat) * padded + row
                    outs[1][first : first + 16, :] = ref[
                        seat, lines : lines + 16, start : start + rank
                    ]

    for half in range(2):

        @pl.when(side_ref[0] == half)
        def _(half=half):
            fill(half, near_ref)
            fill(1 - half, far_ref)


def assemble_pass(side, near, far, lines, shard, rank):
    team, height, columns = near.shape
    shapes = [jax.ShapeDtypeStruct((2 * team * lines, columns), BF)]
    if height > lines:
        shapes.append(jax.ShapeDtypeStruct((shard, rank), BF))
    vmem = pl.BlockSpec(memory_space=pltpu.VMEM)
    return pl.pallas_call(
        lambda *refs: assemble_kernel(lines, *refs),
        in_specs=[pl.BlockSpec(memory_space=pltpu.SMEM), vmem, vmem],
        out_specs=[vmem] * len(shapes),
        out_shape=shapes,
        compiler_params=MEMORY,
        cost_estimate=FREE,
    )(side, near, far)


def fold_ff_kernel(order_ref, *refs):
    slabs = refs[:-7]
    enter_ref, leave_ref, down_enter_ref, down_leave_ref, gateup_out, down_out, blocks = refs[-7:]
    rank = leave_ref.shape[0]
    height, columns = gateup_out.shape
    shard = columns // 2
    step = pl.program_id(0)
    for index in range(2):
        start = index * shard
        lift = matmul(
            enter_ref[:, index * rank : (index + 1) * rank], leave_ref[:, start : start + shard]
        )
        for which, slab_ref in enumerate(slabs):

            @pl.when(step == which)
            def _(slab_ref=slab_ref, lift=lift, start=start):
                part = slab_ref[:height, start : start + shard].astype(F32)
                gateup_out[:, start : start + shard] = (part + lift).astype(BF)

    for which, slab_ref in enumerate(slabs):

        @pl.when(step == which)
        def _(slab_ref=slab_ref):
            blocks[...] = slab_ref[height:, :]

    lift = matmul(down_enter_ref[...], down_leave_ref[...])
    padded, width = down_out.shape
    wide = width // 128
    where, _ = blocks_of(padded, width, columns)
    for first in range(0, len(where), wide):
        r = where[first][0]
        parts = [
            blocks[row : row + 16, lane : lane + 128]
            for _, _, row, lane in where[first : first + wide]
        ]
        part = jnp.concatenate(parts, axis=1).astype(F32)
        down_out[r : r + 16, :] = (part + lift[r : r + 16]).astype(BF)


def fold_ff_pass(order, slabs, enter, leave, down_enter, down_leave, padded):
    count = len(slabs)
    columns, width = leave.shape[1], down_leave.shape[1]
    height = enter.shape[0] // count

    def own(rows, wide):
        return pl.BlockSpec((rows, wide), lambda i, o: (o[i], 0))

    return pl.pallas_call(
        fold_ff_kernel,
        grid_spec=pltpu.PrefetchScalarGridSpec(
            num_scalar_prefetch=1,
            grid=(count,),
            in_specs=[held(slab) for slab in slabs]
            + [
                own(height, enter.shape[1]),
                held(leave),
                own(padded, down_enter.shape[1]),
                held(down_leave),
            ],
            out_specs=[own(height, columns), own(padded, width)],
            scratch_shapes=[pltpu.VMEM((slabs[0].shape[0] - height, columns), BF)],
        ),
        out_shape=[
            jax.ShapeDtypeStruct((count * height, columns), BF),
            jax.ShapeDtypeStruct((count * padded, width), BF),
        ],
        compiler_params=MEMORY,
        cost_estimate=FREE,
    )(order, *slabs, enter, leave, down_enter, down_leave)


def fold_attn_kernel(bands, order_ref, *refs):
    slabs = refs[:-6]
    enter_ref, leave_ref, out_enter_ref, out_leave_ref, in_out, out_out = refs[-6:]
    rank = leave_ref.shape[0]
    height, width = in_out.shape[0], out_out.shape[1]
    step = pl.program_id(0)
    lifts = [
        matmul(enter_ref[:, i * rank : (i + 1) * rank], leave_ref[:, start : start + size])
        for i, (start, size) in enumerate(bands)
    ]
    out_lift = matmul(out_enter_ref[...], out_leave_ref[...])
    for which, slab_ref in enumerate(slabs):

        @pl.when(step == which)
        def _(slab_ref=slab_ref):
            for (start, size), lift in zip(bands, lifts):
                part = slab_ref[:height, start : start + size].astype(F32)
                in_out[:, start : start + size] = (part + lift).astype(BF)
            part = slab_ref[height:, :width].astype(F32)
            out_out[...] = (part + out_lift).astype(BF)


def fold_attn_pass(order, slabs, enter, leave, out_enter, out_leave, bands):
    count = len(slabs)
    height, short = enter.shape[0] // count, out_enter.shape[0] // count

    def own(rows, wide):
        return pl.BlockSpec((rows, wide), lambda i, o: (o[i], 0))

    return pl.pallas_call(
        lambda *refs: fold_attn_kernel(bands, *refs),
        grid_spec=pltpu.PrefetchScalarGridSpec(
            num_scalar_prefetch=1,
            grid=(count,),
            in_specs=[held(slab) for slab in slabs]
            + [
                own(height, enter.shape[1]),
                held(leave),
                own(short, out_enter.shape[1]),
                held(out_leave),
            ],
            out_specs=[own(height, leave.shape[1]), own(short, out_leave.shape[1])],
        ),
        out_shape=[
            jax.ShapeDtypeStruct((enter.shape[0], leave.shape[1]), BF),
            jax.ShapeDtypeStruct((out_enter.shape[0], out_leave.shape[1]), BF),
        ],
        compiler_params=MEMORY,
        cost_estimate=FREE,
    )(order, *slabs, enter, leave, out_enter, out_leave)


def slabs_out_kernel(order_ref, gateup_ref, down_ref, out_ref):
    height, columns = gateup_ref.shape
    padded, width = down_ref.shape
    out_ref[0, :height, :] = gateup_ref[...]
    where, extra = blocks_of(padded, width, columns)
    out_ref[0, height + extra - 16 :, :] = jnp.zeros((16, columns), BF)
    for r, c, row, lane in where:
        value = down_ref[r : r + 16, c : c + 128]
        out_ref[0, height + row : height + row + 16, lane : lane + 128] = value


def slabs_out_pass(order, gateup, down, parts):
    columns, width = gateup.shape[1], down.shape[1]
    height, padded = gateup.shape[0] // parts, down.shape[0] // parts
    rows = height + blocks_of(padded, width, columns)[1]
    count = order.shape[0]
    return pl.pallas_call(
        slabs_out_kernel,
        grid_spec=pltpu.PrefetchScalarGridSpec(
            num_scalar_prefetch=1,
            grid=(count,),
            in_specs=[
                pl.BlockSpec((height, columns), lambda i, o: (o[i], 0)),
                pl.BlockSpec((padded, width), lambda i, o: (o[i], 0)),
            ],
            out_specs=pl.BlockSpec((1, rows, columns), lambda i, o: (i, 0, 0)),
        ),
        out_shape=jax.ShapeDtypeStruct((count, rows, columns), BF),
        compiler_params=MEMORY,
        cost_estimate=FREE,
    )(order, gateup, down)


def sides_kernel(order_ref, *refs):
    enters, grad_ref = refs[:4], refs[4]
    downs = refs[5:-2]
    lines = 2 * enters[0].shape[1]
    shard = grad_ref.shape[1] // 2
    for side, out_ref in enumerate(refs[-2:]):
        team = out_ref.shape[0]
        lines = enters[0].shape[1] // team
        for half in range(2):
            value = outer_sum(
                enters[2 * half + side][...], grad_ref[:, half * shard : (half + 1) * shard]
            ).astype(BF)
            for seat in range(team):
                out_ref[seat, :lines, half * shard : (half + 1) * shard] = value[
                    seat * lines : (seat + 1) * lines
                ]
        if downs:
            value = through(downs[side][...], downs[2][...]).astype(BF)
            rank = value.shape[1]
            padded = value.shape[0] // team
            for seat in range(team):
                for row in range(0, padded, 16):
                    start = row // 16 * rank
                    first = seat * padded + row
                    out_ref[seat, lines : lines + 16, start : start + rank] = value[
                        first : first + 16
                    ]


def sides_pass(order, enter, grad, down, down_leave, team, together):
    width, columns = grad.shape
    half = enter.shape[1] // 4

    def near_or_far(rows, wide, at):
        return pl.BlockSpec((rows, wide), at)

    specs = [
        pl.BlockSpec((width, half), lambda i, o: (0, o[0])),
        pl.BlockSpec((width, half), lambda i, o: (0, o[1])),
        pl.BlockSpec((width, half), lambda i, o: (0, 2 + o[0])),
        pl.BlockSpec((width, half), lambda i, o: (0, 2 + o[1])),
        held(grad),
    ]
    arrays = [enter] * 4 + [grad]
    lines = half // team
    if together:
        lines += 16
        rows = down.shape[0] // 2
        specs += [
            pl.BlockSpec((rows, down.shape[1]), lambda i, o: (o[0], 0)),
            pl.BlockSpec((rows, down.shape[1]), lambda i, o: (o[1], 0)),
            held(down_leave),
        ]
        arrays += [down, down, down_leave]
    shape = (team, lines, columns)
    return pl.pallas_call(
        sides_kernel,
        grid_spec=pltpu.PrefetchScalarGridSpec(
            num_scalar_prefetch=1,
            grid=(1,),
            in_specs=specs,
            out_specs=[pl.BlockSpec(shape, lambda i, o: (0, 0, 0))] * 2,
        ),
        out_shape=[jax.ShapeDtypeStruct(shape, BF)] * 2,
        compiler_params=MEMORY,
        cost_estimate=FREE,
    )(order, *arrays)


def home_kernel(piece, near_ref, far_ref, mine_ref, other_ref, dealt_ref, down_ref):
    team, total, columns = dealt_ref.shape
    lines = mine_ref.shape[1]
    height = total - lines
    base = team * height
    for seat in range(team):
        rest = mine_ref[seat].astype(F32) + other_ref[seat].astype(F32)
        dealt_ref[seat, :lines, :] = rest.astype(BF)
        rows = slice(seat * height, (seat + 1) * height)
        value = near_ref[rows, :].astype(F32) + far_ref[rows, :].astype(F32)
        dealt_ref[seat, lines:total, :] = value.astype(BF)
    width = down_ref.shape[1]
    for r, c, row, lane in blocks_of(even(piece), width, columns)[0]:
        rows, lanes = slice(base + row, base + row + 16), slice(lane, lane + 128)
        value = near_ref[rows, lanes].astype(F32) + far_ref[rows, lanes].astype(F32)
        size = min(16, piece - r)
        down_ref[r : r + size, c : c + 128] = value[:size]


def home_pass(near, far, mine, other, piece, width, height):
    team, lines, columns = mine.shape
    return pl.pallas_call(
        lambda *refs: home_kernel(piece, *refs),
        out_shape=[
            jax.ShapeDtypeStruct((team, lines + height, columns), BF),
            jax.ShapeDtypeStruct((piece, width), F32),
        ],
        compiler_params=MEMORY,
        cost_estimate=FREE,
    )(near, far, mine, other)


def join_kernel(piece, padded, in_ref, *outs):
    team, total, columns = in_ref.shape
    units, shard = outs[0].shape[1] // 2, columns // 2
    lines = outs[0].shape[0]
    for out_ref, row in ((outs[0], 0), (outs[1], total - outs[1].shape[0])):
        height = out_ref.shape[0]
        for half in range(2):
            for block in range(shard // padded):
                first = half * shard + block * padded
                parts = [
                    in_ref[seat, row : row + height, first : first + piece] for seat in range(team)
                ]
                start = half * units + block * team * piece
                joined = jnp.concatenate(parts, axis=1).astype(F32)
                out_ref[:, start : start + team * piece] = joined
    if len(outs) == 3:
        rank = outs[2].shape[1]
        for seat in range(team):
            for row in range(0, padded, 16):
                size = min(16, piece - row)
                start = row // 16 * rank
                value = in_ref[seat, lines : lines + size, start : start + rank]
                first = seat * piece + row
                outs[2][first : first + size, :] = value.astype(F32)


def join_pass(parts, lines, height, piece, padded, rank):
    team, total, columns = parts.shape
    wide = columns // padded * piece * team
    shapes = [(lines, wide), (height, wide)]
    if total > lines + height:
        shapes.append((team * piece, rank))
    return pl.pallas_call(
        lambda *refs: join_kernel(piece, padded, *refs),
        out_shape=[jax.ShapeDtypeStruct(shape, F32) for shape in shapes],
        compiler_params=MEMORY,
        cost_estimate=FREE,
    )(parts)


def per_device(
    tokens,
    cotangent,
    exit_depth,
    lengths,
    loop_index,
    attn_gain,
    mlp_gain,
    qkv_weight,
    out_weight,
    gateup_weight,
    down_weight,
    qkv_enter,
    query_leave,
    kv_leave,
    out_enter,
    out_leave,
    gateup_enter,
    gateup_leave,
    down_enter,
    down_leave,
):
    loops = lax.axis_size("depth")
    rows = lax.axis_size("rows")
    group = lax.axis_index("depth")
    place = lax.axis_index("rows")
    slots, seq_dev, width = tokens.shape
    sub = rows // slots
    team = rows // 2
    count = slots * seq_dev
    teams = [[h * team + k for k in range(team)] for h in range(2)]
    seq_here, mate, core = place // sub, place % sub, place % 2
    side, seat = place // team, place % team
    levels = jnp.arange(loops, dtype=jnp.int32)

    head = kv_leave.shape[2] // 2
    width_q = query_leave.shape[2]
    rank = qkv_enter.shape[2] // 3
    hidden_units = gateup_weight.shape[1] // 2
    piece = down_weight.shape[0]
    padded = -(-piece // 16) * 16
    shard = 2 * loops * padded
    slab = width // (2 * loops)
    gain_size = attn_gain.shape[0]

    def turn(values):
        return jnp.stack(
            [values[0]] + [swap(values[f], "rows", f * sub) for f in range(1, slots)]
        )

    def deal(values):
        return lax.all_to_all(
            values, "rows", split_axis=0, concat_axis=0, axis_index_groups=teams, tiled=True
        )

    def pick(array, index):
        return array.at[index].get(mode="promise_in_bounds")

    def halve(array, bit):
        half = array.shape[0] // 2
        return array[:half], swap(array[half:], "rows", bit)

    def halve_but_last(array, bits):
        for bit in bits[:-1]:
            array = add_low(*halve(array, bit))
        return array

    def own_half(array, which):
        height = array.shape[0] // 2
        return lax.dynamic_slice(array, (which * height, 0), (height, array.shape[1]))

    def positions_of(who):
        blocks = (seq_here ^ levels) * sub + who
        return (blocks[:, None] * seq_dev + jnp.arange(seq_dev, dtype=jnp.int32)[None, :]).reshape(
            count
        )

    depth_flips = [0, 1, 2, 3]
    halves_order = jnp.stack([(group ^ f) * 2 + (core ^ e) for f in depth_flips for e in (0, 1)])
    flips = [(d, f) for d in range(4) for f in range(2)]
    slab_at = {(d, f): (group ^ d) * 2 + (side ^ f) for d, f in flips}
    team_bits, sub_bits, row_bits = bits_of(team), bits_of(sub), bits_of(rows)
    bands = [(0, width_q), (width_q, head), (width_q + head, head)]
    together = team == loops
    lines = gateup_leave.shape[1]
    with_enter = lines + 16 if together else lines

    table = loop_index.reshape(loops, loops)
    mine = lax.dynamic_index_in_dim(table, group, 0, keepdims=False)
    order = jnp.sum((mine[None, :] == levels[:, None]).astype(jnp.int32) * levels[None, :], axis=1)
    sizes_here = jnp.sum(jnp.where(table == group, lengths.reshape(loops, loops), 0), axis=1)
    size_here = lax.dynamic_slice(sizes_here, (seq_here,), (1,))
    positions = positions_of(mate)
    cosine, sine = angles(positions.astype(F32), head)
    gains = jnp.concatenate([attn_gain, mlp_gain])[None]
    gains = jnp.concatenate([gains] + [swap(gains, "depth", f) for f in depth_flips[1:]])
    gains = pick(gains, group ^ levels)
    small = [
        qkv_weight,
        qkv_enter[0],
        jnp.concatenate([query_leave[0], kv_leave[0]], axis=1),
        out_weight,
        out_enter[0],
        out_leave[0],
        gains,
    ]
    small_shapes = [array.shape for array in small]
    late = [gateup_enter[0], down_leave[0]]
    late_shapes = [array.shape for array in late]
    late_packed = pack_pass(late)
    packed = lax.all_gather(pack_pass(small), "rows", axis=0, tiled=True)
    arrived = lax.all_to_all(
        pick(tokens, order), "depth", split_axis=0, concat_axis=0, tiled=True
    )
    dealt = deal_pass(
        [gateup_weight, gateup_leave[0]] + [down_enter[0]] * together, team, piece, padded
    )
    upstream_low = turn(pick(cotangent, seq_here ^ levels)).reshape(count, width)
    arrived, dealt, upstream_low = tie(arrived, dealt, upstream_low)
    inputs = turn(pick(arrived, seq_here ^ levels)).reshape(count, width)
    dealt = deal(dealt)
    inputs, dealt, packed, upstream_low = tie(inputs, dealt, packed, upstream_low)

    slab_near, rest_near = slab_pass(dealt, down_weight, with_enter, padded)
    slab_far = swap(slab_near, "rows", team)
    (
        qkv_slab,
        full_qkv_enter,
        full_leave,
        out_slab,
        full_out_enter,
        full_out_leave,
        gain_slab,
    ) = unpack_pass([packed], small_shapes, BF)
    gain_slab = gain_slab.reshape(rows, loops, 2, -1)
    both_gains = gain_slab.transpose(2, 1, 0, 3).reshape(2, 1, width).astype(F32)
    gain_one, gain_two = both_gains[0], both_gains[1]
    spare = qkv_slab.shape[1] - width

    def both_halves(which):
        return jnp.concatenate(
            [own_half(qkv_slab, which), jnp.pad(own_half(out_slab, which), ((0, 0), (0, spare)))]
        )

    half_here = both_halves(core)
    fetched = [swap(half_here, "depth", f) for f in depth_flips[1:]]
    fetched, slab_near, slab_far, upstream_low, rest_near = tie(
        fetched, slab_near, slab_far, upstream_low, rest_near
    )
    others = swap(jnp.stack(fetched), "rows", 1)
    others, slab_near, rest_near = tie(others, slab_near, rest_near)
    rest_far = swap(rest_near, "rows", team)
    slabs = {(0, 0): slab_near, (0, 1): slab_far}
    slabs[(1, 0)] = swap(slab_near, "depth", 1)
    slabs[(2, 0)] = swap(slab_near, "depth", 2)
    halves = [half_here, both_halves(core ^ 1)]
    for f in range(3):
        halves += [fetched[f], others[f]]
    qkv_eff, out_eff = fold_attn_pass(
        halves_order, halves, full_qkv_enter, full_leave, full_out_enter, full_out_leave, bands
    )
    normed_one, queries, pairs_all = enter_pass(
        inputs, gain_one, qkv_eff, cosine, sine, width_q
    )
    pairs_all, rest_far, slabs, upstream_low, late_packed = tie(
        pairs_all, rest_far, slabs, upstream_low, late_packed
    )
    late_packed = lax.all_gather(late_packed, "rows", axis=0, tiled=True)
    cotan_far = swap(upstream_low, "rows", team_bits[-1])
    slabs[(1, 1)] = swap(slabs[(0, 1)], "depth", 1)
    slabs[(2, 1)] = swap(slabs[(0, 1)], "depth", 2)
    mates = [0]
    for bit in sub_bits:
        pairs_all = jnp.concatenate([pairs_all, swap(pairs_all, "rows", bit)])
        mates = mates + [f | bit for f in mates]
    key_pos = jnp.concatenate([positions_of(mate ^ f) for f in mates])[None]
    attended, log_total = attend_pass(
        size_here, queries, pairs_all, positions[:, None], key_pos, seq_dev
    )
    mixed, normed_two = leave_pass(inputs, attended, out_eff, gain_two)
    normed_two, slabs, cotan_far = tie(normed_two, slabs, cotan_far)

    slabs[(3, 0)] = swap(slabs[(1, 0)], "depth", 2)

    def gather_team(value, far):
        value = jnp.concatenate([value, far])
        for bit in team_bits[-2::-1]:
            value = jnp.concatenate([value, swap(value, "rows", bit)])
        return value

    normed_far = swap(normed_two, "rows", team_bits[-1])
    slabs[(3, 1)] = swap(slabs[(2, 1)], "depth", 1)
    normed_far, slabs = tie(normed_far, slabs)
    cotan_team = gather_team(upstream_low, cotan_far)
    normed_team = gather_team(normed_two, normed_far)
    full_gateup_enter, full_down_leave = unpack_pass([late_packed], late_shapes, BF)
    leave_full, *enter_full = assemble_pass(
        side[None], rest_near, rest_far, lines, shard, rank
    )
    if together:
        enter_full = enter_full[0]
    else:
        enter_every = lax.all_gather(down_enter[0], "rows", axis=0, tiled=True)
        enter_every = enter_every.reshape(loops, 2, team, piece, rank)
        enter_full = lax.dynamic_index_in_dim(enter_every, seat, 2, keepdims=False)
        enter_full = jnp.pad(enter_full, ((0, 0), (0, 0), (0, padded - piece), (0, 0)))
        enter_full = enter_full.reshape(shard, rank)
    gateup_eff, down_eff = fold_ff_pass(
        jnp.stack([slab_at[f] for f in flips]),
        [slabs[f] for f in flips],
        full_gateup_enter,
        leave_full,
        enter_full,
        full_down_leave,
        padded,
    )

    hidden, grad_expanded, grad_normed = ff_pass(
        normed_team, cotan_team, gateup_eff, down_eff, 256
    )

    grad_normed = halve_but_last(grad_normed, team_bits)
    grad_normed, hidden, grad_expanded = tie(grad_normed, hidden, grad_expanded)
    grad_terms = halve(grad_normed, team_bits[-1])
    grad_gateup = outer_sum(normed_team, grad_expanded).astype(BF)
    grad_down = outer_sum(hidden, cotan_team).astype(BF)
    grad_terms, grad_gateup, grad_down, hidden = tie(grad_terms, grad_gateup, grad_down, hidden)

    def slabs_out(*which):
        index = jnp.stack([slab_at[f] for f in which])
        return slabs_out_pass(index, grad_gateup, grad_down, 2 * loops)

    near_sent, far_sent = slabs_out((2, 0), (3, 0)), slabs_out((1, 1), (3, 1))
    near_sent, far_sent, grad_gateup, grad_down = tie(
        near_sent, far_sent, grad_gateup, grad_down
    )
    near_got = swap(near_sent, "depth", 2)
    far_got = swap(far_sent, "depth", 1)
    sides = jnp.stack([side, side ^ 1])
    side_near, side_far = sides_pass(
        sides, full_gateup_enter, grad_gateup, grad_down, full_down_leave, team, together
    )
    side_near, side_far, grad_terms, hidden = tie(side_near, side_far, grad_terms, hidden)
    side_got = swap(side_far, "rows", team)
    grad_mixed, grad_branch, grad_attended, grad_gain_second = leave_back_pass(
        *grad_terms, mixed, gain_two, upstream_low, out_eff
    )
    grad_queries, key_terms = attend_back_pass(
        size_here,
        queries,
        pairs_all,
        grad_attended,
        log_total,
        positions[:, None],
        key_pos,
        cosine,
        sine,
        seq_dev,
    )
    mate_order = halving_order(sub_bits)
    if mate_order != mates:
        key_terms = jnp.concatenate(
            [key_terms[i * count : (i + 1) * count] for i in map(mates.index, mate_order)]
        )
    outcome = matmul(hidden, down_eff).astype(BF)
    near_kept, far_kept = slabs_out((0, 0), (1, 0)), slabs_out((0, 1), (2, 1))
    key_terms, grad_queries, near_got, far_got, outcome, near_kept, far_kept, side_got = tie(
        key_terms, grad_queries, near_got, far_got, outcome, near_kept, far_kept, side_got
    )
    pair_terms = halve(halve_but_last(key_terms, sub_bits), sub_bits[-1])
    outcome = halve_but_last(outcome, team_bits)
    pair_terms, outcome = tie(pair_terms, outcome)

    grad_joined, grad_inputs, grad_gain_first = enter_back_pass(
        grad_queries, pair_terms, cosine, sine, qkv_eff, inputs, gain_one, grad_mixed
    )
    near_one, far_one = add_low(near_kept[1], near_got[1]), add_low(far_kept[1], far_got[1])
    near_one, far_one = swap(near_one, "depth", 1), swap(far_one, "depth", 2)
    outcome = halve(outcome, team_bits[-1])
    grad_qkv = outer_sum(normed_one, grad_joined).astype(BF)
    grad_out = outer_sum(attended, grad_branch).astype(BF)

    near_one, far_one, outcome, grad_inputs, grad_qkv, grad_out = tie(
        near_one, far_one, outcome, grad_inputs, grad_qkv, grad_out
    )

    def loop_part(flip):
        parts = []
        for array in (grad_qkv, grad_out):
            height = array.shape[0] // loops
            part = lax.dynamic_slice(array, ((group ^ flip) * height, 0), (height, array.shape[1]))
            parts.append(jnp.pad(part, ((0, 0), (0, grad_qkv.shape[1] - array.shape[1]))))
        return jnp.concatenate(parts)

    terms = [loop_part(0)] + [swap(loop_part(f), "depth", f) for f in depth_flips[1:]]
    near_sum = add_low(near_kept[0], near_got[0])
    far_sum = add_low(far_kept[0], far_got[0])
    result = mixed + (outcome[0].astype(F32) + outcome[1].astype(F32))
    result_low = result.astype(BF)
    near_sum, far_sum = add_low(near_sum, near_one), add_low(far_sum, far_one)
    far_sum = swap(far_sum, "rows", team)
    result_low, grad_qkv, grad_out, near_sum, far_sum, terms = tie(
        result_low, grad_qkv, grad_out, near_sum, far_sum, terms
    )

    dealt, grad_down_weight = home_pass(
        near_sum, far_sum, side_near, side_got, piece, width, slab // team
    )
    homeward = jnp.concatenate(
        [result_low.reshape(slots, seq_dev, width), grad_inputs.reshape(slots, seq_dev, width)],
        axis=1,
    )

    homeward, dealt = tie(homeward, dealt)
    homeward = turn(homeward)
    dealt = deal(dealt)
    row_place = jnp.arange(rows, dtype=jnp.int32)

    def to_owner(packed):
        return lax.psum_scatter(packed, "rows", scatter_dimension=0, tiled=True)

    qkv_rows = grad_qkv.shape[0] // loops
    rest_grads_of = [
        ((terms[0].shape[0] - qkv_rows) // rows, width),
        (grad_out.shape[0] // rows, rank),
        (rank // rows, width),
        (width // rows, rank),
        (width // rows, rank),
        (rank // rows, width),
    ]
    rest_sum = grads_pass(
        lambda *refs: rest_grads_kernel(qkv_rows, *refs),
        row_place,
        rows,
        rest_grads_of,
        [
            *terms,
            grad_out,
            full_out_enter,
            full_out_leave,
            grad_gateup,
            leave_full,
            grad_down,
            enter_full,
        ],
    )
    rest_sum = to_owner(rest_sum)
    attn_grads_of = attn_grads_shapes(rows, qkv_rows, grad_qkv, full_qkv_enter, full_leave, bands)
    attn_sum = grads_pass(
        lambda *refs: attn_grads_kernel(qkv_rows, bands, *refs),
        row_place,
        rows,
        attn_grads_of,
        [*terms, grad_qkv, full_qkv_enter, full_leave],
    )
    attn_sum = to_owner(attn_sum)
    homeward, dealt = tie(homeward, dealt)
    returned = lax.all_to_all(
        pick(homeward[:, seq_dev:], seq_here ^ levels),
        "depth",
        split_axis=0,
        concat_axis=0,
        tiled=True,
    )

    grad_tokens = pick(returned, mine)
    activations = pick(homeward[:, :seq_dev], seq_here ^ levels)
    own_out, *rest_parts = unpack_pass([rest_sum], rest_grads_of, F32)
    own_qkv, *attn_parts = unpack_pass([attn_sum], attn_grads_of, F32)
    attn_grads = [
        jnp.concatenate(attn_parts[:3], axis=1),
        attn_parts[3],
        jnp.concatenate(attn_parts[4:], axis=1),
    ]
    rest_grads = rest_parts[:2] + [jnp.concatenate(rest_parts[2:4], axis=1), rest_parts[4]]
    grad_gateup_leave, grad_gateup_weight, *grad_down_enter = join_pass(
        dealt, lines, slab // team, piece, padded, rank
    )
    if together:
        grad_down_enter = grad_down_enter[0]
    else:
        grad_down_in = through(grad_down, full_down_leave).astype(BF)
        grad_down_in = grad_down_in.reshape(loops, 2, 1, padded, rank)[:, :, :, :piece]
        spaced = jnp.zeros((loops, 2, team, piece, rank), BF)
        spaced = lax.dynamic_update_slice(spaced, grad_down_in, (0, 0, seat, 0, 0))
        grad_down_enter = lax.psum_scatter(
            spaced.reshape(hidden_units, rank), "rows", scatter_dimension=0, tiled=True
        ).astype(F32)

    block_pos = place * seq_dev + jnp.arange(seq_dev, dtype=jnp.int32)
    valid = block_pos[None, :] < sizes_here[:, None]
    counts_here = jnp.sum(
        ((exit_depth[None] == levels[:, None, None]) & valid[None]).astype(F32), axis=(1, 2)
    )
    given = inputs.astype(F32)
    cross = jnp.sum(given * result, axis=-1)
    own_sq = jnp.sum(given * given, axis=-1)
    out_sq = jnp.sum(result * result, axis=-1)
    cosines = cross * lax.rsqrt(own_sq * out_sq + 1e-06)
    cosine_here = jnp.sum(jnp.where(positions < size_here, cosines, 0.0))
    tallies = jnp.concatenate([counts_here, cosine_here[None]])
    gain_grads = jnp.concatenate([grad_gain_first, grad_gain_second])
    gain_grads = gain_grads.reshape(2, loops * rows, gain_size).transpose(1, 0, 2)
    small = jnp.concatenate(
        [
            jnp.broadcast_to(tallies[None], (loops * rows, loops + 1)),
            gain_grads.reshape(loops * rows, 2 * gain_size),
        ],
        axis=1,
    )
    small = jnp.pad(small, ((0, 0), (0, 127 - loops - 2 * gain_size)))
    small = lax.all_to_all(small, ("depth", "rows"), split_axis=0, concat_axis=0, tiled=True)
    small = jnp.sum(small, axis=0)
    tallies = small[: loops + 1]
    gain_grads = small[loops + 1 : loops + 1 + 2 * gain_size].reshape(2, gain_size)
    exit_counts = tallies[:loops].astype(jnp.int32)
    confidence = tallies[loops] / jnp.sum(lengths).astype(F32)

    return (
        activations,
        grad_tokens,
        exit_counts,
        confidence,
        gain_grads[0],
        gain_grads[1],
        own_qkv,
        own_out,
        grad_gateup_weight,
        grad_down_weight,
        attn_grads[0][None],
        attn_grads[1][None],
        attn_grads[2][None],
        rest_grads[0][None],
        rest_grads[1][None],
        rest_grads[2][None],
        grad_gateup_leave[None],
        grad_down_enter[None],
        rest_grads[3][None],
    )


def solution(mesh):
    split = P("depth", "rows", None)
    flat = P(("depth", "rows"))
    tall = P(("depth", "rows"), None)
    return jax.shard_map(
        per_device,
        mesh=mesh,
        in_specs=(split, split, P("depth", "rows"), P(), P(), flat, flat)
        + (tall,) * 4
        + (split,) * 9,
        out_specs=(split, split, P(), P(), flat, flat) + (tall,) * 4 + (split,) * 9,
        check_vma=False,
    )
```

```python
import math

import jax
import jax.numpy as jnp
from jax import lax
from jax.experimental import pallas as pl
from jax.experimental.pallas import tpu as pltpu
from jax.sharding import PartitionSpec as P

BF = jnp.bfloat16
F32 = jnp.float32
ROOT = math.sqrt(2.0 / math.pi)
CUBE = 0.044715


def angles(positions, size):
    freqs = jnp.exp(jnp.arange(size // 2, dtype=F32) * (-2.0 * math.log(10000.0) / size))
    phase = positions[:, None] * freqs[None, :]
    return (jnp.cos(phase), jnp.sin(phase))


def matmul(left, right):
    return jnp.dot(left, right, preferred_element_type=F32)


def outer_sum(left, right):
    return lax.dot_general(left, right, (((0,), (0,)), ((), ())), preferred_element_type=F32)


def through(left, right):
    return lax.dot_general(left, right, (((1,), (1,)), ((), ())), preferred_element_type=F32)


def swap(value, axis, flip):
    size = lax.axis_size(axis)
    return lax.ppermute(value, axis, [(i, i ^ flip) for i in range(size)])


def add_low(left, right):
    return (left.astype(F32) + right.astype(F32)).astype(BF)


def tie(*values):
    return lax.optimization_barrier(values)


def bits_of(size):
    return [1 << i for i in range(size.bit_length() - 1)]


LANES = 256


def even(height):
    return -(-height // 16) * 16


def segments(shapes):
    out, row = [], 0
    for which, (height, columns) in enumerate(shapes):
        for start in range(0, columns, LANES):
            out.append((which, row, start, min(LANES, columns - start)))
            row += even(height)
    return out, row


def put(out_ref, lead, row, height, value):
    short, narrow = even(height) - height, LANES - value.shape[1]
    if narrow:
        value = jnp.concatenate([value, jnp.zeros((height, narrow), value.dtype)], axis=1)
    if short:
        value = jnp.concatenate([value, jnp.zeros((short, LANES), value.dtype)], axis=0)
    out_ref[lead, row : row + even(height), :] = value


def pack_kernel(shapes, *refs):
    where, _ = segments(shapes)
    for which, row, start, size in where:
        put(refs[-1], 0, row, shapes[which][0], refs[which][:, start : start + size])


def pack_pass(arrays):
    shapes = [array.shape for array in arrays]
    return pl.pallas_call(
        lambda *refs: pack_kernel(shapes, *refs),
        out_shape=jax.ShapeDtypeStruct((1, segments(shapes)[1], LANES), BF),
        compiler_params=MEMORY,
        cost_estimate=FREE,
    )(*arrays)


def unpack_kernel(shapes, terms, *refs):
    where, _ = segments(shapes)
    for which, row, start, size in where:
        height = shapes[which][0]
        out_ref = refs[terms + which]
        for lead in range(refs[0].shape[0]):
            value = refs[0][lead, row : row + height, :size]
            if terms > 1:
                value = value.astype(F32) + refs[1][lead, row : row + height, :size].astype(F32)
            first = lead * height
            out_ref[first : first + height, start : start + size] = value.astype(out_ref.dtype)


def unpack_pass(terms, shapes, dtype):
    lead = terms[0].shape[0]
    return pl.pallas_call(
        lambda *refs: unpack_kernel(shapes, len(terms), *refs),
        out_shape=[jax.ShapeDtypeStruct((lead * h, c), dtype) for h, c in shapes],
        compiler_params=MEMORY,
        cost_estimate=FREE,
    )(*terms)


def spread_rows(pos_ref, out_ref, row, value, first, size):
    leads = out_ref.shape[0]
    height = value.shape[0] // leads
    for lead in range(leads):
        block = value[lead * height : (lead + 1) * height, first : first + size]
        put(out_ref, pos_ref[lead], row, height, block.astype(BF))


def total_of(refs, rows, columns):
    total = refs[0][rows, :columns].astype(F32)
    for ref in refs[1:]:
        total = total + ref[rows, :columns].astype(F32)
    return total


def place_all(pos_ref, out_ref, values):
    shapes = [(value.shape[0] // out_ref.shape[0], value.shape[1]) for value in values]
    for which, row, start, size in segments(shapes)[0]:
        spread_rows(pos_ref, out_ref, row, values[which], start, size)


def attn_grads_kernel(height, bands, pos_ref, *refs):
    grad_ref, enter_ref, leave_ref, out_ref = refs[-4:]
    rank = leave_ref.shape[0]
    values = [total_of(refs[:-4], slice(0, height), grad_ref.shape[1])]
    for start, size in bands:
        values.append(through(grad_ref[:, start : start + size], leave_ref[:, start : start + size]))
    for index, (start, size) in enumerate(bands):
        enter = enter_ref[:, index * rank : (index + 1) * rank]
        values.append(outer_sum(enter, grad_ref[:, start : start + size]))
    place_all(pos_ref, out_ref, values)


def attn_grads_shapes(rows, height, grad, enter, leave, bands):
    rank = leave.shape[0]
    return (
        [(height // rows, grad.shape[1])]
        + [(grad.shape[0] // rows, rank)] * len(bands)
        + [(rank // rows, size) for _, size in bands]
    )


def rest_grads_kernel(first, pos_ref, *refs):
    (
        grad_out_ref,
        out_enter_ref,
        out_leave_ref,
        grad_gateup_ref,
        leave_ref,
        grad_down_ref,
        down_enter_ref,
        out_ref,
    ) = refs[-8:]
    shard = leave_ref.shape[1] // 2
    values = [
        total_of(refs[:-8], slice(first, refs[0].shape[0]), grad_out_ref.shape[1]),
        through(grad_out_ref[...], out_leave_ref[...]),
        outer_sum(out_enter_ref[...], grad_out_ref[...]),
        through(grad_gateup_ref[:, :shard], leave_ref[:, :shard]),
        through(grad_gateup_ref[:, shard:], leave_ref[:, shard:]),
        outer_sum(down_enter_ref[...], grad_down_ref[...]),
    ]
    place_all(pos_ref, out_ref, values)


def grads_pass(kernel, pos, rows, shapes, arrays):
    whole = [pl.BlockSpec(memory_space=pltpu.VMEM)] * len(arrays)
    shape = (rows, segments(shapes)[1], LANES)
    return pl.pallas_call(
        kernel,
        in_specs=[pl.BlockSpec(memory_space=pltpu.SMEM)] + whole,
        out_specs=pl.BlockSpec(memory_space=pltpu.VMEM),
        out_shape=jax.ShapeDtypeStruct(shape, BF),
        compiler_params=MEMORY,
        cost_estimate=FREE,
    )(pos, *arrays)


FREE = pl.CostEstimate(flops=0, transcendentals=0, bytes_accessed=0)
MEMORY = pltpu.CompilerParams(vmem_limit_bytes=60 << 20)


def held(array):
    return pl.BlockSpec(
        array.shape, lambda *_: (0,) * len(array.shape), pipeline_mode=pl.Buffered(1)
    )


def strip(tile, columns):
    return pl.BlockSpec((tile, columns), lambda i: (i, 0))


def mean_scale(values):
    return lax.rsqrt(jnp.mean(values * values, axis=-1, keepdims=True) + 1e-06)


def turned(values, cosine, sine):
    half = values.shape[-1] // 2
    first, second = values[:, :half], values[:, half:]
    return jnp.concatenate(
        [first * cosine - second * sine, second * cosine + first * sine], axis=-1
    )


def enter_kernel(x_ref, gain_ref, weight_ref, cos_ref, sin_ref, n_ref, q_ref, kv_ref):
    head = kv_ref.shape[1] // 2
    width_q = q_ref.shape[1]
    values = x_ref[...].astype(F32)
    normed = (values * mean_scale(values) * gain_ref[...]).astype(BF)
    n_ref[...] = normed
    joined = matmul(normed, weight_ref[...])
    cosine, sine = cos_ref[...], sin_ref[...]
    scale = head ** (-0.5)
    for start in range(0, width_q, head):
        spun = turned(joined[:, start : start + head], cosine, sine)
        q_ref[:, start : start + head] = (spun * scale).astype(BF)
    kv_ref[:, :head] = turned(joined[:, width_q : width_q + head], cosine, sine).astype(BF)
    kv_ref[:, head:] = joined[:, width_q + head :].astype(BF)


def enter_pass(x, gain, weight, cosine, sine, width_q):
    count, width = x.shape
    tile = count // 2
    rest = weight.shape[1] - width_q
    return pl.pallas_call(
        enter_kernel,
        grid=(count // tile,),
        in_specs=[
            strip(tile, width),
            held(gain),
            held(weight),
            strip(tile, cosine.shape[1]),
            strip(tile, cosine.shape[1]),
        ],
        out_specs=[strip(tile, width), strip(tile, width_q), strip(tile, rest)],
        out_shape=[
            jax.ShapeDtypeStruct((count, width), BF),
            jax.ShapeDtypeStruct((count, width_q), BF),
            jax.ShapeDtypeStruct((count, rest), BF),
        ],
        compiler_params=MEMORY,
        cost_estimate=FREE,
    )(x, gain, weight, cosine, sine)


def stack_heads(ref, head):
    return jnp.concatenate(
        [ref[:, start : start + head] for start in range(0, ref.shape[1], head)], axis=0
    )


def allowed_keys(size_ref, pos_ref, key_ref, heads):
    fits = (key_ref[...] <= pos_ref[...]) & (key_ref[...] < size_ref[0])
    return jnp.concatenate([jnp.where(fits, 0.0, -1e30)] * heads, axis=0)


def attend_kernel(size_ref, q_ref, kv_ref, pos_ref, key_ref, o_ref, lse_ref):
    head = kv_ref.shape[1] // 2
    tile = q_ref.shape[0]
    heads = q_ref.shape[1] // head
    scores = through(stack_heads(q_ref, head), kv_ref[:, :head])
    scores = scores + allowed_keys(size_ref, pos_ref, key_ref, heads)
    highest = jnp.max(scores, axis=-1, keepdims=True)
    raised = jnp.exp(scores - highest)
    total = jnp.sum(raised, axis=-1, keepdims=True)
    probs = (raised * (1.0 / total)).astype(BF)
    lse_ref[...] = (highest + jnp.log(total)).reshape(1, heads * tile, 1)
    mixed = matmul(probs, kv_ref[:, head:]).astype(BF)
    for index in range(heads):
        o_ref[:, index * head : (index + 1) * head] = mixed[index * tile : (index + 1) * tile]


def attend_pass(size, q, kv, positions, key_positions, tile):
    count, width_q = q.shape
    heads = 2 * width_q // kv.shape[1]
    steps = count // tile

    def rows(columns):
        return pl.BlockSpec((tile, columns), lambda i, s: (i, 0))

    return pl.pallas_call(
        attend_kernel,
        grid_spec=pltpu.PrefetchScalarGridSpec(
            num_scalar_prefetch=1,
            grid=(steps,),
            in_specs=[rows(width_q), held(kv), rows(1), held(key_positions)],
            out_specs=[rows(width_q), pl.BlockSpec((1, heads * tile, 1), lambda i, s: (i, 0, 0))],
        ),
        out_shape=[
            jax.ShapeDtypeStruct((count, width_q), BF),
            jax.ShapeDtypeStruct((steps, heads * tile, 1), F32),
        ],
        compiler_params=MEMORY,
        cost_estimate=FREE,
    )(size, q, kv, positions, key_positions)


def attend_back_kernel(
    size_ref, q_ref, kv_ref, do_ref, lse_ref, pos_ref, key_ref, cos_ref, sin_ref, dq_ref, dkv_ref, acc
):
    head = kv_ref.shape[1] // 2
    tile = q_ref.shape[0]
    heads = q_ref.shape[1] // head
    step = pl.program_id(0)
    queries = stack_heads(q_ref, head)
    grads = stack_heads(do_ref, head)
    keys = kv_ref[:, :head]
    scores = through(queries, keys) + allowed_keys(size_ref, pos_ref, key_ref, heads)
    probs = jnp.exp(scores - lse_ref[0])
    grad_probs = through(grads, kv_ref[:, head:])
    centre = jnp.sum(probs * grad_probs, axis=-1, keepdims=True)
    grad_scores = (probs * (grad_probs - centre)).astype(BF)
    grad_q = matmul(grad_scores, keys) * (head ** (-0.5))
    cosine, sine = cos_ref[...], -sin_ref[...]
    for index in range(heads):
        spun = turned(grad_q[index * tile : (index + 1) * tile], cosine, sine)
        dq_ref[:, index * head : (index + 1) * head] = spun.astype(BF)
    grad_k = outer_sum(grad_scores, queries)
    grad_v = outer_sum(probs.astype(BF), grads)

    @pl.when(step == 0)
    def _():
        acc[:, :head] = grad_k
        acc[:, head:] = grad_v

    @pl.when(step > 0)
    def _():
        acc[:, :head] += grad_k
        acc[:, head:] += grad_v

    @pl.when(step == pl.num_programs(0) - 1)
    def _():
        dkv_ref[...] = acc[...].astype(BF)


def attend_back_pass(size, q, kv, do, lse, positions, key_positions, cosine, sine, tile):
    count, width_q = q.shape
    heads = 2 * width_q // kv.shape[1]

    def rows(columns):
        return pl.BlockSpec((tile, columns), lambda i, s: (i, 0))

    return pl.pallas_call(
        attend_back_kernel,
        grid_spec=pltpu.PrefetchScalarGridSpec(
            num_scalar_prefetch=1,
            grid=(count // tile,),
            in_specs=[
                rows(width_q),
                held(kv),
                rows(width_q),
                pl.BlockSpec((1, heads * tile, 1), lambda i, s: (i, 0, 0)),
                rows(1),
                held(key_positions),
                rows(cosine.shape[1]),
                rows(cosine.shape[1]),
            ],
            out_specs=[rows(width_q), pl.BlockSpec(kv.shape, lambda i, s: (0, 0))],
            scratch_shapes=[pltpu.VMEM(kv.shape, F32)],
        ),
        out_shape=[jax.ShapeDtypeStruct((count, width_q), BF), jax.ShapeDtypeStruct(kv.shape, BF)],
        compiler_params=MEMORY,
        cost_estimate=FREE,
    )(size, q, kv, do, lse, positions, key_positions, cosine, sine)


def leave_kernel(x_ref, o_ref, weight_ref, gain_ref, h_ref, n_ref):
    mixed = x_ref[...].astype(F32) + matmul(o_ref[...], weight_ref[...])
    h_ref[...] = mixed
    n_ref[...] = (mixed * mean_scale(mixed) * gain_ref[...]).astype(BF)


def leave_pass(x, o, weight, gain):
    count, width = x.shape
    tile = count // 2
    return pl.pallas_call(
        leave_kernel,
        grid=(count // tile,),
        in_specs=[strip(tile, width), strip(tile, o.shape[1]), held(weight), held(gain)],
        out_specs=[strip(tile, width)] * 2,
        out_shape=[jax.ShapeDtypeStruct((count, width), d) for d in (F32, BF)],
        compiler_params=MEMORY,
        cost_estimate=FREE,
    )(x, o, weight, gain)


def norm_grad(grad, values, gain):
    scaling = mean_scale(values)
    unit = values * scaling
    lifted = grad * gain
    back = scaling * (lifted - unit * jnp.mean(lifted * unit, axis=-1, keepdims=True))
    return back, jnp.sum(grad * unit, axis=0, keepdims=True)


def add_step(ref, value):
    @pl.when(pl.program_id(0) == 0)
    def _():
        ref[...] = value

    @pl.when(pl.program_id(0) > 0)
    def _():
        ref[...] += value


def leave_back_kernel(
    one_ref, two_ref, h_ref, gain_ref, dy_ref, weight_ref, dh_ref, dz_ref, do_ref, dgain_ref
):
    grad = one_ref[...].astype(F32) + two_ref[...].astype(F32)
    back, gain_sum = norm_grad(grad, h_ref[...], gain_ref[...])
    total = dy_ref[...].astype(F32) + back
    dh_ref[...] = total
    low = total.astype(BF)
    dz_ref[...] = low
    do_ref[...] = through(low, weight_ref[...]).astype(BF)
    add_step(dgain_ref, gain_sum)


def leave_back_pass(one, two, h, gain, dy, weight):
    count, width = h.shape
    tile = count // 2
    width_q = weight.shape[0]
    return pl.pallas_call(
        leave_back_kernel,
        grid=(count // tile,),
        in_specs=[strip(tile, width)] * 3 + [held(gain), strip(tile, width), held(weight)],
        out_specs=[strip(tile, width)] * 2
        + [strip(tile, width_q), pl.BlockSpec((1, width), lambda i: (0, 0))],
        out_shape=[
            jax.ShapeDtypeStruct((count, width), F32),
            jax.ShapeDtypeStruct((count, width), BF),
            jax.ShapeDtypeStruct((count, width_q), BF),
            jax.ShapeDtypeStruct((1, width), F32),
        ],
        compiler_params=MEMORY,
        cost_estimate=FREE,
    )(one, two, h, gain, dy, weight)


def enter_back_kernel(dq_ref, *refs):
    parts = refs[:-9]
    cos_ref, sin_ref, weight_ref, x_ref, gain_ref, dh_ref, joined_ref, dx_ref, dgain_ref = refs[-9:]
    head = parts[0].shape[1] // 2
    width_q = dq_ref.shape[1]
    pair = parts[0][...].astype(F32)
    for part in parts[1:]:
        pair = pair + part[...].astype(F32)
    joined_ref[:, :width_q] = dq_ref[...]
    spun = turned(pair[:, :head], cos_ref[...], -sin_ref[...])
    joined_ref[:, width_q : width_q + head] = spun.astype(BF)
    joined_ref[:, width_q + head :] = pair[:, head:].astype(BF)
    grad = through(joined_ref[...], weight_ref[...])
    back, gain_sum = norm_grad(grad, x_ref[...].astype(F32), gain_ref[...])
    dx_ref[...] = (dh_ref[...] + back).astype(BF)
    add_step(dgain_ref, gain_sum)


def enter_back_pass(dq, parts, cosine, sine, weight, x, gain, dh):
    count, width = x.shape
    tile = count // 2
    width_q = dq.shape[1]
    return pl.pallas_call(
        enter_back_kernel,
        grid=(count // tile,),
        in_specs=[strip(tile, width_q)]
        + [strip(tile, part.shape[1]) for part in parts]
        + [strip(tile, cosine.shape[1])] * 2
        + [held(weight), strip(tile, width), held(gain), strip(tile, width)],
        out_specs=[
            strip(tile, weight.shape[1]),
            strip(tile, width),
            pl.BlockSpec((1, width), lambda i: (0, 0)),
        ],
        out_shape=[
            jax.ShapeDtypeStruct((count, weight.shape[1]), BF),
            jax.ShapeDtypeStruct((count, width), BF),
            jax.ShapeDtypeStruct((1, width), F32),
        ],
        compiler_params=MEMORY,
        cost_estimate=FREE,
    )(dq, *parts, cosine, sine, weight, x, gain, dh)


def halving_order(bits):
    order = [0]
    for bit in reversed(bits):
        order = order + [flip | bit for flip in order]
    return order


def ff_kernel(n2_ref, df_ref, wg_ref, wd_ref, a_ref, dg_ref, dn_ref):
    hidden = wd_ref.shape[0]
    n2 = n2_ref[...]
    gate = matmul(n2, wg_ref[:, :hidden])
    upper = matmul(n2, wg_ref[:, hidden:])
    grad = through(df_ref[...], wd_ref[...])
    square = gate * gate
    bent = jnp.tanh(gate * (ROOT + ROOT * CUBE * square))
    half = 0.5 + 0.5 * bent
    act = gate * half
    a_ref[...] = (act * upper).astype(BF)
    slope = half + 0.5 * gate * (1.0 - bent * bent) * (ROOT + 3.0 * ROOT * CUBE * square)
    dg_ref[:, :hidden] = (grad * upper * slope).astype(BF)
    dg_ref[:, hidden:] = (grad * act).astype(BF)
    dn_ref[...] = through(dg_ref[...], wg_ref[...]).astype(BF)


def ff_pass(n2, df, wg, wd, tile):
    count, width = n2.shape
    hidden = wd.shape[0]

    return pl.pallas_call(
        ff_kernel,
        grid=(count // tile,),
        in_specs=[strip(tile, width), strip(tile, width), held(wg), held(wd)],
        out_specs=[strip(tile, hidden), strip(tile, 2 * hidden), strip(tile, width)],
        out_shape=[
            jax.ShapeDtypeStruct((count, hidden), BF),
            jax.ShapeDtypeStruct((count, 2 * hidden), BF),
            jax.ShapeDtypeStruct((count, width), BF),
        ],
        compiler_params=MEMORY,
        cost_estimate=FREE,
    )(n2, df, wg, wd)


def blocks_of(padded, width, columns):
    across = columns // 128
    wide = width // 128
    out = []
    for r in range(padded // 16):
        for c in range(wide):
            out.append((16 * r, 128 * c, 16 * ((r * wide + c) // across), 128 * ((r * wide + c) % across)))
    return out, 16 * (-(-len(out) // across))


def tall(value, height):
    short = height - value.shape[0]
    if not short:
        return value
    return jnp.concatenate([value, jnp.zeros((short, value.shape[1]), value.dtype)], axis=0)


def deal_kernel(piece, padded, *refs):
    gateup_ref, leave_ref, out_ref = refs[0], refs[1], refs[-1]
    team, total, columns = out_ref.shape
    units, shard = gateup_ref.shape[1] // 2, columns // 2
    lines = leave_ref.shape[0]
    for in_ref, row in ((leave_ref, 0), (gateup_ref, total - gateup_ref.shape[0])):
        height = in_ref.shape[0]
        gap = jnp.zeros((height, padded - piece), in_ref.dtype)
        for half in range(2):
            for seat in range(team):
                parts = []
                for block in range(shard // padded):
                    start = half * units + (block * team + seat) * piece
                    parts += [in_ref[:, start : start + piece], gap]
                joined = jnp.concatenate(parts, axis=1)
                out_ref[seat, row : row + height, half * shard : (half + 1) * shard] = joined
    if len(refs) == 4:
        rank = refs[2].shape[1]
        for seat in range(team):
            for row in range(0, padded, 16):
                first = seat * piece + row
                value = tall(refs[2][first : first + min(16, piece - row), :], 16)
                start = row // 16 * rank
                out_ref[seat, lines : lines + 16, start : start + rank] = value


def deal_pass(arrays, team, piece, padded):
    lines = sum(array.shape[0] for array in arrays[:2]) + 16 * (len(arrays) == 3)
    columns = arrays[0].shape[1] // (team * piece) * padded
    return pl.pallas_call(
        lambda *refs: deal_kernel(piece, padded, *refs),
        out_shape=jax.ShapeDtypeStruct((team, lines, columns), BF),
        compiler_params=MEMORY,
        cost_estimate=FREE,
    )(*arrays)


def slab_kernel(padded, dealt_ref, down_ref, slab_ref, rest_ref):
    team, total, columns = dealt_ref.shape
    lines = rest_ref.shape[1]
    height = total - lines
    piece, width = down_ref.shape
    base = team * height
    for seat in range(team):
        slab_ref[seat * height : (seat + 1) * height, :] = dealt_ref[seat, lines:total, :]
        rest_ref[seat] = dealt_ref[seat, :lines, :]
    where, extra = blocks_of(padded, width, columns)
    slab_ref[base + extra - 16 : base + extra, :] = jnp.zeros((16, columns), BF)
    for r, c, row, lane in where:
        value = tall(down_ref[r : r + min(16, piece - r), c : c + 128], 16)
        slab_ref[base + row : base + row + 16, lane : lane + 128] = value


def slab_pass(dealt, down, lines, padded):
    team, total, columns = dealt.shape
    extra = blocks_of(padded, down.shape[1], columns)[1]
    return pl.pallas_call(
        lambda *refs: slab_kernel(padded, *refs),
        out_shape=[
            jax.ShapeDtypeStruct((team * (total - lines) + extra, columns), BF),
            jax.ShapeDtypeStruct((team, lines, columns), BF),
        ],
        compiler_params=MEMORY,
        cost_estimate=FREE,
    )(dealt, down)


def assemble_kernel(lines, side_ref, near_ref, far_ref, *outs):
    team = near_ref.shape[0]

    def fill(half, ref):
        for seat in range(team):
            first = (half * team + seat) * lines
            outs[0][first : first + lines, :] = ref[seat, :lines, :]
            if len(outs) == 2:
                rank = outs[1].shape[1]
                padded = outs[1].shape[0] // (2 * team)
                for row in range(0, padded, 16):
                    start = row // 16 * rank
                    first = (half * team + seat) * padded + row
                    outs[1][first : first + 16, :] = ref[
                        seat, lines : lines + 16, start : start + rank
                    ]

    for half in range(2):

        @pl.when(side_ref[0] == half)
        def _(half=half):
            fill(half, near_ref)
            fill(1 - half, far_ref)


def assemble_pass(side, near, far, lines, shard, rank):
    team, height, columns = near.shape
    shapes = [jax.ShapeDtypeStruct((2 * team * lines, columns), BF)]
    if height > lines:
        shapes.append(jax.ShapeDtypeStruct((shard, rank), BF))
    vmem = pl.BlockSpec(memory_space=pltpu.VMEM)
    return pl.pallas_call(
        lambda *refs: assemble_kernel(lines, *refs),
        in_specs=[pl.BlockSpec(memory_space=pltpu.SMEM), vmem, vmem],
        out_specs=[vmem] * len(shapes),
        out_shape=shapes,
        compiler_params=MEMORY,
        cost_estimate=FREE,
    )(side, near, far)


def fold_ff_kernel(order_ref, *refs):
    slabs = refs[:-7]
    enter_ref, leave_ref, down_enter_ref, down_leave_ref, gateup_out, down_out, blocks = refs[-7:]
    rank = leave_ref.shape[0]
    height, columns = gateup_out.shape
    shard = columns // 2
    step = pl.program_id(0)
    for index in range(2):
        start = index * shard
        lift = matmul(
            enter_ref[:, index * rank : (index + 1) * rank], leave_ref[:, start : start + shard]
        )
        for which, slab_ref in enumerate(slabs):

            @pl.when(step == which)
            def _(slab_ref=slab_ref, lift=lift, start=start):
                part = slab_ref[:height, start : start + shard].astype(F32)
                gateup_out[:, start : start + shard] = (part + lift).astype(BF)

    for which, slab_ref in enumerate(slabs):

        @pl.when(step == which)
        def _(slab_ref=slab_ref):
            blocks[...] = slab_ref[height:, :]

    lift = matmul(down_enter_ref[...], down_leave_ref[...])
    padded, width = down_out.shape
    wide = width // 128
    where, _ = blocks_of(padded, width, columns)
    for first in range(0, len(where), wide):
        r = where[first][0]
        parts = [
            blocks[row : row + 16, lane : lane + 128]
            for _, _, row, lane in where[first : first + wide]
        ]
        part = jnp.concatenate(parts, axis=1).astype(F32)
        down_out[r : r + 16, :] = (part + lift[r : r + 16]).astype(BF)


def fold_ff_pass(order, slabs, enter, leave, down_enter, down_leave, padded):
    count = len(slabs)
    columns, width = leave.shape[1], down_leave.shape[1]
    height = enter.shape[0] // count

    def own(rows, wide):
        return pl.BlockSpec((rows, wide), lambda i, o: (o[i], 0))

    return pl.pallas_call(
        fold_ff_kernel,
        grid_spec=pltpu.PrefetchScalarGridSpec(
            num_scalar_prefetch=1,
            grid=(count,),
            in_specs=[held(slab) for slab in slabs]
            + [
                own(height, enter.shape[1]),
                held(leave),
                own(padded, down_enter.shape[1]),
                held(down_leave),
            ],
            out_specs=[own(height, columns), own(padded, width)],
            scratch_shapes=[pltpu.VMEM((slabs[0].shape[0] - height, columns), BF)],
        ),
        out_shape=[
            jax.ShapeDtypeStruct((count * height, columns), BF),
            jax.ShapeDtypeStruct((count * padded, width), BF),
        ],
        compiler_params=MEMORY,
        cost_estimate=FREE,
    )(order, *slabs, enter, leave, down_enter, down_leave)


def fold_attn_kernel(bands, order_ref, *refs):
    slabs = refs[:-6]
    enter_ref, leave_ref, out_enter_ref, out_leave_ref, in_out, out_out = refs[-6:]
    rank = leave_ref.shape[0]
    height, width = in_out.shape[0], out_out.shape[1]
    step = pl.program_id(0)
    lifts = [
        matmul(enter_ref[:, i * rank : (i + 1) * rank], leave_ref[:, start : start + size])
        for i, (start, size) in enumerate(bands)
    ]
    out_lift = matmul(out_enter_ref[...], out_leave_ref[...])
    for which, slab_ref in enumerate(slabs):

        @pl.when(step == which)
        def _(slab_ref=slab_ref):
            for (start, size), lift in zip(bands, lifts):
                part = slab_ref[:height, start : start + size].astype(F32)
                in_out[:, start : start + size] = (part + lift).astype(BF)
            part = slab_ref[height:, :width].astype(F32)
            out_out[...] = (part + out_lift).astype(BF)


def fold_attn_pass(order, slabs, enter, leave, out_enter, out_leave, bands):
    count = len(slabs)
    height, short = enter.shape[0] // count, out_enter.shape[0] // count

    def own(rows, wide):
        return pl.BlockSpec((rows, wide), lambda i, o: (o[i], 0))

    return pl.pallas_call(
        lambda *refs: fold_attn_kernel(bands, *refs),
        grid_spec=pltpu.PrefetchScalarGridSpec(
            num_scalar_prefetch=1,
            grid=(count,),
            in_specs=[held(slab) for slab in slabs]
            + [
                own(height, enter.shape[1]),
                held(leave),
                own(short, out_enter.shape[1]),
                held(out_leave),
            ],
            out_specs=[own(height, leave.shape[1]), own(short, out_leave.shape[1])],
        ),
        out_shape=[
            jax.ShapeDtypeStruct((enter.shape[0], leave.shape[1]), BF),
            jax.ShapeDtypeStruct((out_enter.shape[0], out_leave.shape[1]), BF),
        ],
        compiler_params=MEMORY,
        cost_estimate=FREE,
    )(order, *slabs, enter, leave, out_enter, out_leave)


def slabs_out_kernel(order_ref, gateup_ref, down_ref, out_ref):
    height, columns = gateup_ref.shape
    padded, width = down_ref.shape
    out_ref[0, :height, :] = gateup_ref[...]
    where, extra = blocks_of(padded, width, columns)
    out_ref[0, height + extra - 16 :, :] = jnp.zeros((16, columns), BF)
    for r, c, row, lane in where:
        value = down_ref[r : r + 16, c : c + 128]
        out_ref[0, height + row : height + row + 16, lane : lane + 128] = value


def slabs_out_pass(order, gateup, down, parts):
    columns, width = gateup.shape[1], down.shape[1]
    height, padded = gateup.shape[0] // parts, down.shape[0] // parts
    rows = height + blocks_of(padded, width, columns)[1]
    count = order.shape[0]
    return pl.pallas_call(
        slabs_out_kernel,
        grid_spec=pltpu.PrefetchScalarGridSpec(
            num_scalar_prefetch=1,
            grid=(count,),
            in_specs=[
                pl.BlockSpec((height, columns), lambda i, o: (o[i], 0)),
                pl.BlockSpec((padded, width), lambda i, o: (o[i], 0)),
            ],
            out_specs=pl.BlockSpec((1, rows, columns), lambda i, o: (i, 0, 0)),
        ),
        out_shape=jax.ShapeDtypeStruct((count, rows, columns), BF),
        compiler_params=MEMORY,
        cost_estimate=FREE,
    )(order, gateup, down)


def sides_kernel(order_ref, *refs):
    enters, grad_ref = refs[:4], refs[4]
    downs = refs[5:-2]
    lines = 2 * enters[0].shape[1]
    shard = grad_ref.shape[1] // 2
    for side, out_ref in enumerate(refs[-2:]):
        team = out_ref.shape[0]
        lines = enters[0].shape[1] // team
        for half in range(2):
            value = outer_sum(
                enters[2 * half + side][...], grad_ref[:, half * shard : (half + 1) * shard]
            ).astype(BF)
            for seat in range(team):
                out_ref[seat, :lines, half * shard : (half + 1) * shard] = value[
                    seat * lines : (seat + 1) * lines
                ]
        if downs:
            value = through(downs[side][...], downs[2][...]).astype(BF)
            rank = value.shape[1]
            padded = value.shape[0] // team
            for seat in range(team):
                for row in range(0, padded, 16):
                    start = row // 16 * rank
                    first = seat * padded + row
                    out_ref[seat, lines : lines + 16, start : start + rank] = value[
                        first : first + 16
                    ]


def sides_pass(order, enter, grad, down, down_leave, team, together):
    width, columns = grad.shape
    half = enter.shape[1] // 4

    def near_or_far(rows, wide, at):
        return pl.BlockSpec((rows, wide), at)

    specs = [
        pl.BlockSpec((width, half), lambda i, o: (0, o[0])),
        pl.BlockSpec((width, half), lambda i, o: (0, o[1])),
        pl.BlockSpec((width, half), lambda i, o: (0, 2 + o[0])),
        pl.BlockSpec((width, half), lambda i, o: (0, 2 + o[1])),
        held(grad),
    ]
    arrays = [enter] * 4 + [grad]
    lines = half // team
    if together:
        lines += 16
        rows = down.shape[0] // 2
        specs += [
            pl.BlockSpec((rows, down.shape[1]), lambda i, o: (o[0], 0)),
            pl.BlockSpec((rows, down.shape[1]), lambda i, o: (o[1], 0)),
            held(down_leave),
        ]
        arrays += [down, down, down_leave]
    shape = (team, lines, columns)
    return pl.pallas_call(
        sides_kernel,
        grid_spec=pltpu.PrefetchScalarGridSpec(
            num_scalar_prefetch=1,
            grid=(1,),
            in_specs=specs,
            out_specs=[pl.BlockSpec(shape, lambda i, o: (0, 0, 0))] * 2,
        ),
        out_shape=[jax.ShapeDtypeStruct(shape, BF)] * 2,
        compiler_params=MEMORY,
        cost_estimate=FREE,
    )(order, *arrays)


def home_kernel(piece, near_ref, far_ref, mine_ref, other_ref, dealt_ref, down_ref):
    team, total, columns = dealt_ref.shape
    lines = mine_ref.shape[1]
    height = total - lines
    base = team * height
    for seat in range(team):
        rest = mine_ref[seat].astype(F32) + other_ref[seat].astype(F32)
        dealt_ref[seat, :lines, :] = rest.astype(BF)
        rows = slice(seat * height, (seat + 1) * height)
        value = near_ref[rows, :].astype(F32) + far_ref[rows, :].astype(F32)
        dealt_ref[seat, lines:total, :] = value.astype(BF)
    width = down_ref.shape[1]
    for r, c, row, lane in blocks_of(even(piece), width, columns)[0]:
        rows, lanes = slice(base + row, base + row + 16), slice(lane, lane + 128)
        value = near_ref[rows, lanes].astype(F32) + far_ref[rows, lanes].astype(F32)
        size = min(16, piece - r)
        down_ref[r : r + size, c : c + 128] = value[:size]


def home_pass(near, far, mine, other, piece, width, height):
    team, lines, columns = mine.shape
    return pl.pallas_call(
        lambda *refs: home_kernel(piece, *refs),
        out_shape=[
            jax.ShapeDtypeStruct((team, lines + height, columns), BF),
            jax.ShapeDtypeStruct((piece, width), F32),
        ],
        compiler_params=MEMORY,
        cost_estimate=FREE,
    )(near, far, mine, other)


def join_kernel(piece, padded, in_ref, *outs):
    team, total, columns = in_ref.shape
    units, shard = outs[0].shape[1] // 2, columns // 2
    lines = outs[0].shape[0]
    for out_ref, row in ((outs[0], 0), (outs[1], total - outs[1].shape[0])):
        height = out_ref.shape[0]
        for half in range(2):
            for block in range(shard // padded):
                first = half * shard + block * padded
                parts = [
                    in_ref[seat, row : row + height, first : first + piece] for seat in range(team)
                ]
                start = half * units + block * team * piece
                joined = jnp.concatenate(parts, axis=1).astype(F32)
                out_ref[:, start : start + team * piece] = joined
    if len(outs) == 3:
        rank = outs[2].shape[1]
        for seat in range(team):
            for row in range(0, padded, 16):
                size = min(16, piece - row)
                start = row // 16 * rank
                value = in_ref[seat, lines : lines + size, start : start + rank]
                first = seat * piece + row
                outs[2][first : first + size, :] = value.astype(F32)


def join_pass(parts, lines, height, piece, padded, rank):
    team, total, columns = parts.shape
    wide = columns // padded * piece * team
    shapes = [(lines, wide), (height, wide)]
    if total > lines + height:
        shapes.append((team * piece, rank))
    return pl.pallas_call(
        lambda *refs: join_kernel(piece, padded, *refs),
        out_shape=[jax.ShapeDtypeStruct(shape, F32) for shape in shapes],
        compiler_params=MEMORY,
        cost_estimate=FREE,
    )(parts)


def per_device(
    tokens,
    cotangent,
    exit_depth,
    lengths,
    loop_index,
    attn_gain,
    mlp_gain,
    qkv_weight,
    out_weight,
    gateup_weight,
    down_weight,
    qkv_enter,
    query_leave,
    kv_leave,
    out_enter,
    out_leave,
    gateup_enter,
    gateup_leave,
    down_enter,
    down_leave,
):
    loops = lax.axis_size("depth")
    rows = lax.axis_size("rows")
    group = lax.axis_index("depth")
    place = lax.axis_index("rows")
    slots, seq_dev, width = tokens.shape
    sub = rows // slots
    team = rows // 2
    count = slots * seq_dev
    teams = [[h * team + k for k in range(team)] for h in range(2)]
    seq_here, mate, core = place // sub, place % sub, place % 2
    side, seat = place // team, place % team
    levels = jnp.arange(loops, dtype=jnp.int32)

    head = kv_leave.shape[2] // 2
    width_q = query_leave.shape[2]
    rank = qkv_enter.shape[2] // 3
    hidden_units = gateup_weight.shape[1] // 2
    piece = down_weight.shape[0]
    padded = -(-piece // 16) * 16
    shard = 2 * loops * padded
    slab = width // (2 * loops)
    gain_size = attn_gain.shape[0]

    def turn(values):
        return jnp.stack(
            [values[0]] + [swap(values[f], "rows", f * sub) for f in range(1, slots)]
        )

    def deal(values):
        return lax.all_to_all(
            values, "rows", split_axis=0, concat_axis=0, axis_index_groups=teams, tiled=True
        )

    def pick(array, index):
        return array.at[index].get(mode="promise_in_bounds")

    def halve(array, bit):
        half = array.shape[0] // 2
        return array[:half], swap(array[half:], "rows", bit)

    def halve_but_last(array, bits):
        for bit in bits[:-1]:
            array = add_low(*halve(array, bit))
        return array

    def own_half(array, which):
        height = array.shape[0] // 2
        return lax.dynamic_slice(array, (which * height, 0), (height, array.shape[1]))

    def positions_of(who):
        blocks = (seq_here ^ levels) * sub + who
        return (blocks[:, None] * seq_dev + jnp.arange(seq_dev, dtype=jnp.int32)[None, :]).reshape(
            count
        )

    depth_flips = [0, 1, 2, 3]
    halves_order = jnp.stack([(group ^ f) * 2 + (core ^ e) for f in depth_flips for e in (0, 1)])
    flips = [(d, f) for d in range(4) for f in range(2)]
    slab_at = {(d, f): (group ^ d) * 2 + (side ^ f) for d, f in flips}
    team_bits, sub_bits, row_bits = bits_of(team), bits_of(sub), bits_of(rows)
    bands = [(0, width_q), (width_q, head), (width_q + head, head)]
    together = team == loops
    lines = gateup_leave.shape[1]
    with_enter = lines + 16 if together else lines

    table = loop_index.reshape(loops, loops)
    mine = lax.dynamic_index_in_dim(table, group, 0, keepdims=False)
    order = jnp.sum((mine[None, :] == levels[:, None]).astype(jnp.int32) * levels[None, :], axis=1)
    sizes_here = jnp.sum(jnp.where(table == group, lengths.reshape(loops, loops), 0), axis=1)
    size_here = lax.dynamic_slice(sizes_here, (seq_here,), (1,))
    positions = positions_of(mate)
    cosine, sine = angles(positions.astype(F32), head)
    gains = jnp.concatenate([attn_gain, mlp_gain])[None]
    gains = jnp.concatenate([gains] + [swap(gains, "depth", f) for f in depth_flips[1:]])
    gains = pick(gains, group ^ levels)
    small = [
        qkv_weight,
        qkv_enter[0],
        jnp.concatenate([query_leave[0], kv_leave[0]], axis=1),
        out_weight,
        out_enter[0],
        out_leave[0],
        gains,
    ]
    small_shapes = [array.shape for array in small]
    late = [gateup_enter[0], down_leave[0]]
    late_shapes = [array.shape for array in late]
    late_packed = pack_pass(late)
    packed = lax.all_gather(pack_pass(small), "rows", axis=0, tiled=True)
    arrived = lax.all_to_all(
        pick(tokens, order), "depth", split_axis=0, concat_axis=0, tiled=True
    )
    dealt = deal_pass(
        [gateup_weight, gateup_leave[0]] + [down_enter[0]] * together, team, piece, padded
    )
    upstream_low = turn(pick(cotangent, seq_here ^ levels)).reshape(count, width)
    arrived, dealt, upstream_low = tie(arrived, dealt, upstream_low)
    inputs = turn(pick(arrived, seq_here ^ levels)).reshape(count, width)
    dealt = deal(dealt)
    inputs, dealt, packed, upstream_low = tie(inputs, dealt, packed, upstream_low)

    slab_near, rest_near = slab_pass(dealt, down_weight, with_enter, padded)
    slab_far = swap(slab_near, "rows", team)
    (
        qkv_slab,
        full_qkv_enter,
        full_leave,
        out_slab,
        full_out_enter,
        full_out_leave,
        gain_slab,
    ) = unpack_pass([packed], small_shapes, BF)
    gain_slab = gain_slab.reshape(rows, loops, 2, -1)
    both_gains = gain_slab.transpose(2, 1, 0, 3).reshape(2, 1, width).astype(F32)
    gain_one, gain_two = both_gains[0], both_gains[1]
    spare = qkv_slab.shape[1] - width

    def both_halves(which):
        return jnp.concatenate(
            [own_half(qkv_slab, which), jnp.pad(own_half(out_slab, which), ((0, 0), (0, spare)))]
        )

    half_here = both_halves(core)
    fetched = [swap(half_here, "depth", f) for f in depth_flips[1:]]
    fetched, slab_near, slab_far, upstream_low, rest_near = tie(
        fetched, slab_near, slab_far, upstream_low, rest_near
    )
    others = swap(jnp.stack(fetched), "rows", 1)
    others, slab_near, rest_near, late_packed = tie(others, slab_near, rest_near, late_packed)
    late_packed = lax.all_gather(late_packed, "rows", axis=0, tiled=True)
    rest_far = swap(rest_near, "rows", team)
    slabs = {(0, 0): slab_near, (0, 1): slab_far}
    slabs[(1, 0)] = swap(slab_near, "depth", 1)
    slabs[(2, 0)] = swap(slab_near, "depth", 2)
    slabs[(1, 1)] = swap(slab_far, "depth", 1)
    slabs[(2, 1)] = swap(slab_far, "depth", 2)
    halves = [half_here, both_halves(core ^ 1)]
    for f in range(3):
        halves += [fetched[f], others[f]]
    qkv_eff, out_eff = fold_attn_pass(
        halves_order, halves, full_qkv_enter, full_leave, full_out_enter, full_out_leave, bands
    )
    normed_one, queries, pairs_all = enter_pass(
        inputs, gain_one, qkv_eff, cosine, sine, width_q
    )
    pairs_all, rest_far, slabs, upstream_low = tie(pairs_all, rest_far, slabs, upstream_low)
    cotan_far = swap(upstream_low, "rows", team_bits[-1])
    slabs[(3, 0)] = swap(slabs[(1, 0)], "depth", 2)
    slabs[(3, 1)] = swap(slabs[(2, 1)], "depth", 1)
    mates = [0]
    for bit in sub_bits:
        pairs_all = jnp.concatenate([pairs_all, swap(pairs_all, "rows", bit)])
        mates = mates + [f | bit for f in mates]
    key_pos = jnp.concatenate([positions_of(mate ^ f) for f in mates])[None]
    attended, log_total = attend_pass(
        size_here, queries, pairs_all, positions[:, None], key_pos, seq_dev
    )
    mixed, normed_two = leave_pass(inputs, attended, out_eff, gain_two)
    normed_two, slabs, cotan_far = tie(normed_two, slabs, cotan_far)

    def gather_team(value, far):
        value = jnp.concatenate([value, far])
        for bit in team_bits[-2::-1]:
            value = jnp.concatenate([value, swap(value, "rows", bit)])
        return value

    normed_far = swap(normed_two, "rows", team_bits[-1])
    full_gateup_enter, full_down_leave = unpack_pass([late_packed], late_shapes, BF)
    leave_full, *enter_full = assemble_pass(
        side[None], rest_near, rest_far, lines, shard, rank
    )
    if together:
        enter_full = enter_full[0]
    else:
        enter_every = lax.all_gather(down_enter[0], "rows", axis=0, tiled=True)
        enter_every = enter_every.reshape(loops, 2, team, piece, rank)
        enter_full = lax.dynamic_index_in_dim(enter_every, seat, 2, keepdims=False)
        enter_full = jnp.pad(enter_full, ((0, 0), (0, 0), (0, padded - piece), (0, 0)))
        enter_full = enter_full.reshape(shard, rank)
    gateup_eff, down_eff = fold_ff_pass(
        jnp.stack([slab_at[f] for f in flips]),
        [slabs[f] for f in flips],
        full_gateup_enter,
        leave_full,
        enter_full,
        full_down_leave,
        padded,
    )
    normed_far, gateup_eff, down_eff = tie(normed_far, gateup_eff, down_eff)
    cotan_team = gather_team(upstream_low, cotan_far)
    normed_team = gather_team(normed_two, normed_far)

    hidden, grad_expanded, grad_normed = ff_pass(
        normed_team, cotan_team, gateup_eff, down_eff, 256
    )

    grad_normed = halve_but_last(grad_normed, team_bits)
    grad_normed, hidden, grad_expanded = tie(grad_normed, hidden, grad_expanded)
    grad_terms = halve(grad_normed, team_bits[-1])
    grad_gateup = outer_sum(normed_team, grad_expanded).astype(BF)
    grad_down = outer_sum(hidden, cotan_team).astype(BF)
    grad_terms, grad_gateup, grad_down, hidden = tie(grad_terms, grad_gateup, grad_down, hidden)

    def slabs_out(*which):
        index = jnp.stack([slab_at[f] for f in which])
        return slabs_out_pass(index, grad_gateup, grad_down, 2 * loops)

    near_sent, far_sent = slabs_out((2, 0), (3, 0)), slabs_out((1, 1), (3, 1))
    near_sent, far_sent, grad_gateup, grad_down = tie(
        near_sent, far_sent, grad_gateup, grad_down
    )
    near_got = swap(near_sent, "depth", 2)
    far_got = swap(far_sent, "depth", 1)
    sides = jnp.stack([side, side ^ 1])
    side_near, side_far = sides_pass(
        sides, full_gateup_enter, grad_gateup, grad_down, full_down_leave, team, together
    )
    side_near, side_far, grad_terms, hidden = tie(side_near, side_far, grad_terms, hidden)
    side_got = swap(side_far, "rows", team)
    grad_mixed, grad_branch, grad_attended, grad_gain_second = leave_back_pass(
        *grad_terms, mixed, gain_two, upstream_low, out_eff
    )
    grad_queries, key_terms = attend_back_pass(
        size_here,
        queries,
        pairs_all,
        grad_attended,
        log_total,
        positions[:, None],
        key_pos,
        cosine,
        sine,
        seq_dev,
    )
    mate_order = halving_order(sub_bits)
    if mate_order != mates:
        key_terms = jnp.concatenate(
            [key_terms[i * count : (i + 1) * count] for i in map(mates.index, mate_order)]
        )
    outcome = matmul(hidden, down_eff).astype(BF)
    near_kept, far_kept = slabs_out((0, 0), (1, 0)), slabs_out((0, 1), (2, 1))
    key_terms, grad_queries, near_got, far_got, outcome, near_kept, far_kept, side_got = tie(
        key_terms, grad_queries, near_got, far_got, outcome, near_kept, far_kept, side_got
    )
    pair_terms = halve(halve_but_last(key_terms, sub_bits), sub_bits[-1])
    outcome = halve_but_last(outcome, team_bits)
    pair_terms, outcome = tie(pair_terms, outcome)

    grad_joined, grad_inputs, grad_gain_first = enter_back_pass(
        grad_queries, pair_terms, cosine, sine, qkv_eff, inputs, gain_one, grad_mixed
    )
    near_one, far_one = add_low(near_kept[1], near_got[1]), add_low(far_kept[1], far_got[1])
    near_one, far_one = swap(near_one, "depth", 1), swap(far_one, "depth", 2)
    outcome = halve(outcome, team_bits[-1])
    grad_qkv = outer_sum(normed_one, grad_joined).astype(BF)
    grad_out = outer_sum(attended, grad_branch).astype(BF)

    near_one, far_one, outcome, grad_inputs, grad_qkv, grad_out = tie(
        near_one, far_one, outcome, grad_inputs, grad_qkv, grad_out
    )

    def loop_part(flip):
        parts = []
        for array in (grad_qkv, grad_out):
            height = array.shape[0] // loops
            part = lax.dynamic_slice(array, ((group ^ flip) * height, 0), (height, array.shape[1]))
            parts.append(jnp.pad(part, ((0, 0), (0, grad_qkv.shape[1] - array.shape[1]))))
        return jnp.concatenate(parts)

    terms = [loop_part(0)] + [swap(loop_part(f), "depth", f) for f in depth_flips[1:]]
    near_sum = add_low(near_kept[0], near_got[0])
    far_sum = add_low(far_kept[0], far_got[0])
    result = mixed + (outcome[0].astype(F32) + outcome[1].astype(F32))
    result_low = result.astype(BF)
    near_sum, far_sum = add_low(near_sum, near_one), add_low(far_sum, far_one)
    far_sum = swap(far_sum, "rows", team)
    result_low, grad_qkv, grad_out, near_sum, far_sum, terms = tie(
        result_low, grad_qkv, grad_out, near_sum, far_sum, terms
    )

    dealt, grad_down_weight = home_pass(
        near_sum, far_sum, side_near, side_got, piece, width, slab // team
    )
    homeward = jnp.concatenate(
        [result_low.reshape(slots, seq_dev, width), grad_inputs.reshape(slots, seq_dev, width)],
        axis=1,
    )

    homeward, dealt = tie(homeward, dealt)
    homeward = turn(homeward)
    dealt = deal(dealt)
    row_place = jnp.arange(rows, dtype=jnp.int32)

    def to_owner(packed):
        return lax.psum_scatter(packed, "rows", scatter_dimension=0, tiled=True)

    qkv_rows = grad_qkv.shape[0] // loops
    rest_grads_of = [
        ((terms[0].shape[0] - qkv_rows) // rows, width),
        (grad_out.shape[0] // rows, rank),
        (rank // rows, width),
        (width // rows, rank),
        (width // rows, rank),
        (rank // rows, width),
    ]
    rest_sum = grads_pass(
        lambda *refs: rest_grads_kernel(qkv_rows, *refs),
        row_place,
        rows,
        rest_grads_of,
        [
            *terms,
            grad_out,
            full_out_enter,
            full_out_leave,
            grad_gateup,
            leave_full,
            grad_down,
            enter_full,
        ],
    )
    rest_sum = to_owner(rest_sum)
    attn_grads_of = attn_grads_shapes(rows, qkv_rows, grad_qkv, full_qkv_enter, full_leave, bands)
    attn_sum = grads_pass(
        lambda *refs: attn_grads_kernel(qkv_rows, bands, *refs),
        row_place,
        rows,
        attn_grads_of,
        [*terms, grad_qkv, full_qkv_enter, full_leave],
    )
    attn_sum = to_owner(attn_sum)
    homeward, dealt = tie(homeward, dealt)
    returned = lax.all_to_all(
        pick(homeward[:, seq_dev:], seq_here ^ levels),
        "depth",
        split_axis=0,
        concat_axis=0,
        tiled=True,
    )

    grad_tokens = pick(returned, mine)
    activations = pick(homeward[:, :seq_dev], seq_here ^ levels)
    own_out, *rest_parts = unpack_pass([rest_sum], rest_grads_of, F32)
    own_qkv, *attn_parts = unpack_pass([attn_sum], attn_grads_of, F32)
    attn_grads = [
        jnp.concatenate(attn_parts[:3], axis=1),
        attn_parts[3],
        jnp.concatenate(attn_parts[4:], axis=1),
    ]
    rest_grads = rest_parts[:2] + [jnp.concatenate(rest_parts[2:4], axis=1), rest_parts[4]]
    grad_gateup_leave, grad_gateup_weight, *grad_down_enter = join_pass(
        dealt, lines, slab // team, piece, padded, rank
    )
    if together:
        grad_down_enter = grad_down_enter[0]
    else:
        grad_down_in = through(grad_down, full_down_leave).astype(BF)
        grad_down_in = grad_down_in.reshape(loops, 2, 1, padded, rank)[:, :, :, :piece]
        spaced = jnp.zeros((loops, 2, team, piece, rank), BF)
        spaced = lax.dynamic_update_slice(spaced, grad_down_in, (0, 0, seat, 0, 0))
        grad_down_enter = lax.psum_scatter(
            spaced.reshape(hidden_units, rank), "rows", scatter_dimension=0, tiled=True
        ).astype(F32)

    block_pos = place * seq_dev + jnp.arange(seq_dev, dtype=jnp.int32)
    valid = block_pos[None, :] < sizes_here[:, None]
    counts_here = jnp.sum(
        ((exit_depth[None] == levels[:, None, None]) & valid[None]).astype(F32), axis=(1, 2)
    )
    given = inputs.astype(F32)
    cross = jnp.sum(given * result, axis=-1)
    own_sq = jnp.sum(given * given, axis=-1)
    out_sq = jnp.sum(result * result, axis=-1)
    cosines = cross * lax.rsqrt(own_sq * out_sq + 1e-06)
    cosine_here = jnp.sum(jnp.where(positions < size_here, cosines, 0.0))
    tallies = jnp.concatenate([counts_here, cosine_here[None]])
    gain_grads = jnp.concatenate([grad_gain_first, grad_gain_second])
    gain_grads = gain_grads.reshape(2, loops * rows, gain_size).transpose(1, 0, 2)
    small = jnp.concatenate(
        [
            jnp.broadcast_to(tallies[None], (loops * rows, loops + 1)),
            gain_grads.reshape(loops * rows, 2 * gain_size),
        ],
        axis=1,
    )
    small = jnp.pad(small, ((0, 0), (0, 127 - loops - 2 * gain_size)))
    small = lax.all_to_all(small, ("depth", "rows"), split_axis=0, concat_axis=0, tiled=True)
    small = jnp.sum(small, axis=0)
    tallies = small[: loops + 1]
    gain_grads = small[loops + 1 : loops + 1 + 2 * gain_size].reshape(2, gain_size)
    exit_counts = tallies[:loops].astype(jnp.int32)
    confidence = tallies[loops] / jnp.sum(lengths).astype(F32)

    return (
        activations,
        grad_tokens,
        exit_counts,
        confidence,
        gain_grads[0],
        gain_grads[1],
        own_qkv,
        own_out,
        grad_gateup_weight,
        grad_down_weight,
        attn_grads[0][None],
        attn_grads[1][None],
        attn_grads[2][None],
        rest_grads[0][None],
        rest_grads[1][None],
        rest_grads[2][None],
        grad_gateup_leave[None],
        grad_down_enter[None],
        rest_grads[3][None],
    )


def solution(mesh):
    split = P("depth", "rows", None)
    flat = P(("depth", "rows"))
    tall = P(("depth", "rows"), None)
    return jax.shard_map(
        per_device,
        mesh=mesh,
        in_specs=(split, split, P("depth", "rows"), P(), P(), flat, flat)
        + (tall,) * 4
        + (split,) * 9,
        out_specs=(split, split, P(), P(), flat, flat) + (tall,) * 4 + (split,) * 9,
        check_vma=False,
    )
```

```python
import math

import jax
import jax.numpy as jnp
from jax import lax
from jax.experimental import pallas as pl
from jax.experimental.pallas import tpu as pltpu
from jax.sharding import PartitionSpec as P

BF = jnp.bfloat16
F32 = jnp.float32
ROOT = math.sqrt(2.0 / math.pi)
CUBE = 0.044715


def angles(positions, size):
    freqs = jnp.exp(jnp.arange(size // 2, dtype=F32) * (-2.0 * math.log(10000.0) / size))
    phase = positions[:, None] * freqs[None, :]
    return (jnp.cos(phase), jnp.sin(phase))


def matmul(left, right):
    return jnp.dot(left, right, preferred_element_type=F32)


def outer_sum(left, right):
    return lax.dot_general(left, right, (((0,), (0,)), ((), ())), preferred_element_type=F32)


def through(left, right):
    return lax.dot_general(left, right, (((1,), (1,)), ((), ())), preferred_element_type=F32)


def swap(value, axis, flip):
    size = lax.axis_size(axis)
    return lax.ppermute(value, axis, [(i, i ^ flip) for i in range(size)])


def add_low(left, right):
    return (left.astype(F32) + right.astype(F32)).astype(BF)


def tie(*values):
    return lax.optimization_barrier(values)


def bits_of(size):
    return [1 << i for i in range(size.bit_length() - 1)]


LANES = 256


def even(height):
    return -(-height // 16) * 16


def segments(shapes):
    out, row = [], 0
    for which, (height, columns) in enumerate(shapes):
        for start in range(0, columns, LANES):
            out.append((which, row, start, min(LANES, columns - start)))
            row += even(height)
    return out, row


def put(out_ref, lead, row, height, value):
    short, narrow = even(height) - height, LANES - value.shape[1]
    if narrow:
        value = jnp.concatenate([value, jnp.zeros((height, narrow), value.dtype)], axis=1)
    if short:
        value = jnp.concatenate([value, jnp.zeros((short, LANES), value.dtype)], axis=0)
    out_ref[lead, row : row + even(height), :] = value


def pack_kernel(shapes, *refs):
    where, _ = segments(shapes)
    for which, row, start, size in where:
        put(refs[-1], 0, row, shapes[which][0], refs[which][:, start : start + size])


def pack_pass(arrays):
    shapes = [array.shape for array in arrays]
    return pl.pallas_call(
        lambda *refs: pack_kernel(shapes, *refs),
        out_shape=jax.ShapeDtypeStruct((1, segments(shapes)[1], LANES), BF),
        compiler_params=MEMORY,
        cost_estimate=FREE,
    )(*arrays)


def unpack_kernel(shapes, into, in_ref, *outs):
    for which, row, start, size in segments(shapes)[0]:
        height = shapes[which][0]
        out, column = into[which]
        column += start
        for lead in range(in_ref.shape[0]):
            value = in_ref[lead, row : row + height, :size]
            first = lead * height
            outs[out][first : first + height, column : column + size] = value.astype(
                outs[out].dtype
            )


def unpack_pass(packed, shapes, dtype, groups=None):
    lead = packed.shape[0]
    groups = groups or [[which] for which in range(len(shapes))]
    into, out_shapes = {}, []
    for out, group in enumerate(groups):
        column = 0
        for which in group:
            into[which] = (out, column)
            column += shapes[which][1]
        shape = (lead * shapes[group[0]][0], column)
        out_shapes.append(jax.ShapeDtypeStruct(shape, dtype))
    return pl.pallas_call(
        lambda *refs: unpack_kernel(shapes, into, *refs),
        out_shape=out_shapes,
        compiler_params=MEMORY,
        cost_estimate=FREE,
    )(packed)


def spread_rows(pos_ref, out_ref, row, value, first, size):
    leads = out_ref.shape[0]
    height = value.shape[0] // leads
    for lead in range(leads):
        block = value[lead * height : (lead + 1) * height, first : first + size]
        put(out_ref, pos_ref[lead], row, height, block.astype(BF))


def total_of(refs, rows, columns):
    total = refs[0][rows, :columns].astype(F32)
    for ref in refs[1:]:
        total = total + ref[rows, :columns].astype(F32)
    return total


def place_all(pos_ref, out_ref, values):
    shapes = [(value.shape[0] // out_ref.shape[0], value.shape[1]) for value in values]
    for which, row, start, size in segments(shapes)[0]:
        spread_rows(pos_ref, out_ref, row, values[which], start, size)


def attn_grads_kernel(height, bands, pos_ref, *refs):
    grad_ref, enter_ref, leave_ref, out_ref = refs[-4:]
    rank = leave_ref.shape[0]
    values = [total_of(refs[:-4], slice(0, height), grad_ref.shape[1])]
    for start, size in bands:
        values.append(through(grad_ref[:, start : start + size], leave_ref[:, start : start + size]))
    for index, (start, size) in enumerate(bands):
        enter = enter_ref[:, index * rank : (index + 1) * rank]
        values.append(outer_sum(enter, grad_ref[:, start : start + size]))
    place_all(pos_ref, out_ref, values)


def attn_grads_shapes(rows, height, grad, enter, leave, bands):
    rank = leave.shape[0]
    return (
        [(height // rows, grad.shape[1])]
        + [(grad.shape[0] // rows, rank)] * len(bands)
        + [(rank // rows, size) for _, size in bands]
    )


def rest_grads_kernel(first, pos_ref, *refs):
    (
        grad_out_ref,
        out_enter_ref,
        out_leave_ref,
        grad_gateup_ref,
        leave_ref,
        grad_down_ref,
        down_enter_ref,
        out_ref,
    ) = refs[-8:]
    shard = leave_ref.shape[1] // 2
    values = [
        total_of(refs[:-8], slice(first, refs[0].shape[0]), grad_out_ref.shape[1]),
        through(grad_out_ref[...], out_leave_ref[...]),
        outer_sum(out_enter_ref[...], grad_out_ref[...]),
        through(grad_gateup_ref[:, :shard], leave_ref[:, :shard]),
        through(grad_gateup_ref[:, shard:], leave_ref[:, shard:]),
        outer_sum(down_enter_ref[...], grad_down_ref[...]),
    ]
    place_all(pos_ref, out_ref, values)


def grads_pass(kernel, pos, rows, shapes, arrays):
    whole = [pl.BlockSpec(memory_space=pltpu.VMEM)] * len(arrays)
    shape = (rows, segments(shapes)[1], LANES)
    return pl.pallas_call(
        kernel,
        in_specs=[pl.BlockSpec(memory_space=pltpu.SMEM)] + whole,
        out_specs=pl.BlockSpec(memory_space=pltpu.VMEM),
        out_shape=jax.ShapeDtypeStruct(shape, BF),
        compiler_params=MEMORY,
        cost_estimate=FREE,
    )(pos, *arrays)


FREE = pl.CostEstimate(flops=0, transcendentals=0, bytes_accessed=0)
MEMORY = pltpu.CompilerParams(vmem_limit_bytes=60 << 20)


def held(array):
    return pl.BlockSpec(
        array.shape, lambda *_: (0,) * len(array.shape), pipeline_mode=pl.Buffered(1)
    )


def strip(tile, columns):
    return pl.BlockSpec((tile, columns), lambda i: (i, 0))


def mean_scale(values):
    return lax.rsqrt(jnp.mean(values * values, axis=-1, keepdims=True) + 1e-06)


def turned(values, cosine, sine):
    half = values.shape[-1] // 2
    first, second = values[:, :half], values[:, half:]
    return jnp.concatenate(
        [first * cosine - second * sine, second * cosine + first * sine], axis=-1
    )


def enter_kernel(x_ref, gain_ref, weight_ref, cos_ref, sin_ref, n_ref, q_ref, kv_ref):
    head = kv_ref.shape[1] // 2
    width_q = q_ref.shape[1]
    values = x_ref[...].astype(F32)
    normed = (values * mean_scale(values) * gain_ref[...]).astype(BF)
    n_ref[...] = normed
    joined = matmul(normed, weight_ref[...])
    cosine, sine = cos_ref[...], sin_ref[...]
    scale = head ** (-0.5)
    for start in range(0, width_q, head):
        spun = turned(joined[:, start : start + head], cosine, sine)
        q_ref[:, start : start + head] = (spun * scale).astype(BF)
    kv_ref[:, :head] = turned(joined[:, width_q : width_q + head], cosine, sine).astype(BF)
    kv_ref[:, head:] = joined[:, width_q + head :].astype(BF)


def enter_pass(x, gain, weight, cosine, sine, width_q):
    count, width = x.shape
    tile = count // 2
    rest = weight.shape[1] - width_q
    return pl.pallas_call(
        enter_kernel,
        grid=(count // tile,),
        in_specs=[
            strip(tile, width),
            held(gain),
            held(weight),
            strip(tile, cosine.shape[1]),
            strip(tile, cosine.shape[1]),
        ],
        out_specs=[strip(tile, width), strip(tile, width_q), strip(tile, rest)],
        out_shape=[
            jax.ShapeDtypeStruct((count, width), BF),
            jax.ShapeDtypeStruct((count, width_q), BF),
            jax.ShapeDtypeStruct((count, rest), BF),
        ],
        compiler_params=MEMORY,
        cost_estimate=FREE,
    )(x, gain, weight, cosine, sine)


def stack_heads(ref, head):
    return jnp.concatenate(
        [ref[:, start : start + head] for start in range(0, ref.shape[1], head)], axis=0
    )


def allowed_keys(size_ref, pos_ref, key_ref, heads):
    fits = (key_ref[...] <= pos_ref[...]) & (key_ref[...] < size_ref[0])
    return jnp.concatenate([jnp.where(fits, 0.0, -1e30)] * heads, axis=0)


def attend_kernel(size_ref, q_ref, kv_ref, pos_ref, key_ref, o_ref, lse_ref):
    head = kv_ref.shape[1] // 2
    tile = q_ref.shape[0]
    heads = q_ref.shape[1] // head
    scores = through(stack_heads(q_ref, head), kv_ref[:, :head])
    scores = scores + allowed_keys(size_ref, pos_ref, key_ref, heads)
    highest = jnp.max(scores, axis=-1, keepdims=True)
    raised = jnp.exp(scores - highest)
    total = jnp.sum(raised, axis=-1, keepdims=True)
    probs = (raised * (1.0 / total)).astype(BF)
    lse_ref[...] = (highest + jnp.log(total)).reshape(1, heads * tile, 1)
    mixed = matmul(probs, kv_ref[:, head:]).astype(BF)
    for index in range(heads):
        o_ref[:, index * head : (index + 1) * head] = mixed[index * tile : (index + 1) * tile]


def attend_pass(size, q, kv, positions, key_positions, tile):
    count, width_q = q.shape
    heads = 2 * width_q // kv.shape[1]
    steps = count // tile

    def rows(columns):
        return pl.BlockSpec((tile, columns), lambda i, s: (i, 0))

    return pl.pallas_call(
        attend_kernel,
        grid_spec=pltpu.PrefetchScalarGridSpec(
            num_scalar_prefetch=1,
            grid=(steps,),
            in_specs=[rows(width_q), held(kv), rows(1), held(key_positions)],
            out_specs=[rows(width_q), pl.BlockSpec((1, heads * tile, 1), lambda i, s: (i, 0, 0))],
        ),
        out_shape=[
            jax.ShapeDtypeStruct((count, width_q), BF),
            jax.ShapeDtypeStruct((steps, heads * tile, 1), F32),
        ],
        compiler_params=MEMORY,
        cost_estimate=FREE,
    )(size, q, kv, positions, key_positions)


def attend_back_kernel(
    size_ref, q_ref, kv_ref, do_ref, lse_ref, pos_ref, key_ref, cos_ref, sin_ref, dq_ref, dkv_ref, acc
):
    head = kv_ref.shape[1] // 2
    tile = q_ref.shape[0]
    heads = q_ref.shape[1] // head
    step = pl.program_id(0)
    queries = stack_heads(q_ref, head)
    grads = stack_heads(do_ref, head)
    keys = kv_ref[:, :head]
    scores = through(queries, keys) + allowed_keys(size_ref, pos_ref, key_ref, heads)
    probs = jnp.exp(scores - lse_ref[0])
    grad_probs = through(grads, kv_ref[:, head:])
    centre = jnp.sum(probs * grad_probs, axis=-1, keepdims=True)
    grad_scores = (probs * (grad_probs - centre)).astype(BF)
    grad_q = matmul(grad_scores, keys) * (head ** (-0.5))
    cosine, sine = cos_ref[...], -sin_ref[...]
    for index in range(heads):
        spun = turned(grad_q[index * tile : (index + 1) * tile], cosine, sine)
        dq_ref[:, index * head : (index + 1) * head] = spun.astype(BF)
    grad_k = outer_sum(grad_scores, queries)
    grad_v = outer_sum(probs.astype(BF), grads)

    @pl.when(step == 0)
    def _():
        acc[:, :head] = grad_k
        acc[:, head:] = grad_v

    @pl.when(step > 0)
    def _():
        acc[:, :head] += grad_k
        acc[:, head:] += grad_v

    @pl.when(step == pl.num_programs(0) - 1)
    def _():
        dkv_ref[...] = acc[...].astype(BF)


def attend_back_pass(size, q, kv, do, lse, positions, key_positions, cosine, sine, tile):
    count, width_q = q.shape
    heads = 2 * width_q // kv.shape[1]

    def rows(columns):
        return pl.BlockSpec((tile, columns), lambda i, s: (i, 0))

    return pl.pallas_call(
        attend_back_kernel,
        grid_spec=pltpu.PrefetchScalarGridSpec(
            num_scalar_prefetch=1,
            grid=(count // tile,),
            in_specs=[
                rows(width_q),
                held(kv),
                rows(width_q),
                pl.BlockSpec((1, heads * tile, 1), lambda i, s: (i, 0, 0)),
                rows(1),
                held(key_positions),
                rows(cosine.shape[1]),
                rows(cosine.shape[1]),
            ],
            out_specs=[rows(width_q), pl.BlockSpec(kv.shape, lambda i, s: (0, 0))],
            scratch_shapes=[pltpu.VMEM(kv.shape, F32)],
        ),
        out_shape=[jax.ShapeDtypeStruct((count, width_q), BF), jax.ShapeDtypeStruct(kv.shape, BF)],
        compiler_params=MEMORY,
        cost_estimate=FREE,
    )(size, q, kv, do, lse, positions, key_positions, cosine, sine)


def leave_kernel(x_ref, o_ref, weight_ref, gain_ref, h_ref, n_ref):
    mixed = x_ref[...].astype(F32) + matmul(o_ref[...], weight_ref[...])
    h_ref[...] = mixed
    n_ref[...] = (mixed * mean_scale(mixed) * gain_ref[...]).astype(BF)


def leave_pass(x, o, weight, gain):
    count, width = x.shape
    tile = count // 2
    return pl.pallas_call(
        leave_kernel,
        grid=(count // tile,),
        in_specs=[strip(tile, width), strip(tile, o.shape[1]), held(weight), held(gain)],
        out_specs=[strip(tile, width)] * 2,
        out_shape=[jax.ShapeDtypeStruct((count, width), d) for d in (F32, BF)],
        compiler_params=MEMORY,
        cost_estimate=FREE,
    )(x, o, weight, gain)


def norm_grad(grad, values, gain):
    scaling = mean_scale(values)
    unit = values * scaling
    lifted = grad * gain
    back = scaling * (lifted - unit * jnp.mean(lifted * unit, axis=-1, keepdims=True))
    return back, jnp.sum(grad * unit, axis=0, keepdims=True)


def add_step(ref, value):
    @pl.when(pl.program_id(0) == 0)
    def _():
        ref[...] = value

    @pl.when(pl.program_id(0) > 0)
    def _():
        ref[...] += value


def leave_back_kernel(
    one_ref, two_ref, h_ref, gain_ref, dy_ref, weight_ref, dh_ref, dz_ref, do_ref, dgain_ref
):
    grad = one_ref[...].astype(F32) + two_ref[...].astype(F32)
    back, gain_sum = norm_grad(grad, h_ref[...], gain_ref[...])
    total = dy_ref[...].astype(F32) + back
    dh_ref[...] = total
    low = total.astype(BF)
    dz_ref[...] = low
    do_ref[...] = through(low, weight_ref[...]).astype(BF)
    add_step(dgain_ref, gain_sum)


def leave_back_pass(one, two, h, gain, dy, weight):
    count, width = h.shape
    tile = count // 2
    width_q = weight.shape[0]
    return pl.pallas_call(
        leave_back_kernel,
        grid=(count // tile,),
        in_specs=[strip(tile, width)] * 3 + [held(gain), strip(tile, width), held(weight)],
        out_specs=[strip(tile, width)] * 2
        + [strip(tile, width_q), pl.BlockSpec((1, width), lambda i: (0, 0))],
        out_shape=[
            jax.ShapeDtypeStruct((count, width), F32),
            jax.ShapeDtypeStruct((count, width), BF),
            jax.ShapeDtypeStruct((count, width_q), BF),
            jax.ShapeDtypeStruct((1, width), F32),
        ],
        compiler_params=MEMORY,
        cost_estimate=FREE,
    )(one, two, h, gain, dy, weight)


def enter_back_kernel(dq_ref, *refs):
    parts = refs[:-9]
    cos_ref, sin_ref, weight_ref, x_ref, gain_ref, dh_ref, joined_ref, dx_ref, dgain_ref = refs[-9:]
    head = parts[0].shape[1] // 2
    width_q = dq_ref.shape[1]
    pair = parts[0][...].astype(F32)
    for part in parts[1:]:
        pair = pair + part[...].astype(F32)
    joined_ref[:, :width_q] = dq_ref[...]
    spun = turned(pair[:, :head], cos_ref[...], -sin_ref[...])
    joined_ref[:, width_q : width_q + head] = spun.astype(BF)
    joined_ref[:, width_q + head :] = pair[:, head:].astype(BF)
    grad = through(joined_ref[...], weight_ref[...])
    back, gain_sum = norm_grad(grad, x_ref[...].astype(F32), gain_ref[...])
    dx_ref[...] = (dh_ref[...] + back).astype(BF)
    add_step(dgain_ref, gain_sum)


def enter_back_pass(dq, parts, cosine, sine, weight, x, gain, dh):
    count, width = x.shape
    tile = count // 2
    width_q = dq.shape[1]
    return pl.pallas_call(
        enter_back_kernel,
        grid=(count // tile,),
        in_specs=[strip(tile, width_q)]
        + [strip(tile, part.shape[1]) for part in parts]
        + [strip(tile, cosine.shape[1])] * 2
        + [held(weight), strip(tile, width), held(gain), strip(tile, width)],
        out_specs=[
            strip(tile, weight.shape[1]),
            strip(tile, width),
            pl.BlockSpec((1, width), lambda i: (0, 0)),
        ],
        out_shape=[
            jax.ShapeDtypeStruct((count, weight.shape[1]), BF),
            jax.ShapeDtypeStruct((count, width), BF),
            jax.ShapeDtypeStruct((1, width), F32),
        ],
        compiler_params=MEMORY,
        cost_estimate=FREE,
    )(dq, *parts, cosine, sine, weight, x, gain, dh)


def halving_order(bits):
    order = [0]
    for bit in reversed(bits):
        order = order + [flip | bit for flip in order]
    return order


def ff_kernel(n2_ref, df_ref, wg_ref, wd_ref, a_ref, dg_ref, dn_ref):
    hidden = wd_ref.shape[0]
    n2 = n2_ref[...]
    gate = matmul(n2, wg_ref[:, :hidden])
    upper = matmul(n2, wg_ref[:, hidden:])
    grad = through(df_ref[...], wd_ref[...])
    square = gate * gate
    bent = jnp.tanh(gate * (ROOT + ROOT * CUBE * square))
    half = 0.5 + 0.5 * bent
    act = gate * half
    a_ref[...] = (act * upper).astype(BF)
    slope = half + 0.5 * gate * (1.0 - bent * bent) * (ROOT + 3.0 * ROOT * CUBE * square)
    dg_ref[:, :hidden] = (grad * upper * slope).astype(BF)
    dg_ref[:, hidden:] = (grad * act).astype(BF)
    dn_ref[...] = through(dg_ref[...], wg_ref[...]).astype(BF)


def ff_pass(n2, df, wg, wd, tile):
    count, width = n2.shape
    hidden = wd.shape[0]

    return pl.pallas_call(
        ff_kernel,
        grid=(count // tile,),
        in_specs=[strip(tile, width), strip(tile, width), held(wg), held(wd)],
        out_specs=[strip(tile, hidden), strip(tile, 2 * hidden), strip(tile, width)],
        out_shape=[
            jax.ShapeDtypeStruct((count, hidden), BF),
            jax.ShapeDtypeStruct((count, 2 * hidden), BF),
            jax.ShapeDtypeStruct((count, width), BF),
        ],
        compiler_params=MEMORY,
        cost_estimate=FREE,
    )(n2, df, wg, wd)


def blocks_of(padded, width, columns):
    across = columns // 128
    wide = width // 128
    out = []
    for r in range(padded // 16):
        for c in range(wide):
            out.append((16 * r, 128 * c, 16 * ((r * wide + c) // across), 128 * ((r * wide + c) % across)))
    return out, 16 * (-(-len(out) // across))


def tall(value, height):
    short = height - value.shape[0]
    if not short:
        return value
    return jnp.concatenate([value, jnp.zeros((short, value.shape[1]), value.dtype)], axis=0)


def deal_kernel(piece, padded, *refs):
    gateup_ref, leave_ref, out_ref = refs[0], refs[1], refs[-1]
    team, total, columns = out_ref.shape
    units, shard = gateup_ref.shape[1] // 2, columns // 2
    lines = leave_ref.shape[0]
    for in_ref, row in ((leave_ref, 0), (gateup_ref, total - gateup_ref.shape[0])):
        height = in_ref.shape[0]
        gap = jnp.zeros((height, padded - piece), in_ref.dtype)
        for half in range(2):
            for seat in range(team):
                parts = []
                for block in range(shard // padded):
                    start = half * units + (block * team + seat) * piece
                    parts += [in_ref[:, start : start + piece], gap]
                joined = jnp.concatenate(parts, axis=1)
                out_ref[seat, row : row + height, half * shard : (half + 1) * shard] = joined
    if len(refs) == 4:
        rank = refs[2].shape[1]
        for seat in range(team):
            for row in range(0, padded, 16):
                first = seat * piece + row
                value = tall(refs[2][first : first + min(16, piece - row), :], 16)
                start = row // 16 * rank
                out_ref[seat, lines : lines + 16, start : start + rank] = value


def deal_pass(arrays, team, piece, padded):
    lines = sum(array.shape[0] for array in arrays[:2]) + 16 * (len(arrays) == 3)
    columns = arrays[0].shape[1] // (team * piece) * padded
    return pl.pallas_call(
        lambda *refs: deal_kernel(piece, padded, *refs),
        out_shape=jax.ShapeDtypeStruct((team, lines, columns), BF),
        compiler_params=MEMORY,
        cost_estimate=FREE,
    )(*arrays)


def slab_kernel(padded, dealt_ref, down_ref, slab_ref, rest_ref):
    team, total, columns = dealt_ref.shape
    lines = rest_ref.shape[1]
    height = total - lines
    piece, width = down_ref.shape
    base = team * height
    for seat in range(team):
        slab_ref[seat * height : (seat + 1) * height, :] = dealt_ref[seat, lines:total, :]
        rest_ref[seat] = dealt_ref[seat, :lines, :]
    where, extra = blocks_of(padded, width, columns)
    slab_ref[base + extra - 16 : base + extra, :] = jnp.zeros((16, columns), BF)
    for r, c, row, lane in where:
        value = tall(down_ref[r : r + min(16, piece - r), c : c + 128], 16)
        slab_ref[base + row : base + row + 16, lane : lane + 128] = value


def slab_pass(dealt, down, lines, padded):
    team, total, columns = dealt.shape
    extra = blocks_of(padded, down.shape[1], columns)[1]
    return pl.pallas_call(
        lambda *refs: slab_kernel(padded, *refs),
        out_shape=[
            jax.ShapeDtypeStruct((team * (total - lines) + extra, columns), BF),
            jax.ShapeDtypeStruct((team, lines, columns), BF),
        ],
        compiler_params=MEMORY,
        cost_estimate=FREE,
    )(dealt, down)


def assemble_kernel(lines, side_ref, near_ref, far_ref, *outs):
    team = near_ref.shape[0]

    def fill(half, ref):
        for seat in range(team):
            first = (half * team + seat) * lines
            outs[0][first : first + lines, :] = ref[seat, :lines, :]
            if len(outs) == 2:
                rank = outs[1].shape[1]
                padded = outs[1].shape[0] // (2 * team)
                for row in range(0, padded, 16):
                    start = row // 16 * rank
                    first = (half * team + seat) * padded + row
                    outs[1][first : first + 16, :] = ref[
                        seat, lines : lines + 16, start : start + rank
                    ]

    for half in range(2):

        @pl.when(side_ref[0] == half)
        def _(half=half):
            fill(half, near_ref)
            fill(1 - half, far_ref)


def assemble_pass(side, near, far, lines, shard, rank):
    team, height, columns = near.shape
    shapes = [jax.ShapeDtypeStruct((2 * team * lines, columns), BF)]
    if height > lines:
        shapes.append(jax.ShapeDtypeStruct((shard, rank), BF))
    vmem = pl.BlockSpec(memory_space=pltpu.VMEM)
    return pl.pallas_call(
        lambda *refs: assemble_kernel(lines, *refs),
        in_specs=[pl.BlockSpec(memory_space=pltpu.SMEM), vmem, vmem],
        out_specs=[vmem] * len(shapes),
        out_shape=shapes,
        compiler_params=MEMORY,
        cost_estimate=FREE,
    )(side, near, far)


def fold_ff_kernel(order_ref, *refs):
    slabs = refs[:-7]
    enter_ref, leave_ref, down_enter_ref, down_leave_ref, gateup_out, down_out, blocks = refs[-7:]
    rank = leave_ref.shape[0]
    height, columns = gateup_out.shape
    shard = columns // 2
    step = pl.program_id(0)
    for index in range(2):
        start = index * shard
        lift = matmul(
            enter_ref[:, index * rank : (index + 1) * rank], leave_ref[:, start : start + shard]
        )
        for which, slab_ref in enumerate(slabs):

            @pl.when(step == which)
            def _(slab_ref=slab_ref, lift=lift, start=start):
                part = slab_ref[:height, start : start + shard].astype(F32)
                gateup_out[:, start : start + shard] = (part + lift).astype(BF)

    for which, slab_ref in enumerate(slabs):

        @pl.when(step == which)
        def _(slab_ref=slab_ref):
            blocks[...] = slab_ref[height:, :]

    lift = matmul(down_enter_ref[...], down_leave_ref[...])
    padded, width = down_out.shape
    wide = width // 128
    where, _ = blocks_of(padded, width, columns)
    for first in range(0, len(where), wide):
        r = where[first][0]
        parts = [
            blocks[row : row + 16, lane : lane + 128]
            for _, _, row, lane in where[first : first + wide]
        ]
        part = jnp.concatenate(parts, axis=1).astype(F32)
        down_out[r : r + 16, :] = (part + lift[r : r + 16]).astype(BF)


def fold_ff_pass(order, slabs, enter, leave, down_enter, down_leave, padded):
    count = len(slabs)
    columns, width = leave.shape[1], down_leave.shape[1]
    height = enter.shape[0] // count

    def own(rows, wide):
        return pl.BlockSpec((rows, wide), lambda i, o: (o[i], 0))

    return pl.pallas_call(
        fold_ff_kernel,
        grid_spec=pltpu.PrefetchScalarGridSpec(
            num_scalar_prefetch=1,
            grid=(count,),
            in_specs=[held(slab) for slab in slabs]
            + [
                own(height, enter.shape[1]),
                held(leave),
                own(padded, down_enter.shape[1]),
                held(down_leave),
            ],
            out_specs=[own(height, columns), own(padded, width)],
            scratch_shapes=[pltpu.VMEM((slabs[0].shape[0] - height, columns), BF)],
        ),
        out_shape=[
            jax.ShapeDtypeStruct((count * height, columns), BF),
            jax.ShapeDtypeStruct((count * padded, width), BF),
        ],
        compiler_params=MEMORY,
        cost_estimate=FREE,
    )(order, *slabs, enter, leave, down_enter, down_leave)


def fold_attn_kernel(bands, order_ref, *refs):
    slabs = refs[:-6]
    enter_ref, leave_ref, out_enter_ref, out_leave_ref, in_out, out_out = refs[-6:]
    rank = leave_ref.shape[0]
    height, width = in_out.shape[0], out_out.shape[1]
    step = pl.program_id(0)
    lifts = [
        matmul(enter_ref[:, i * rank : (i + 1) * rank], leave_ref[:, start : start + size])
        for i, (start, size) in enumerate(bands)
    ]
    out_lift = matmul(out_enter_ref[...], out_leave_ref[...])
    for which, slab_ref in enumerate(slabs):

        @pl.when(step == which)
        def _(slab_ref=slab_ref):
            for (start, size), lift in zip(bands, lifts):
                part = slab_ref[:height, start : start + size].astype(F32)
                in_out[:, start : start + size] = (part + lift).astype(BF)
            part = slab_ref[height:, :width].astype(F32)
            out_out[...] = (part + out_lift).astype(BF)


def fold_attn_pass(order, slabs, enter, leave, out_enter, out_leave, bands):
    count = len(slabs)
    height, short = enter.shape[0] // count, out_enter.shape[0] // count

    def own(rows, wide):
        return pl.BlockSpec((rows, wide), lambda i, o: (o[i], 0))

    return pl.pallas_call(
        lambda *refs: fold_attn_kernel(bands, *refs),
        grid_spec=pltpu.PrefetchScalarGridSpec(
            num_scalar_prefetch=1,
            grid=(count,),
            in_specs=[held(slab) for slab in slabs]
            + [
                own(height, enter.shape[1]),
                held(leave),
                own(short, out_enter.shape[1]),
                held(out_leave),
            ],
            out_specs=[own(height, leave.shape[1]), own(short, out_leave.shape[1])],
        ),
        out_shape=[
            jax.ShapeDtypeStruct((enter.shape[0], leave.shape[1]), BF),
            jax.ShapeDtypeStruct((out_enter.shape[0], out_leave.shape[1]), BF),
        ],
        compiler_params=MEMORY,
        cost_estimate=FREE,
    )(order, *slabs, enter, leave, out_enter, out_leave)


def slabs_out_kernel(order_ref, gateup_ref, down_ref, out_ref):
    height, columns = gateup_ref.shape
    padded, width = down_ref.shape
    out_ref[0, :height, :] = gateup_ref[...]
    where, extra = blocks_of(padded, width, columns)
    out_ref[0, height + extra - 16 :, :] = jnp.zeros((16, columns), BF)
    for r, c, row, lane in where:
        value = down_ref[r : r + 16, c : c + 128]
        out_ref[0, height + row : height + row + 16, lane : lane + 128] = value


def slabs_out_pass(order, gateup, down, parts):
    columns, width = gateup.shape[1], down.shape[1]
    height, padded = gateup.shape[0] // parts, down.shape[0] // parts
    rows = height + blocks_of(padded, width, columns)[1]
    count = order.shape[0]
    return pl.pallas_call(
        slabs_out_kernel,
        grid_spec=pltpu.PrefetchScalarGridSpec(
            num_scalar_prefetch=1,
            grid=(count,),
            in_specs=[
                pl.BlockSpec((height, columns), lambda i, o: (o[i], 0)),
                pl.BlockSpec((padded, width), lambda i, o: (o[i], 0)),
            ],
            out_specs=pl.BlockSpec((1, rows, columns), lambda i, o: (i, 0, 0)),
        ),
        out_shape=jax.ShapeDtypeStruct((count, rows, columns), BF),
        compiler_params=MEMORY,
        cost_estimate=FREE,
    )(order, gateup, down)


def sides_kernel(order_ref, *refs):
    enters, grad_ref = refs[:4], refs[4]
    downs = refs[5:-2]
    lines = 2 * enters[0].shape[1]
    shard = grad_ref.shape[1] // 2
    for side, out_ref in enumerate(refs[-2:]):
        team = out_ref.shape[0]
        lines = enters[0].shape[1] // team
        for half in range(2):
            value = outer_sum(
                enters[2 * half + side][...], grad_ref[:, half * shard : (half + 1) * shard]
            ).astype(BF)
            for seat in range(team):
                out_ref[seat, :lines, half * shard : (half + 1) * shard] = value[
                    seat * lines : (seat + 1) * lines
                ]
        if downs:
            value = through(downs[side][...], downs[2][...]).astype(BF)
            rank = value.shape[1]
            padded = value.shape[0] // team
            for seat in range(team):
                for row in range(0, padded, 16):
                    start = row // 16 * rank
                    first = seat * padded + row
                    out_ref[seat, lines : lines + 16, start : start + rank] = value[
                        first : first + 16
                    ]


def sides_pass(order, enter, grad, down, down_leave, team, together):
    width, columns = grad.shape
    half = enter.shape[1] // 4

    def near_or_far(rows, wide, at):
        return pl.BlockSpec((rows, wide), at)

    specs = [
        pl.BlockSpec((width, half), lambda i, o: (0, o[0])),
        pl.BlockSpec((width, half), lambda i, o: (0, o[1])),
        pl.BlockSpec((width, half), lambda i, o: (0, 2 + o[0])),
        pl.BlockSpec((width, half), lambda i, o: (0, 2 + o[1])),
        held(grad),
    ]
    arrays = [enter] * 4 + [grad]
    lines = half // team
    if together:
        lines += 16
        rows = down.shape[0] // 2
        specs += [
            pl.BlockSpec((rows, down.shape[1]), lambda i, o: (o[0], 0)),
            pl.BlockSpec((rows, down.shape[1]), lambda i, o: (o[1], 0)),
            held(down_leave),
        ]
        arrays += [down, down, down_leave]
    shape = (team, lines, columns)
    return pl.pallas_call(
        sides_kernel,
        grid_spec=pltpu.PrefetchScalarGridSpec(
            num_scalar_prefetch=1,
            grid=(1,),
            in_specs=specs,
            out_specs=[pl.BlockSpec(shape, lambda i, o: (0, 0, 0))] * 2,
        ),
        out_shape=[jax.ShapeDtypeStruct(shape, BF)] * 2,
        compiler_params=MEMORY,
        cost_estimate=FREE,
    )(order, *arrays)


def home_kernel(piece, near_ref, far_ref, mine_ref, other_ref, dealt_ref, down_ref):
    team, total, columns = dealt_ref.shape
    lines = mine_ref.shape[1]
    height = total - lines
    base = team * height
    for seat in range(team):
        rest = mine_ref[seat].astype(F32) + other_ref[seat].astype(F32)
        dealt_ref[seat, :lines, :] = rest.astype(BF)
        rows = slice(seat * height, (seat + 1) * height)
        value = near_ref[rows, :].astype(F32) + far_ref[rows, :].astype(F32)
        dealt_ref[seat, lines:total, :] = value.astype(BF)
    width = down_ref.shape[1]
    for r, c, row, lane in blocks_of(even(piece), width, columns)[0]:
        rows, lanes = slice(base + row, base + row + 16), slice(lane, lane + 128)
        value = near_ref[rows, lanes].astype(F32) + far_ref[rows, lanes].astype(F32)
        size = min(16, piece - r)
        down_ref[r : r + size, c : c + 128] = value[:size]


def home_pass(near, far, mine, other, piece, width, height):
    team, lines, columns = mine.shape
    return pl.pallas_call(
        lambda *refs: home_kernel(piece, *refs),
        out_shape=[
            jax.ShapeDtypeStruct((team, lines + height, columns), BF),
            jax.ShapeDtypeStruct((piece, width), F32),
        ],
        compiler_params=MEMORY,
        cost_estimate=FREE,
    )(near, far, mine, other)


def join_kernel(piece, padded, in_ref, *outs):
    team, total, columns = in_ref.shape
    units, shard = outs[0].shape[1] // 2, columns // 2
    lines = outs[0].shape[0]
    for out_ref, row in ((outs[0], 0), (outs[1], total - outs[1].shape[0])):
        height = out_ref.shape[0]
        for half in range(2):
            for block in range(shard // padded):
                first = half * shard + block * padded
                parts = [
                    in_ref[seat, row : row + height, first : first + piece] for seat in range(team)
                ]
                start = half * units + block * team * piece
                joined = jnp.concatenate(parts, axis=1).astype(F32)
                out_ref[:, start : start + team * piece] = joined
    if len(outs) == 3:
        rank = outs[2].shape[1]
        for seat in range(team):
            for row in range(0, padded, 16):
                size = min(16, piece - row)
                start = row // 16 * rank
                value = in_ref[seat, lines : lines + size, start : start + rank]
                first = seat * piece + row
                outs[2][first : first + size, :] = value.astype(F32)


def join_pass(parts, lines, height, piece, padded, rank):
    team, total, columns = parts.shape
    wide = columns // padded * piece * team
    shapes = [(lines, wide), (height, wide)]
    if total > lines + height:
        shapes.append((team * piece, rank))
    return pl.pallas_call(
        lambda *refs: join_kernel(piece, padded, *refs),
        out_shape=[jax.ShapeDtypeStruct(shape, F32) for shape in shapes],
        compiler_params=MEMORY,
        cost_estimate=FREE,
    )(parts)


def per_device(
    tokens,
    cotangent,
    exit_depth,
    lengths,
    loop_index,
    attn_gain,
    mlp_gain,
    qkv_weight,
    out_weight,
    gateup_weight,
    down_weight,
    qkv_enter,
    query_leave,
    kv_leave,
    out_enter,
    out_leave,
    gateup_enter,
    gateup_leave,
    down_enter,
    down_leave,
):
    loops = lax.axis_size("depth")
    rows = lax.axis_size("rows")
    group = lax.axis_index("depth")
    place = lax.axis_index("rows")
    slots, seq_dev, width = tokens.shape
    sub = rows // slots
    team = rows // 2
    count = slots * seq_dev
    teams = [[h * team + k for k in range(team)] for h in range(2)]
    seq_here, mate, core = place // sub, place % sub, place % 2
    side, seat = place // team, place % team
    levels = jnp.arange(loops, dtype=jnp.int32)

    head = kv_leave.shape[2] // 2
    width_q = query_leave.shape[2]
    rank = qkv_enter.shape[2] // 3
    hidden_units = gateup_weight.shape[1] // 2
    piece = down_weight.shape[0]
    padded = -(-piece // 16) * 16
    shard = 2 * loops * padded
    slab = width // (2 * loops)
    gain_size = attn_gain.shape[0]

    def turn(values):
        return jnp.stack(
            [values[0]] + [swap(values[f], "rows", f * sub) for f in range(1, slots)]
        )

    def deal(values):
        return lax.all_to_all(
            values, "rows", split_axis=0, concat_axis=0, axis_index_groups=teams, tiled=True
        )

    def pick(array, index):
        return array.at[index].get(mode="promise_in_bounds")

    def halve(array, bit):
        half = array.shape[0] // 2
        return array[:half], swap(array[half:], "rows", bit)

    def halve_but_last(array, bits):
        for bit in bits[:-1]:
            array = add_low(*halve(array, bit))
        return array

    def own_half(array, which):
        height = array.shape[0] // 2
        return lax.dynamic_slice(array, (which * height, 0), (height, array.shape[1]))

    def positions_of(who):
        blocks = (seq_here ^ levels) * sub + who
        return (blocks[:, None] * seq_dev + jnp.arange(seq_dev, dtype=jnp.int32)[None, :]).reshape(
            count
        )

    depth_flips = [0, 1, 2, 3]
    halves_order = jnp.stack([(group ^ f) * 2 + (core ^ e) for f in depth_flips for e in (0, 1)])
    flips = [(d, f) for d in range(4) for f in range(2)]
    slab_at = {(d, f): (group ^ d) * 2 + (side ^ f) for d, f in flips}
    team_bits, sub_bits, row_bits = bits_of(team), bits_of(sub), bits_of(rows)
    bands = [(0, width_q), (width_q, head), (width_q + head, head)]
    together = team == loops
    lines = gateup_leave.shape[1]
    with_enter = lines + 16 if together else lines

    table = loop_index.reshape(loops, loops)
    mine = lax.dynamic_index_in_dim(table, group, 0, keepdims=False)
    order = jnp.sum((mine[None, :] == levels[:, None]).astype(jnp.int32) * levels[None, :], axis=1)
    sizes_here = jnp.sum(jnp.where(table == group, lengths.reshape(loops, loops), 0), axis=1)
    size_here = lax.dynamic_slice(sizes_here, (seq_here,), (1,))
    positions = positions_of(mate)
    cosine, sine = angles(positions.astype(F32), head)
    gains = jnp.concatenate([attn_gain, mlp_gain])[None]
    gains = jnp.concatenate([gains] + [swap(gains, "depth", f) for f in depth_flips[1:]])
    gains = pick(gains, group ^ levels)
    small = [
        qkv_weight,
        qkv_enter[0],
        jnp.concatenate([query_leave[0], kv_leave[0]], axis=1),
        out_weight,
        out_enter[0],
        out_leave[0],
        gains,
    ]
    small_shapes = [array.shape for array in small]
    late = [gateup_enter[0], down_leave[0]]
    late_shapes = [array.shape for array in late]
    late_packed = pack_pass(late)
    packed = lax.all_gather(pack_pass(small), "rows", axis=0, tiled=True)
    arrived = lax.all_to_all(
        pick(tokens, order), "depth", split_axis=0, concat_axis=0, tiled=True
    )
    dealt = deal_pass(
        [gateup_weight, gateup_leave[0]] + [down_enter[0]] * together, team, piece, padded
    )
    upstream_low = turn(pick(cotangent, seq_here ^ levels)).reshape(count, width)
    arrived, dealt, upstream_low = tie(arrived, dealt, upstream_low)
    inputs = turn(pick(arrived, seq_here ^ levels)).reshape(count, width)
    dealt = deal(dealt)
    inputs, dealt, packed, upstream_low = tie(inputs, dealt, packed, upstream_low)

    slab_near, rest_near = slab_pass(dealt, down_weight, with_enter, padded)
    slab_far = swap(slab_near, "rows", team)
    (
        qkv_slab,
        full_qkv_enter,
        full_leave,
        out_slab,
        full_out_enter,
        full_out_leave,
        gain_slab,
    ) = unpack_pass(packed, small_shapes, BF)
    gain_slab = gain_slab.reshape(rows, loops, 2, -1)
    both_gains = gain_slab.transpose(2, 1, 0, 3).reshape(2, 1, width).astype(F32)
    gain_one, gain_two = both_gains[0], both_gains[1]
    spare = qkv_slab.shape[1] - width

    def both_halves(which):
        return jnp.concatenate(
            [own_half(qkv_slab, which), jnp.pad(own_half(out_slab, which), ((0, 0), (0, spare)))]
        )

    half_here = both_halves(core)
    fetched = [swap(half_here, "depth", f) for f in depth_flips[1:]]
    fetched, slab_near, slab_far, upstream_low, rest_near = tie(
        fetched, slab_near, slab_far, upstream_low, rest_near
    )
    others = swap(jnp.stack(fetched), "rows", 1)
    others, slab_near, rest_near, late_packed = tie(others, slab_near, rest_near, late_packed)
    late_packed = lax.all_gather(late_packed, "rows", axis=0, tiled=True)
    rest_far = swap(rest_near, "rows", team)
    slabs = {(0, 0): slab_near, (0, 1): slab_far}
    slabs[(1, 0)] = swap(slab_near, "depth", 1)
    slabs[(2, 0)] = swap(slab_near, "depth", 2)
    slabs[(1, 1)] = swap(slab_far, "depth", 1)
    slabs[(2, 1)] = swap(slab_far, "depth", 2)
    halves = [half_here, both_halves(core ^ 1)]
    for f in range(3):
        halves += [fetched[f], others[f]]
    qkv_eff, out_eff = fold_attn_pass(
        halves_order, halves, full_qkv_enter, full_leave, full_out_enter, full_out_leave, bands
    )
    normed_one, queries, pairs_all = enter_pass(
        inputs, gain_one, qkv_eff, cosine, sine, width_q
    )
    pairs_all, rest_far, slabs, upstream_low = tie(pairs_all, rest_far, slabs, upstream_low)
    cotan_far = swap(upstream_low, "rows", team_bits[-1])
    slabs[(3, 0)] = swap(slabs[(1, 0)], "depth", 2)
    slabs[(3, 1)] = swap(slabs[(2, 1)], "depth", 1)
    mates = [0]
    for bit in sub_bits:
        pairs_all = jnp.concatenate([pairs_all, swap(pairs_all, "rows", bit)])
        mates = mates + [f | bit for f in mates]
    key_pos = jnp.concatenate([positions_of(mate ^ f) for f in mates])[None]
    attended, log_total = attend_pass(
        size_here, queries, pairs_all, positions[:, None], key_pos, seq_dev
    )
    mixed, normed_two = leave_pass(inputs, attended, out_eff, gain_two)
    normed_two, slabs, cotan_far = tie(normed_two, slabs, cotan_far)

    def gather_team(value, far):
        value = jnp.concatenate([value, far])
        for bit in team_bits[-2::-1]:
            value = jnp.concatenate([value, swap(value, "rows", bit)])
        return value

    normed_far = swap(normed_two, "rows", team_bits[-1])
    full_gateup_enter, full_down_leave = unpack_pass(late_packed, late_shapes, BF)
    leave_full, *enter_full = assemble_pass(
        side[None], rest_near, rest_far, lines, shard, rank
    )
    if together:
        enter_full = enter_full[0]
    else:
        enter_every = lax.all_gather(down_enter[0], "rows", axis=0, tiled=True)
        enter_every = enter_every.reshape(loops, 2, team, piece, rank)
        enter_full = lax.dynamic_index_in_dim(enter_every, seat, 2, keepdims=False)
        enter_full = jnp.pad(enter_full, ((0, 0), (0, 0), (0, padded - piece), (0, 0)))
        enter_full = enter_full.reshape(shard, rank)
    gateup_eff, down_eff = fold_ff_pass(
        jnp.stack([slab_at[f] for f in flips]),
        [slabs[f] for f in flips],
        full_gateup_enter,
        leave_full,
        enter_full,
        full_down_leave,
        padded,
    )
    normed_far, gateup_eff, down_eff = tie(normed_far, gateup_eff, down_eff)
    cotan_team = gather_team(upstream_low, cotan_far)
    normed_team = gather_team(normed_two, normed_far)

    hidden, grad_expanded, grad_normed = ff_pass(
        normed_team, cotan_team, gateup_eff, down_eff, 256
    )

    grad_normed = halve_but_last(grad_normed, team_bits)
    grad_normed, hidden, grad_expanded = tie(grad_normed, hidden, grad_expanded)
    grad_terms = halve(grad_normed, team_bits[-1])
    grad_gateup = outer_sum(normed_team, grad_expanded).astype(BF)
    grad_down = outer_sum(hidden, cotan_team).astype(BF)
    grad_terms, grad_gateup, grad_down, hidden = tie(grad_terms, grad_gateup, grad_down, hidden)

    def slabs_out(*which):
        index = jnp.stack([slab_at[f] for f in which])
        return slabs_out_pass(index, grad_gateup, grad_down, 2 * loops)

    near_sent, far_sent = slabs_out((2, 0), (3, 0)), slabs_out((1, 1), (3, 1))
    near_sent, far_sent, grad_gateup, grad_down = tie(
        near_sent, far_sent, grad_gateup, grad_down
    )
    near_got = swap(near_sent, "depth", 2)
    far_got = swap(far_sent, "depth", 1)
    sides = jnp.stack([side, side ^ 1])
    side_near, side_far = sides_pass(
        sides, full_gateup_enter, grad_gateup, grad_down, full_down_leave, team, together
    )
    side_near, side_far, grad_terms, hidden = tie(side_near, side_far, grad_terms, hidden)
    side_got = swap(side_far, "rows", team)
    grad_mixed, grad_branch, grad_attended, grad_gain_second = leave_back_pass(
        *grad_terms, mixed, gain_two, upstream_low, out_eff
    )
    grad_queries, key_terms = attend_back_pass(
        size_here,
        queries,
        pairs_all,
        grad_attended,
        log_total,
        positions[:, None],
        key_pos,
        cosine,
        sine,
        seq_dev,
    )
    mate_order = halving_order(sub_bits)
    if mate_order != mates:
        key_terms = jnp.concatenate(
            [key_terms[i * count : (i + 1) * count] for i in map(mates.index, mate_order)]
        )
    outcome = matmul(hidden, down_eff).astype(BF)
    near_kept, far_kept = slabs_out((0, 0), (1, 0)), slabs_out((0, 1), (2, 1))
    key_terms, grad_queries, near_got, far_got, outcome, near_kept, far_kept, side_got = tie(
        key_terms, grad_queries, near_got, far_got, outcome, near_kept, far_kept, side_got
    )
    pair_terms = halve(halve_but_last(key_terms, sub_bits), sub_bits[-1])
    outcome = halve_but_last(outcome, team_bits)
    pair_terms, outcome = tie(pair_terms, outcome)

    grad_joined, grad_inputs, grad_gain_first = enter_back_pass(
        grad_queries, pair_terms, cosine, sine, qkv_eff, inputs, gain_one, grad_mixed
    )
    near_one, far_one = add_low(near_kept[1], near_got[1]), add_low(far_kept[1], far_got[1])
    near_one, far_one = swap(near_one, "depth", 1), swap(far_one, "depth", 2)
    outcome = halve(outcome, team_bits[-1])
    grad_qkv = outer_sum(normed_one, grad_joined).astype(BF)
    grad_out = outer_sum(attended, grad_branch).astype(BF)

    near_one, far_one, outcome, grad_inputs, grad_qkv, grad_out = tie(
        near_one, far_one, outcome, grad_inputs, grad_qkv, grad_out
    )

    def loop_part(flip):
        parts = []
        for array in (grad_qkv, grad_out):
            height = array.shape[0] // loops
            part = lax.dynamic_slice(array, ((group ^ flip) * height, 0), (height, array.shape[1]))
            parts.append(jnp.pad(part, ((0, 0), (0, grad_qkv.shape[1] - array.shape[1]))))
        return jnp.concatenate(parts)

    terms = [loop_part(0)] + [swap(loop_part(f), "depth", f) for f in depth_flips[1:]]
    near_sum = add_low(near_kept[0], near_got[0])
    far_sum = add_low(far_kept[0], far_got[0])
    result = mixed + (outcome[0].astype(F32) + outcome[1].astype(F32))
    result_low = result.astype(BF)
    near_sum, far_sum = add_low(near_sum, near_one), add_low(far_sum, far_one)
    far_sum = swap(far_sum, "rows", team)
    result_low, grad_qkv, grad_out, near_sum, far_sum, terms = tie(
        result_low, grad_qkv, grad_out, near_sum, far_sum, terms
    )

    dealt, grad_down_weight = home_pass(
        near_sum, far_sum, side_near, side_got, piece, width, slab // team
    )
    homeward = jnp.concatenate(
        [result_low.reshape(slots, seq_dev, width), grad_inputs.reshape(slots, seq_dev, width)],
        axis=1,
    )

    homeward, dealt = tie(homeward, dealt)
    homeward = turn(homeward)
    dealt = deal(dealt)
    row_place = jnp.arange(rows, dtype=jnp.int32)

    def to_owner(packed):
        return lax.psum_scatter(packed, "rows", scatter_dimension=0, tiled=True)

    qkv_rows = grad_qkv.shape[0] // loops
    rest_grads_of = [
        ((terms[0].shape[0] - qkv_rows) // rows, width),
        (grad_out.shape[0] // rows, rank),
        (rank // rows, width),
        (width // rows, rank),
        (width // rows, rank),
        (rank // rows, width),
    ]
    rest_sum = grads_pass(
        lambda *refs: rest_grads_kernel(qkv_rows, *refs),
        row_place,
        rows,
        rest_grads_of,
        [
            *terms,
            grad_out,
            full_out_enter,
            full_out_leave,
            grad_gateup,
            leave_full,
            grad_down,
            enter_full,
        ],
    )
    rest_sum = to_owner(rest_sum)
    attn_grads_of = attn_grads_shapes(rows, qkv_rows, grad_qkv, full_qkv_enter, full_leave, bands)
    attn_sum = grads_pass(
        lambda *refs: attn_grads_kernel(qkv_rows, bands, *refs),
        row_place,
        rows,
        attn_grads_of,
        [*terms, grad_qkv, full_qkv_enter, full_leave],
    )
    attn_sum = to_owner(attn_sum)
    homeward, dealt = tie(homeward, dealt)
    returned = lax.all_to_all(
        pick(homeward[:, seq_dev:], seq_here ^ levels),
        "depth",
        split_axis=0,
        concat_axis=0,
        tiled=True,
    )

    grad_tokens = pick(returned, mine)
    activations = pick(homeward[:, :seq_dev], seq_here ^ levels)
    own_out, *rest_grads = unpack_pass(
        rest_sum, rest_grads_of, F32, [[0], [1], [2], [3, 4], [5]]
    )
    own_qkv, *attn_grads = unpack_pass(
        attn_sum, attn_grads_of, F32, [[0], [1, 2, 3], [4], [5, 6]]
    )
    grad_gateup_leave, grad_gateup_weight, *grad_down_enter = join_pass(
        dealt, lines, slab // team, piece, padded, rank
    )
    if together:
        grad_down_enter = grad_down_enter[0]
    else:
        grad_down_in = through(grad_down, full_down_leave).astype(BF)
        grad_down_in = grad_down_in.reshape(loops, 2, 1, padded, rank)[:, :, :, :piece]
        spaced = jnp.zeros((loops, 2, team, piece, rank), BF)
        spaced = lax.dynamic_update_slice(spaced, grad_down_in, (0, 0, seat, 0, 0))
        grad_down_enter = lax.psum_scatter(
            spaced.reshape(hidden_units, rank), "rows", scatter_dimension=0, tiled=True
        ).astype(F32)

    block_pos = place * seq_dev + jnp.arange(seq_dev, dtype=jnp.int32)
    valid = block_pos[None, :] < sizes_here[:, None]
    counts_here = jnp.sum(
        ((exit_depth[None] == levels[:, None, None]) & valid[None]).astype(F32), axis=(1, 2)
    )
    given = inputs.astype(F32)
    cross = jnp.sum(given * result, axis=-1)
    own_sq = jnp.sum(given * given, axis=-1)
    out_sq = jnp.sum(result * result, axis=-1)
    cosines = cross * lax.rsqrt(own_sq * out_sq + 1e-06)
    cosine_here = jnp.sum(jnp.where(positions < size_here, cosines, 0.0))
    tallies = jnp.concatenate([counts_here, cosine_here[None]])
    gain_grads = jnp.concatenate([grad_gain_first, grad_gain_second])
    gain_grads = gain_grads.reshape(2, loops * rows, gain_size).transpose(1, 0, 2)
    small = jnp.concatenate(
        [
            jnp.broadcast_to(tallies[None], (loops * rows, loops + 1)),
            gain_grads.reshape(loops * rows, 2 * gain_size),
        ],
        axis=1,
    )
    small = jnp.pad(small, ((0, 0), (0, 127 - loops - 2 * gain_size)))
    small = lax.all_to_all(small, ("depth", "rows"), split_axis=0, concat_axis=0, tiled=True)
    small = jnp.sum(small, axis=0)
    tallies = small[: loops + 1]
    gain_grads = small[loops + 1 : loops + 1 + 2 * gain_size].reshape(2, gain_size)
    exit_counts = tallies[:loops].astype(jnp.int32)
    confidence = tallies[loops] / jnp.sum(lengths).astype(F32)

    return (
        activations,
        grad_tokens,
        exit_counts,
        confidence,
        gain_grads[0],
        gain_grads[1],
        own_qkv,
        own_out,
        grad_gateup_weight,
        grad_down_weight,
        attn_grads[0][None],
        attn_grads[1][None],
        attn_grads[2][None],
        rest_grads[0][None],
        rest_grads[1][None],
        rest_grads[2][None],
        grad_gateup_leave[None],
        grad_down_enter[None],
        rest_grads[3][None],
    )


def solution(mesh):
    split = P("depth", "rows", None)
    flat = P(("depth", "rows"))
    tall = P(("depth", "rows"), None)
    return jax.shard_map(
        per_device,
        mesh=mesh,
        in_specs=(split, split, P("depth", "rows"), P(), P(), flat, flat)
        + (tall,) * 4
        + (split,) * 9,
        out_specs=(split, split, P(), P(), flat, flat) + (tall,) * 4 + (split,) * 9,
        check_vma=False,
    )
```

```python
import math

import jax
import jax.numpy as jnp
from jax import lax
from jax.experimental import pallas as pl
from jax.experimental.pallas import tpu as pltpu
from jax.sharding import PartitionSpec as P

BF = jnp.bfloat16
F32 = jnp.float32
ROOT = math.sqrt(2.0 / math.pi)
CUBE = 0.044715


def angles(positions, size):
    freqs = jnp.exp(jnp.arange(size // 2, dtype=F32) * (-2.0 * math.log(10000.0) / size))
    phase = positions[:, None] * freqs[None, :]
    return (jnp.cos(phase), jnp.sin(phase))


def matmul(left, right):
    return jnp.dot(left, right, preferred_element_type=F32)


def outer_sum(left, right):
    return lax.dot_general(left, right, (((0,), (0,)), ((), ())), preferred_element_type=F32)


def through(left, right):
    return lax.dot_general(left, right, (((1,), (1,)), ((), ())), preferred_element_type=F32)


def swap(value, axis, flip):
    size = lax.axis_size(axis)
    return lax.ppermute(value, axis, [(i, i ^ flip) for i in range(size)])


def add_low(left, right):
    return (left.astype(F32) + right.astype(F32)).astype(BF)


def tie(*values):
    return lax.optimization_barrier(values)


def bits_of(size):
    return [1 << i for i in range(size.bit_length() - 1)]


LANES = 256


def even(height):
    return -(-height // 16) * 16


def segments(shapes):
    out, row = [], 0
    for which, (height, columns) in enumerate(shapes):
        for start in range(0, columns, LANES):
            out.append((which, row, start, min(LANES, columns - start)))
            row += even(height)
    return out, row


def put(out_ref, lead, row, height, value):
    short, narrow = even(height) - height, LANES - value.shape[1]
    if narrow:
        value = jnp.concatenate([value, jnp.zeros((height, narrow), value.dtype)], axis=1)
    if short:
        value = jnp.concatenate([value, jnp.zeros((short, LANES), value.dtype)], axis=0)
    out_ref[lead, row : row + even(height), :] = value


def pack_kernel(shapes, *refs):
    where, _ = segments(shapes)
    for which, row, start, size in where:
        put(refs[-1], 0, row, shapes[which][0], refs[which][:, start : start + size])


def pack_pass(arrays):
    shapes = [array.shape for array in arrays]
    return pl.pallas_call(
        lambda *refs: pack_kernel(shapes, *refs),
        out_shape=jax.ShapeDtypeStruct((1, segments(shapes)[1], LANES), BF),
        compiler_params=MEMORY,
        cost_estimate=FREE,
    )(*arrays)


def unpack_kernel(shapes, into, in_ref, *outs):
    for which, row, start, size in segments(shapes)[0]:
        height = shapes[which][0]
        out, column = into[which]
        column += start
        for lead in range(in_ref.shape[0]):
            value = in_ref[lead, row : row + height, :size]
            first = lead * height
            outs[out][first : first + height, column : column + size] = value.astype(
                outs[out].dtype
            )


def unpack_pass(packed, shapes, dtype, groups=None):
    lead = packed.shape[0]
    groups = groups or [[which] for which in range(len(shapes))]
    into, out_shapes = {}, []
    for out, group in enumerate(groups):
        column = 0
        for which in group:
            into[which] = (out, column)
            column += shapes[which][1]
        shape = (lead * shapes[group[0]][0], column)
        out_shapes.append(jax.ShapeDtypeStruct(shape, dtype))
    return pl.pallas_call(
        lambda *refs: unpack_kernel(shapes, into, *refs),
        out_shape=out_shapes,
        compiler_params=MEMORY,
        cost_estimate=FREE,
    )(packed)


def spread_rows(pos_ref, out_ref, row, value, first, size):
    leads = out_ref.shape[0]
    height = value.shape[0] // leads
    for lead in range(leads):
        block = value[lead * height : (lead + 1) * height, first : first + size]
        put(out_ref, pos_ref[lead], row, height, block.astype(BF))


def total_of(refs, rows, columns):
    total = refs[0][rows, :columns].astype(F32)
    for ref in refs[1:]:
        total = total + ref[rows, :columns].astype(F32)
    return total


def place_all(pos_ref, out_ref, values):
    shapes = [(value.shape[0] // out_ref.shape[0], value.shape[1]) for value in values]
    for which, row, start, size in segments(shapes)[0]:
        spread_rows(pos_ref, out_ref, row, values[which], start, size)


def attn_grads_kernel(height, bands, pos_ref, *refs):
    grad_ref, enter_ref, leave_ref, out_ref = refs[-4:]
    rank = leave_ref.shape[0]
    values = [total_of(refs[:-4], slice(0, height), grad_ref.shape[1])]
    for start, size in bands:
        values.append(through(grad_ref[:, start : start + size], leave_ref[:, start : start + size]))
    for index, (start, size) in enumerate(bands):
        enter = enter_ref[:, index * rank : (index + 1) * rank]
        values.append(outer_sum(enter, grad_ref[:, start : start + size]))
    place_all(pos_ref, out_ref, values)


def attn_grads_shapes(rows, height, grad, enter, leave, bands):
    rank = leave.shape[0]
    return (
        [(height // rows, grad.shape[1])]
        + [(grad.shape[0] // rows, rank)] * len(bands)
        + [(rank // rows, size) for _, size in bands]
    )


def rest_grads_kernel(first, pos_ref, *refs):
    (
        grad_out_ref,
        out_enter_ref,
        out_leave_ref,
        grad_gateup_ref,
        leave_ref,
        grad_down_ref,
        down_enter_ref,
        out_ref,
    ) = refs[-8:]
    shard = leave_ref.shape[1] // 2
    values = [
        total_of(refs[:-8], slice(first, refs[0].shape[0]), grad_out_ref.shape[1]),
        through(grad_out_ref[...], out_leave_ref[...]),
        outer_sum(out_enter_ref[...], grad_out_ref[...]),
        through(grad_gateup_ref[:, :shard], leave_ref[:, :shard]),
        through(grad_gateup_ref[:, shard:], leave_ref[:, shard:]),
        outer_sum(down_enter_ref[...], grad_down_ref[...]),
    ]
    place_all(pos_ref, out_ref, values)


def grads_pass(kernel, pos, rows, shapes, arrays):
    whole = [pl.BlockSpec(memory_space=pltpu.VMEM)] * len(arrays)
    shape = (rows, segments(shapes)[1], LANES)
    return pl.pallas_call(
        kernel,
        in_specs=[pl.BlockSpec(memory_space=pltpu.SMEM)] + whole,
        out_specs=pl.BlockSpec(memory_space=pltpu.VMEM),
        out_shape=jax.ShapeDtypeStruct(shape, BF),
        compiler_params=MEMORY,
        cost_estimate=FREE,
    )(pos, *arrays)


FREE = pl.CostEstimate(flops=0, transcendentals=0, bytes_accessed=0)
MEMORY = pltpu.CompilerParams(vmem_limit_bytes=60 << 20)


def held(array):
    return pl.BlockSpec(
        array.shape, lambda *_: (0,) * len(array.shape), pipeline_mode=pl.Buffered(1)
    )


def strip(tile, columns):
    return pl.BlockSpec((tile, columns), lambda i: (i, 0))


def mean_scale(values):
    return lax.rsqrt(jnp.mean(values * values, axis=-1, keepdims=True) + 1e-06)


def turned(values, cosine, sine):
    half = values.shape[-1] // 2
    first, second = values[:, :half], values[:, half:]
    return jnp.concatenate(
        [first * cosine - second * sine, second * cosine + first * sine], axis=-1
    )


def enter_kernel(x_ref, gain_ref, weight_ref, cos_ref, sin_ref, n_ref, q_ref, kv_ref):
    head = kv_ref.shape[1] // 2
    width_q = q_ref.shape[1]
    values = x_ref[...].astype(F32)
    normed = (values * mean_scale(values) * gain_ref[...]).astype(BF)
    n_ref[...] = normed
    joined = matmul(normed, weight_ref[...])
    cosine, sine = cos_ref[...], sin_ref[...]
    scale = head ** (-0.5)
    for start in range(0, width_q, head):
        spun = turned(joined[:, start : start + head], cosine, sine)
        q_ref[:, start : start + head] = (spun * scale).astype(BF)
    kv_ref[:, :head] = turned(joined[:, width_q : width_q + head], cosine, sine).astype(BF)
    kv_ref[:, head:] = joined[:, width_q + head :].astype(BF)


def enter_pass(x, gain, weight, cosine, sine, width_q):
    count, width = x.shape
    tile = count // 2
    rest = weight.shape[1] - width_q
    return pl.pallas_call(
        enter_kernel,
        grid=(count // tile,),
        in_specs=[
            strip(tile, width),
            held(gain),
            held(weight),
            strip(tile, cosine.shape[1]),
            strip(tile, cosine.shape[1]),
        ],
        out_specs=[strip(tile, width), strip(tile, width_q), strip(tile, rest)],
        out_shape=[
            jax.ShapeDtypeStruct((count, width), BF),
            jax.ShapeDtypeStruct((count, width_q), BF),
            jax.ShapeDtypeStruct((count, rest), BF),
        ],
        compiler_params=MEMORY,
        cost_estimate=FREE,
    )(x, gain, weight, cosine, sine)


def stack_heads(ref, head):
    return jnp.concatenate(
        [ref[:, start : start + head] for start in range(0, ref.shape[1], head)], axis=0
    )


def allowed_keys(size_ref, pos_ref, key_ref, heads):
    fits = (key_ref[...] <= pos_ref[...]) & (key_ref[...] < size_ref[0])
    return jnp.concatenate([jnp.where(fits, 0.0, -1e30)] * heads, axis=0)


def attend_kernel(size_ref, q_ref, kv_ref, pos_ref, key_ref, o_ref, lse_ref):
    head = kv_ref.shape[1] // 2
    tile = q_ref.shape[0]
    heads = q_ref.shape[1] // head
    scores = through(stack_heads(q_ref, head), kv_ref[:, :head])
    scores = scores + allowed_keys(size_ref, pos_ref, key_ref, heads)
    highest = jnp.max(scores, axis=-1, keepdims=True)
    raised = jnp.exp(scores - highest)
    total = jnp.sum(raised, axis=-1, keepdims=True)
    probs = (raised * (1.0 / total)).astype(BF)
    lse_ref[...] = (highest + jnp.log(total)).reshape(1, heads * tile, 1)
    mixed = matmul(probs, kv_ref[:, head:]).astype(BF)
    for index in range(heads):
        o_ref[:, index * head : (index + 1) * head] = mixed[index * tile : (index + 1) * tile]


def attend_pass(size, q, kv, positions, key_positions, tile):
    count, width_q = q.shape
    heads = 2 * width_q // kv.shape[1]
    steps = count // tile

    def rows(columns):
        return pl.BlockSpec((tile, columns), lambda i, s: (i, 0))

    return pl.pallas_call(
        attend_kernel,
        grid_spec=pltpu.PrefetchScalarGridSpec(
            num_scalar_prefetch=1,
            grid=(steps,),
            in_specs=[rows(width_q), held(kv), rows(1), held(key_positions)],
            out_specs=[rows(width_q), pl.BlockSpec((1, heads * tile, 1), lambda i, s: (i, 0, 0))],
        ),
        out_shape=[
            jax.ShapeDtypeStruct((count, width_q), BF),
            jax.ShapeDtypeStruct((steps, heads * tile, 1), F32),
        ],
        compiler_params=MEMORY,
        cost_estimate=FREE,
    )(size, q, kv, positions, key_positions)


def attend_back_kernel(
    size_ref, q_ref, kv_ref, do_ref, lse_ref, pos_ref, key_ref, cos_ref, sin_ref, dq_ref, dkv_ref, acc
):
    head = kv_ref.shape[1] // 2
    tile = q_ref.shape[0]
    heads = q_ref.shape[1] // head
    step = pl.program_id(0)
    queries = stack_heads(q_ref, head)
    grads = stack_heads(do_ref, head)
    keys = kv_ref[:, :head]
    scores = through(queries, keys) + allowed_keys(size_ref, pos_ref, key_ref, heads)
    probs = jnp.exp(scores - lse_ref[0])
    grad_probs = through(grads, kv_ref[:, head:])
    centre = jnp.sum(probs * grad_probs, axis=-1, keepdims=True)
    grad_scores = (probs * (grad_probs - centre)).astype(BF)
    grad_q = matmul(grad_scores, keys) * (head ** (-0.5))
    cosine, sine = cos_ref[...], -sin_ref[...]
    for index in range(heads):
        spun = turned(grad_q[index * tile : (index + 1) * tile], cosine, sine)
        dq_ref[:, index * head : (index + 1) * head] = spun.astype(BF)
    grad_k = outer_sum(grad_scores, queries)
    grad_v = outer_sum(probs.astype(BF), grads)

    @pl.when(step == 0)
    def _():
        acc[:, :head] = grad_k
        acc[:, head:] = grad_v

    @pl.when(step > 0)
    def _():
        acc[:, :head] += grad_k
        acc[:, head:] += grad_v

    @pl.when(step == pl.num_programs(0) - 1)
    def _():
        dkv_ref[...] = acc[...].astype(BF)


def attend_back_pass(size, q, kv, do, lse, positions, key_positions, cosine, sine, tile):
    count, width_q = q.shape
    heads = 2 * width_q // kv.shape[1]

    def rows(columns):
        return pl.BlockSpec((tile, columns), lambda i, s: (i, 0))

    return pl.pallas_call(
        attend_back_kernel,
        grid_spec=pltpu.PrefetchScalarGridSpec(
            num_scalar_prefetch=1,
            grid=(count // tile,),
            in_specs=[
                rows(width_q),
                held(kv),
                rows(width_q),
                pl.BlockSpec((1, heads * tile, 1), lambda i, s: (i, 0, 0)),
                rows(1),
                held(key_positions),
                rows(cosine.shape[1]),
                rows(cosine.shape[1]),
            ],
            out_specs=[rows(width_q), pl.BlockSpec(kv.shape, lambda i, s: (0, 0))],
            scratch_shapes=[pltpu.VMEM(kv.shape, F32)],
        ),
        out_shape=[jax.ShapeDtypeStruct((count, width_q), BF), jax.ShapeDtypeStruct(kv.shape, BF)],
        compiler_params=MEMORY,
        cost_estimate=FREE,
    )(size, q, kv, do, lse, positions, key_positions, cosine, sine)


def leave_kernel(x_ref, o_ref, weight_ref, gain_ref, h_ref, n_ref):
    mixed = x_ref[...].astype(F32) + matmul(o_ref[...], weight_ref[...])
    h_ref[...] = mixed
    n_ref[...] = (mixed * mean_scale(mixed) * gain_ref[...]).astype(BF)


def leave_pass(x, o, weight, gain):
    count, width = x.shape
    tile = count // 2
    return pl.pallas_call(
        leave_kernel,
        grid=(count // tile,),
        in_specs=[strip(tile, width), strip(tile, o.shape[1]), held(weight), held(gain)],
        out_specs=[strip(tile, width)] * 2,
        out_shape=[jax.ShapeDtypeStruct((count, width), d) for d in (F32, BF)],
        compiler_params=MEMORY,
        cost_estimate=FREE,
    )(x, o, weight, gain)


def norm_grad(grad, values, gain):
    scaling = mean_scale(values)
    unit = values * scaling
    lifted = grad * gain
    back = scaling * (lifted - unit * jnp.mean(lifted * unit, axis=-1, keepdims=True))
    return back, jnp.sum(grad * unit, axis=0, keepdims=True)


def add_step(ref, value):
    @pl.when(pl.program_id(0) == 0)
    def _():
        ref[...] = value

    @pl.when(pl.program_id(0) > 0)
    def _():
        ref[...] += value


def leave_back_kernel(
    one_ref, two_ref, h_ref, gain_ref, dy_ref, weight_ref, dh_ref, dz_ref, do_ref, dgain_ref
):
    grad = one_ref[...].astype(F32) + two_ref[...].astype(F32)
    back, gain_sum = norm_grad(grad, h_ref[...], gain_ref[...])
    total = dy_ref[...].astype(F32) + back
    dh_ref[...] = total
    low = total.astype(BF)
    dz_ref[...] = low
    do_ref[...] = through(low, weight_ref[...]).astype(BF)
    add_step(dgain_ref, gain_sum)


def leave_back_pass(one, two, h, gain, dy, weight):
    count, width = h.shape
    tile = count // 2
    width_q = weight.shape[0]
    return pl.pallas_call(
        leave_back_kernel,
        grid=(count // tile,),
        in_specs=[strip(tile, width)] * 3 + [held(gain), strip(tile, width), held(weight)],
        out_specs=[strip(tile, width)] * 2
        + [strip(tile, width_q), pl.BlockSpec((1, width), lambda i: (0, 0))],
        out_shape=[
            jax.ShapeDtypeStruct((count, width), F32),
            jax.ShapeDtypeStruct((count, width), BF),
            jax.ShapeDtypeStruct((count, width_q), BF),
            jax.ShapeDtypeStruct((1, width), F32),
        ],
        compiler_params=MEMORY,
        cost_estimate=FREE,
    )(one, two, h, gain, dy, weight)


def enter_back_kernel(dq_ref, *refs):
    parts = refs[:-9]
    cos_ref, sin_ref, weight_ref, x_ref, gain_ref, dh_ref, joined_ref, dx_ref, dgain_ref = refs[-9:]
    head = parts[0].shape[1] // 2
    width_q = dq_ref.shape[1]
    pair = parts[0][...].astype(F32)
    for part in parts[1:]:
        pair = pair + part[...].astype(F32)
    joined_ref[:, :width_q] = dq_ref[...]
    spun = turned(pair[:, :head], cos_ref[...], -sin_ref[...])
    joined_ref[:, width_q : width_q + head] = spun.astype(BF)
    joined_ref[:, width_q + head :] = pair[:, head:].astype(BF)
    grad = through(joined_ref[...], weight_ref[...])
    back, gain_sum = norm_grad(grad, x_ref[...].astype(F32), gain_ref[...])
    dx_ref[...] = (dh_ref[...] + back).astype(BF)
    add_step(dgain_ref, gain_sum)


def enter_back_pass(dq, parts, cosine, sine, weight, x, gain, dh):
    count, width = x.shape
    tile = count // 2
    width_q = dq.shape[1]
    return pl.pallas_call(
        enter_back_kernel,
        grid=(count // tile,),
        in_specs=[strip(tile, width_q)]
        + [strip(tile, part.shape[1]) for part in parts]
        + [strip(tile, cosine.shape[1])] * 2
        + [held(weight), strip(tile, width), held(gain), strip(tile, width)],
        out_specs=[
            strip(tile, weight.shape[1]),
            strip(tile, width),
            pl.BlockSpec((1, width), lambda i: (0, 0)),
        ],
        out_shape=[
            jax.ShapeDtypeStruct((count, weight.shape[1]), BF),
            jax.ShapeDtypeStruct((count, width), BF),
            jax.ShapeDtypeStruct((1, width), F32),
        ],
        compiler_params=MEMORY,
        cost_estimate=FREE,
    )(dq, *parts, cosine, sine, weight, x, gain, dh)


def halving_order(bits):
    order = [0]
    for bit in reversed(bits):
        order = order + [flip | bit for flip in order]
    return order


def ff_kernel(n2_ref, df_ref, wg_ref, wd_ref, a_ref, dg_ref, dn_ref):
    hidden = wd_ref.shape[0]
    n2 = n2_ref[...]
    gate = matmul(n2, wg_ref[:, :hidden])
    upper = matmul(n2, wg_ref[:, hidden:])
    grad = through(df_ref[...], wd_ref[...])
    square = gate * gate
    bent = jnp.tanh(gate * (ROOT + ROOT * CUBE * square))
    half = 0.5 + 0.5 * bent
    act = gate * half
    a_ref[...] = (act * upper).astype(BF)
    slope = half + 0.5 * gate * (1.0 - bent * bent) * (ROOT + 3.0 * ROOT * CUBE * square)
    dg_ref[:, :hidden] = (grad * upper * slope).astype(BF)
    dg_ref[:, hidden:] = (grad * act).astype(BF)
    dn_ref[...] = through(dg_ref[...], wg_ref[...]).astype(BF)


def ff_pass(n2, df, wg, wd, tile):
    count, width = n2.shape
    hidden = wd.shape[0]

    return pl.pallas_call(
        ff_kernel,
        grid=(count // tile,),
        in_specs=[strip(tile, width), strip(tile, width), held(wg), held(wd)],
        out_specs=[strip(tile, hidden), strip(tile, 2 * hidden), strip(tile, width)],
        out_shape=[
            jax.ShapeDtypeStruct((count, hidden), BF),
            jax.ShapeDtypeStruct((count, 2 * hidden), BF),
            jax.ShapeDtypeStruct((count, width), BF),
        ],
        compiler_params=MEMORY,
        cost_estimate=FREE,
    )(n2, df, wg, wd)


def blocks_of(padded, width, columns):
    across = columns // 128
    wide = width // 128
    out = []
    for r in range(padded // 16):
        for c in range(wide):
            out.append((16 * r, 128 * c, 16 * ((r * wide + c) // across), 128 * ((r * wide + c) % across)))
    return out, 16 * (-(-len(out) // across))


def tall(value, height):
    short = height - value.shape[0]
    if not short:
        return value
    return jnp.concatenate([value, jnp.zeros((short, value.shape[1]), value.dtype)], axis=0)


def deal_kernel(piece, padded, *refs):
    gateup_ref, leave_ref, out_ref = refs[0], refs[1], refs[-1]
    team, total, columns = out_ref.shape
    units, shard = gateup_ref.shape[1] // 2, columns // 2
    lines = leave_ref.shape[0]
    for in_ref, row in ((leave_ref, 0), (gateup_ref, total - gateup_ref.shape[0])):
        height = in_ref.shape[0]
        gap = jnp.zeros((height, padded - piece), in_ref.dtype)
        for half in range(2):
            for seat in range(team):
                parts = []
                for block in range(shard // padded):
                    start = half * units + (block * team + seat) * piece
                    parts += [in_ref[:, start : start + piece], gap]
                joined = jnp.concatenate(parts, axis=1)
                out_ref[seat, row : row + height, half * shard : (half + 1) * shard] = joined
    if len(refs) == 4:
        rank = refs[2].shape[1]
        for seat in range(team):
            for row in range(0, padded, 16):
                first = seat * piece + row
                value = tall(refs[2][first : first + min(16, piece - row), :], 16)
                start = row // 16 * rank
                out_ref[seat, lines : lines + 16, start : start + rank] = value


def deal_pass(arrays, team, piece, padded):
    lines = sum(array.shape[0] for array in arrays[:2]) + 16 * (len(arrays) == 3)
    columns = arrays[0].shape[1] // (team * piece) * padded
    return pl.pallas_call(
        lambda *refs: deal_kernel(piece, padded, *refs),
        out_shape=jax.ShapeDtypeStruct((team, lines, columns), BF),
        compiler_params=MEMORY,
        cost_estimate=FREE,
    )(*arrays)


def slab_kernel(padded, dealt_ref, down_ref, slab_ref, rest_ref):
    team, total, columns = dealt_ref.shape
    lines = rest_ref.shape[1]
    height = total - lines
    piece, width = down_ref.shape
    base = team * height
    for seat in range(team):
        slab_ref[seat * height : (seat + 1) * height, :] = dealt_ref[seat, lines:total, :]
        rest_ref[seat] = dealt_ref[seat, :lines, :]
    where, extra = blocks_of(padded, width, columns)
    slab_ref[base + extra - 16 : base + extra, :] = jnp.zeros((16, columns), BF)
    for r, c, row, lane in where:
        value = tall(down_ref[r : r + min(16, piece - r), c : c + 128], 16)
        slab_ref[base + row : base + row + 16, lane : lane + 128] = value


def slab_pass(dealt, down, lines, padded):
    team, total, columns = dealt.shape
    extra = blocks_of(padded, down.shape[1], columns)[1]
    return pl.pallas_call(
        lambda *refs: slab_kernel(padded, *refs),
        out_shape=[
            jax.ShapeDtypeStruct((team * (total - lines) + extra, columns), BF),
            jax.ShapeDtypeStruct((team, lines, columns), BF),
        ],
        compiler_params=MEMORY,
        cost_estimate=FREE,
    )(dealt, down)


def assemble_kernel(lines, side_ref, near_ref, far_ref, *outs):
    team = near_ref.shape[0]

    def fill(half, ref):
        for seat in range(team):
            first = (half * team + seat) * lines
            outs[0][first : first + lines, :] = ref[seat, :lines, :]
            if len(outs) == 2:
                rank = outs[1].shape[1]
                padded = outs[1].shape[0] // (2 * team)
                for row in range(0, padded, 16):
                    start = row // 16 * rank
                    first = (half * team + seat) * padded + row
                    outs[1][first : first + 16, :] = ref[
                        seat, lines : lines + 16, start : start + rank
                    ]

    for half in range(2):

        @pl.when(side_ref[0] == half)
        def _(half=half):
            fill(half, near_ref)
            fill(1 - half, far_ref)


def assemble_pass(side, near, far, lines, shard, rank):
    team, height, columns = near.shape
    shapes = [jax.ShapeDtypeStruct((2 * team * lines, columns), BF)]
    if height > lines:
        shapes.append(jax.ShapeDtypeStruct((shard, rank), BF))
    vmem = pl.BlockSpec(memory_space=pltpu.VMEM)
    return pl.pallas_call(
        lambda *refs: assemble_kernel(lines, *refs),
        in_specs=[pl.BlockSpec(memory_space=pltpu.SMEM), vmem, vmem],
        out_specs=[vmem] * len(shapes),
        out_shape=shapes,
        compiler_params=MEMORY,
        cost_estimate=FREE,
    )(side, near, far)


def fold_ff_kernel(order_ref, *refs):
    slabs = refs[:-7]
    enter_ref, leave_ref, down_enter_ref, down_leave_ref, gateup_out, down_out, blocks = refs[-7:]
    rank = leave_ref.shape[0]
    height, columns = gateup_out.shape
    shard = columns // 2
    step = pl.program_id(0)
    for index in range(2):
        start = index * shard
        lift = matmul(
            enter_ref[:, index * rank : (index + 1) * rank], leave_ref[:, start : start + shard]
        )
        for which, slab_ref in enumerate(slabs):

            @pl.when(step == which)
            def _(slab_ref=slab_ref, lift=lift, start=start):
                part = slab_ref[:height, start : start + shard].astype(F32)
                gateup_out[:, start : start + shard] = (part + lift).astype(BF)

    for which, slab_ref in enumerate(slabs):

        @pl.when(step == which)
        def _(slab_ref=slab_ref):
            blocks[...] = slab_ref[height:, :]

    lift = matmul(down_enter_ref[...], down_leave_ref[...])
    padded, width = down_out.shape
    wide = width // 128
    where, _ = blocks_of(padded, width, columns)
    for first in range(0, len(where), wide):
        r = where[first][0]
        parts = [
            blocks[row : row + 16, lane : lane + 128]
            for _, _, row, lane in where[first : first + wide]
        ]
        part = jnp.concatenate(parts, axis=1).astype(F32)
        down_out[r : r + 16, :] = (part + lift[r : r + 16]).astype(BF)


def fold_ff_pass(order, slabs, enter, leave, down_enter, down_leave, padded):
    count = len(slabs)
    columns, width = leave.shape[1], down_leave.shape[1]
    height = enter.shape[0] // count

    def own(rows, wide):
        return pl.BlockSpec((rows, wide), lambda i, o: (o[i], 0))

    return pl.pallas_call(
        fold_ff_kernel,
        grid_spec=pltpu.PrefetchScalarGridSpec(
            num_scalar_prefetch=1,
            grid=(count,),
            in_specs=[held(slab) for slab in slabs]
            + [
                own(height, enter.shape[1]),
                held(leave),
                own(padded, down_enter.shape[1]),
                held(down_leave),
            ],
            out_specs=[own(height, columns), own(padded, width)],
            scratch_shapes=[pltpu.VMEM((slabs[0].shape[0] - height, columns), BF)],
        ),
        out_shape=[
            jax.ShapeDtypeStruct((count * height, columns), BF),
            jax.ShapeDtypeStruct((count * padded, width), BF),
        ],
        compiler_params=MEMORY,
        cost_estimate=FREE,
    )(order, *slabs, enter, leave, down_enter, down_leave)


def fold_attn_kernel(bands, order_ref, *refs):
    slabs = refs[:-6]
    enter_ref, leave_ref, out_enter_ref, out_leave_ref, in_out, out_out = refs[-6:]
    rank = leave_ref.shape[0]
    height, width = in_out.shape[0], out_out.shape[1]
    step = pl.program_id(0)
    lifts = [
        matmul(enter_ref[:, i * rank : (i + 1) * rank], leave_ref[:, start : start + size])
        for i, (start, size) in enumerate(bands)
    ]
    out_lift = matmul(out_enter_ref[...], out_leave_ref[...])
    for which, slab_ref in enumerate(slabs):

        @pl.when(step == which)
        def _(slab_ref=slab_ref):
            for (start, size), lift in zip(bands, lifts):
                part = slab_ref[:height, start : start + size].astype(F32)
                in_out[:, start : start + size] = (part + lift).astype(BF)
            part = slab_ref[height:, :width].astype(F32)
            out_out[...] = (part + out_lift).astype(BF)


def fold_attn_pass(order, slabs, enter, leave, out_enter, out_leave, bands):
    count = len(slabs)
    height, short = enter.shape[0] // count, out_enter.shape[0] // count

    def own(rows, wide):
        return pl.BlockSpec((rows, wide), lambda i, o: (o[i], 0))

    return pl.pallas_call(
        lambda *refs: fold_attn_kernel(bands, *refs),
        grid_spec=pltpu.PrefetchScalarGridSpec(
            num_scalar_prefetch=1,
            grid=(count,),
            in_specs=[held(slab) for slab in slabs]
            + [
                own(height, enter.shape[1]),
                held(leave),
                own(short, out_enter.shape[1]),
                held(out_leave),
            ],
            out_specs=[own(height, leave.shape[1]), own(short, out_leave.shape[1])],
        ),
        out_shape=[
            jax.ShapeDtypeStruct((enter.shape[0], leave.shape[1]), BF),
            jax.ShapeDtypeStruct((out_enter.shape[0], out_leave.shape[1]), BF),
        ],
        compiler_params=MEMORY,
        cost_estimate=FREE,
    )(order, *slabs, enter, leave, out_enter, out_leave)


def slabs_out_kernel(order_ref, gateup_ref, down_ref, out_ref):
    height, columns = gateup_ref.shape
    padded, width = down_ref.shape
    out_ref[0, :height, :] = gateup_ref[...]
    where, extra = blocks_of(padded, width, columns)
    out_ref[0, height + extra - 16 :, :] = jnp.zeros((16, columns), BF)
    for r, c, row, lane in where:
        value = down_ref[r : r + 16, c : c + 128]
        out_ref[0, height + row : height + row + 16, lane : lane + 128] = value


def slabs_out_pass(order, gateup, down, parts):
    columns, width = gateup.shape[1], down.shape[1]
    height, padded = gateup.shape[0] // parts, down.shape[0] // parts
    rows = height + blocks_of(padded, width, columns)[1]
    count = order.shape[0]
    return pl.pallas_call(
        slabs_out_kernel,
        grid_spec=pltpu.PrefetchScalarGridSpec(
            num_scalar_prefetch=1,
            grid=(count,),
            in_specs=[
                pl.BlockSpec((height, columns), lambda i, o: (o[i], 0)),
                pl.BlockSpec((padded, width), lambda i, o: (o[i], 0)),
            ],
            out_specs=pl.BlockSpec((1, rows, columns), lambda i, o: (i, 0, 0)),
        ),
        out_shape=jax.ShapeDtypeStruct((count, rows, columns), BF),
        compiler_params=MEMORY,
        cost_estimate=FREE,
    )(order, gateup, down)


def sides_kernel(order_ref, *refs):
    enters, grad_ref = refs[:4], refs[4]
    downs = refs[5:-2]
    lines = 2 * enters[0].shape[1]
    shard = grad_ref.shape[1] // 2
    for side, out_ref in enumerate(refs[-2:]):
        team = out_ref.shape[0]
        lines = enters[0].shape[1] // team
        for half in range(2):
            value = outer_sum(
                enters[2 * half + side][...], grad_ref[:, half * shard : (half + 1) * shard]
            ).astype(BF)
            for seat in range(team):
                out_ref[seat, :lines, half * shard : (half + 1) * shard] = value[
                    seat * lines : (seat + 1) * lines
                ]
        if downs:
            value = through(downs[side][...], downs[2][...]).astype(BF)
            rank = value.shape[1]
            padded = value.shape[0] // team
            for seat in range(team):
                for row in range(0, padded, 16):
                    start = row // 16 * rank
                    first = seat * padded + row
                    out_ref[seat, lines : lines + 16, start : start + rank] = value[
                        first : first + 16
                    ]


def sides_pass(order, enter, grad, down, down_leave, team, together):
    width, columns = grad.shape
    half = enter.shape[1] // 4

    def near_or_far(rows, wide, at):
        return pl.BlockSpec((rows, wide), at)

    specs = [
        pl.BlockSpec((width, half), lambda i, o: (0, o[0])),
        pl.BlockSpec((width, half), lambda i, o: (0, o[1])),
        pl.BlockSpec((width, half), lambda i, o: (0, 2 + o[0])),
        pl.BlockSpec((width, half), lambda i, o: (0, 2 + o[1])),
        held(grad),
    ]
    arrays = [enter] * 4 + [grad]
    lines = half // team
    if together:
        lines += 16
        rows = down.shape[0] // 2
        specs += [
            pl.BlockSpec((rows, down.shape[1]), lambda i, o: (o[0], 0)),
            pl.BlockSpec((rows, down.shape[1]), lambda i, o: (o[1], 0)),
            held(down_leave),
        ]
        arrays += [down, down, down_leave]
    shape = (team, lines, columns)
    return pl.pallas_call(
        sides_kernel,
        grid_spec=pltpu.PrefetchScalarGridSpec(
            num_scalar_prefetch=1,
            grid=(1,),
            in_specs=specs,
            out_specs=[pl.BlockSpec(shape, lambda i, o: (0, 0, 0))] * 2,
        ),
        out_shape=[jax.ShapeDtypeStruct(shape, BF)] * 2,
        compiler_params=MEMORY,
        cost_estimate=FREE,
    )(order, *arrays)


def home_kernel(piece, near_ref, far_ref, mine_ref, other_ref, dealt_ref, down_ref):
    team, total, columns = dealt_ref.shape
    lines = mine_ref.shape[1]
    height = total - lines
    base = team * height
    for seat in range(team):
        rest = mine_ref[seat].astype(F32) + other_ref[seat].astype(F32)
        dealt_ref[seat, :lines, :] = rest.astype(BF)
        rows = slice(seat * height, (seat + 1) * height)
        value = near_ref[rows, :].astype(F32) + far_ref[rows, :].astype(F32)
        dealt_ref[seat, lines:total, :] = value.astype(BF)
    width = down_ref.shape[1]
    for r, c, row, lane in blocks_of(even(piece), width, columns)[0]:
        rows, lanes = slice(base + row, base + row + 16), slice(lane, lane + 128)
        value = near_ref[rows, lanes].astype(F32) + far_ref[rows, lanes].astype(F32)
        size = min(16, piece - r)
        down_ref[r : r + size, c : c + 128] = value[:size]


def home_pass(near, far, mine, other, piece, width, height):
    team, lines, columns = mine.shape
    return pl.pallas_call(
        lambda *refs: home_kernel(piece, *refs),
        out_shape=[
            jax.ShapeDtypeStruct((team, lines + height, columns), BF),
            jax.ShapeDtypeStruct((piece, width), F32),
        ],
        compiler_params=MEMORY,
        cost_estimate=FREE,
    )(near, far, mine, other)


def join_kernel(piece, padded, in_ref, *outs):
    team, total, columns = in_ref.shape
    units, shard = outs[0].shape[1] // 2, columns // 2
    lines = outs[0].shape[0]
    for out_ref, row in ((outs[0], 0), (outs[1], total - outs[1].shape[0])):
        height = out_ref.shape[0]
        for half in range(2):
            for block in range(shard // padded):
                first = half * shard + block * padded
                parts = [
                    in_ref[seat, row : row + height, first : first + piece] for seat in range(team)
                ]
                start = half * units + block * team * piece
                joined = jnp.concatenate(parts, axis=1).astype(F32)
                out_ref[:, start : start + team * piece] = joined
    if len(outs) == 3:
        rank = outs[2].shape[1]
        for seat in range(team):
            for row in range(0, padded, 16):
                size = min(16, piece - row)
                start = row // 16 * rank
                value = in_ref[seat, lines : lines + size, start : start + rank]
                first = seat * piece + row
                outs[2][first : first + size, :] = value.astype(F32)


def join_pass(parts, lines, height, piece, padded, rank):
    team, total, columns = parts.shape
    wide = columns // padded * piece * team
    shapes = [(lines, wide), (height, wide)]
    if total > lines + height:
        shapes.append((team * piece, rank))
    return pl.pallas_call(
        lambda *refs: join_kernel(piece, padded, *refs),
        out_shape=[jax.ShapeDtypeStruct(shape, F32) for shape in shapes],
        compiler_params=MEMORY,
        cost_estimate=FREE,
    )(parts)


def per_device(
    tokens,
    cotangent,
    exit_depth,
    lengths,
    loop_index,
    attn_gain,
    mlp_gain,
    qkv_weight,
    out_weight,
    gateup_weight,
    down_weight,
    qkv_enter,
    query_leave,
    kv_leave,
    out_enter,
    out_leave,
    gateup_enter,
    gateup_leave,
    down_enter,
    down_leave,
):
    loops = lax.axis_size("depth")
    rows = lax.axis_size("rows")
    group = lax.axis_index("depth")
    place = lax.axis_index("rows")
    slots, seq_dev, width = tokens.shape
    sub = rows // slots
    team = rows // 2
    count = slots * seq_dev
    teams = [[h * team + k for k in range(team)] for h in range(2)]
    seq_here, mate, core = place // sub, place % sub, place % 2
    side, seat = place // team, place % team
    levels = jnp.arange(loops, dtype=jnp.int32)

    head = kv_leave.shape[2] // 2
    width_q = query_leave.shape[2]
    rank = qkv_enter.shape[2] // 3
    hidden_units = gateup_weight.shape[1] // 2
    piece = down_weight.shape[0]
    padded = -(-piece // 16) * 16
    shard = 2 * loops * padded
    slab = width // (2 * loops)
    gain_size = attn_gain.shape[0]

    def turn(values):
        return jnp.stack(
            [values[0]] + [swap(values[f], "rows", f * sub) for f in range(1, slots)]
        )

    def deal(values):
        return lax.all_to_all(
            values, "rows", split_axis=0, concat_axis=0, axis_index_groups=teams, tiled=True
        )

    def pick(array, index):
        return array.at[index].get(mode="promise_in_bounds")

    def halve(array, bit):
        half = array.shape[0] // 2
        return array[:half], swap(array[half:], "rows", bit)

    def halve_but_last(array, bits):
        for bit in bits[:-1]:
            array = add_low(*halve(array, bit))
        return array

    def own_half(array, which):
        height = array.shape[0] // 2
        return lax.dynamic_slice(array, (which * height, 0), (height, array.shape[1]))

    def positions_of(who):
        blocks = (seq_here ^ levels) * sub + who
        return (blocks[:, None] * seq_dev + jnp.arange(seq_dev, dtype=jnp.int32)[None, :]).reshape(
            count
        )

    depth_flips = [0, 1, 2, 3]
    halves_order = jnp.stack([(group ^ f) * 2 + (core ^ e) for f in depth_flips for e in (0, 1)])
    flips = [(d, f) for d in range(4) for f in range(2)]
    slab_at = {(d, f): (group ^ d) * 2 + (side ^ f) for d, f in flips}
    team_bits, sub_bits, row_bits = bits_of(team), bits_of(sub), bits_of(rows)
    bands = [(0, width_q), (width_q, head), (width_q + head, head)]
    together = team == loops
    lines = gateup_leave.shape[1]
    with_enter = lines + 16 if together else lines

    table = loop_index.reshape(loops, loops)
    mine = lax.dynamic_index_in_dim(table, group, 0, keepdims=False)
    order = jnp.sum((mine[None, :] == levels[:, None]).astype(jnp.int32) * levels[None, :], axis=1)
    sizes_here = jnp.sum(jnp.where(table == group, lengths.reshape(loops, loops), 0), axis=1)
    size_here = lax.dynamic_slice(sizes_here, (seq_here,), (1,))
    positions = positions_of(mate)
    cosine, sine = angles(positions.astype(F32), head)
    gains = jnp.concatenate([attn_gain, mlp_gain])[None]
    gains = jnp.concatenate([gains] + [swap(gains, "depth", f) for f in depth_flips[1:]])
    gains = pick(gains, group ^ levels)
    small = [
        qkv_weight,
        qkv_enter[0],
        jnp.concatenate([query_leave[0], kv_leave[0]], axis=1),
        out_weight,
        out_enter[0],
        out_leave[0],
        gains,
    ]
    small_shapes = [array.shape for array in small]
    late = [gateup_enter[0], down_leave[0]]
    late_shapes = [array.shape for array in late]
    late_packed = pack_pass(late)
    packed = lax.all_gather(pack_pass(small), "rows", axis=0, tiled=True)
    arrived = lax.all_to_all(
        pick(tokens, order), "depth", split_axis=0, concat_axis=0, tiled=True
    )
    dealt = deal_pass(
        [gateup_weight, gateup_leave[0]] + [down_enter[0]] * together, team, piece, padded
    )
    upstream_low = turn(pick(cotangent, seq_here ^ levels)).reshape(count, width)
    arrived, dealt, upstream_low = tie(arrived, dealt, upstream_low)
    inputs = turn(pick(arrived, seq_here ^ levels)).reshape(count, width)
    dealt = deal(dealt)
    inputs, dealt, packed, upstream_low = tie(inputs, dealt, packed, upstream_low)

    slab_near, rest_near = slab_pass(dealt, down_weight, with_enter, padded)
    slab_far = swap(slab_near, "rows", team)
    (
        qkv_slab,
        full_qkv_enter,
        full_leave,
        out_slab,
        full_out_enter,
        full_out_leave,
        gain_slab,
    ) = unpack_pass(packed, small_shapes, BF)
    gain_slab = gain_slab.reshape(rows, loops, 2, -1)
    both_gains = gain_slab.transpose(2, 1, 0, 3).reshape(2, 1, width).astype(F32)
    gain_one, gain_two = both_gains[0], both_gains[1]
    spare = qkv_slab.shape[1] - width

    def both_halves(which):
        return jnp.concatenate(
            [own_half(qkv_slab, which), jnp.pad(own_half(out_slab, which), ((0, 0), (0, spare)))]
        )

    half_here = both_halves(core)
    fetched = [swap(half_here, "depth", f) for f in depth_flips[1:]]
    fetched, slab_near, slab_far, upstream_low, rest_near = tie(
        fetched, slab_near, slab_far, upstream_low, rest_near
    )
    others = swap(jnp.stack(fetched), "rows", 1)
    others, slab_near, rest_near, late_packed = tie(others, slab_near, rest_near, late_packed)
    late_packed = lax.all_gather(late_packed, "rows", axis=0, tiled=True)
    rest_far = swap(rest_near, "rows", team)
    slabs = {(0, 0): slab_near, (0, 1): slab_far}
    slabs[(1, 0)] = swap(slab_near, "depth", 1)
    slabs[(2, 0)] = swap(slab_near, "depth", 2)
    slabs[(1, 1)] = swap(slab_far, "depth", 1)
    slabs[(2, 1)] = swap(slab_far, "depth", 2)
    halves = [half_here, both_halves(core ^ 1)]
    for f in range(3):
        halves += [fetched[f], others[f]]
    qkv_eff, out_eff = fold_attn_pass(
        halves_order, halves, full_qkv_enter, full_leave, full_out_enter, full_out_leave, bands
    )
    normed_one, queries, pairs_all = enter_pass(
        inputs, gain_one, qkv_eff, cosine, sine, width_q
    )
    pairs_all, rest_far, slabs, upstream_low = tie(pairs_all, rest_far, slabs, upstream_low)
    cotan_far = swap(upstream_low, "rows", team_bits[-1])
    slabs[(3, 0)] = swap(slabs[(1, 0)], "depth", 2)
    slabs[(3, 1)] = swap(slabs[(2, 1)], "depth", 1)
    mates = [0]
    for bit in sub_bits:
        pairs_all = jnp.concatenate([pairs_all, swap(pairs_all, "rows", bit)])
        mates = mates + [f | bit for f in mates]
    key_pos = jnp.concatenate([positions_of(mate ^ f) for f in mates])[None]
    attended, log_total = attend_pass(
        size_here, queries, pairs_all, positions[:, None], key_pos, seq_dev
    )
    mixed, normed_two = leave_pass(inputs, attended, out_eff, gain_two)
    normed_two, slabs, cotan_far = tie(normed_two, slabs, cotan_far)

    def gather_team(value, far):
        value = jnp.concatenate([value, far])
        for bit in team_bits[-2::-1]:
            value = jnp.concatenate([value, swap(value, "rows", bit)])
        return value

    normed_far = swap(normed_two, "rows", team_bits[-1])
    full_gateup_enter, full_down_leave = unpack_pass(late_packed, late_shapes, BF)
    leave_full, *enter_full = assemble_pass(
        side[None], rest_near, rest_far, lines, shard, rank
    )
    if together:
        enter_full = enter_full[0]
    else:
        enter_every = lax.all_gather(down_enter[0], "rows", axis=0, tiled=True)
        enter_every = enter_every.reshape(loops, 2, team, piece, rank)
        enter_full = lax.dynamic_index_in_dim(enter_every, seat, 2, keepdims=False)
        enter_full = jnp.pad(enter_full, ((0, 0), (0, 0), (0, padded - piece), (0, 0)))
        enter_full = enter_full.reshape(shard, rank)
    gateup_eff, down_eff = fold_ff_pass(
        jnp.stack([slab_at[f] for f in flips]),
        [slabs[f] for f in flips],
        full_gateup_enter,
        leave_full,
        enter_full,
        full_down_leave,
        padded,
    )
    cotan_team = gather_team(upstream_low, cotan_far)
    normed_far, gateup_eff, down_eff, cotan_team = tie(
        normed_far, gateup_eff, down_eff, cotan_team
    )
    normed_team = gather_team(normed_two, normed_far)

    hidden, grad_expanded, grad_normed = ff_pass(
        normed_team, cotan_team, gateup_eff, down_eff, 256
    )

    grad_normed = halve_but_last(grad_normed, team_bits)
    grad_normed, hidden, grad_expanded = tie(grad_normed, hidden, grad_expanded)
    grad_terms = halve(grad_normed, team_bits[-1])
    grad_gateup = outer_sum(normed_team, grad_expanded).astype(BF)
    grad_down = outer_sum(hidden, cotan_team).astype(BF)
    grad_terms, grad_gateup, grad_down, hidden = tie(grad_terms, grad_gateup, grad_down, hidden)

    def slabs_out(*which):
        index = jnp.stack([slab_at[f] for f in which])
        return slabs_out_pass(index, grad_gateup, grad_down, 2 * loops)

    near_sent, far_sent = slabs_out((2, 0), (3, 0)), slabs_out((1, 1), (3, 1))
    near_sent, far_sent, grad_gateup, grad_down = tie(
        near_sent, far_sent, grad_gateup, grad_down
    )
    near_got = swap(near_sent, "depth", 2)
    far_got = swap(far_sent, "depth", 1)
    sides = jnp.stack([side, side ^ 1])
    side_near, side_far = sides_pass(
        sides, full_gateup_enter, grad_gateup, grad_down, full_down_leave, team, together
    )
    side_near, side_far, grad_terms, hidden = tie(side_near, side_far, grad_terms, hidden)
    side_got = swap(side_far, "rows", team)
    grad_mixed, grad_branch, grad_attended, grad_gain_second = leave_back_pass(
        *grad_terms, mixed, gain_two, upstream_low, out_eff
    )
    grad_queries, key_terms = attend_back_pass(
        size_here,
        queries,
        pairs_all,
        grad_attended,
        log_total,
        positions[:, None],
        key_pos,
        cosine,
        sine,
        seq_dev,
    )
    mate_order = halving_order(sub_bits)
    if mate_order != mates:
        key_terms = jnp.concatenate(
            [key_terms[i * count : (i + 1) * count] for i in map(mates.index, mate_order)]
        )
    outcome = matmul(hidden, down_eff).astype(BF)
    near_kept, far_kept = slabs_out((0, 0), (1, 0)), slabs_out((0, 1), (2, 1))
    key_terms, grad_queries, near_got, far_got, outcome, near_kept, far_kept, side_got = tie(
        key_terms, grad_queries, near_got, far_got, outcome, near_kept, far_kept, side_got
    )
    pair_terms = halve(halve_but_last(key_terms, sub_bits), sub_bits[-1])
    outcome = halve_but_last(outcome, team_bits)
    pair_terms, outcome = tie(pair_terms, outcome)

    grad_joined, grad_inputs, grad_gain_first = enter_back_pass(
        grad_queries, pair_terms, cosine, sine, qkv_eff, inputs, gain_one, grad_mixed
    )
    near_one, far_one = add_low(near_kept[1], near_got[1]), add_low(far_kept[1], far_got[1])
    near_one, far_one = swap(near_one, "depth", 1), swap(far_one, "depth", 2)
    outcome = halve(outcome, team_bits[-1])
    grad_qkv = outer_sum(normed_one, grad_joined).astype(BF)
    grad_out = outer_sum(attended, grad_branch).astype(BF)

    near_one, far_one, outcome, grad_inputs, grad_qkv, grad_out = tie(
        near_one, far_one, outcome, grad_inputs, grad_qkv, grad_out
    )

    def loop_part(flip):
        parts = []
        for array in (grad_qkv, grad_out):
            height = array.shape[0] // loops
            part = lax.dynamic_slice(array, ((group ^ flip) * height, 0), (height, array.shape[1]))
            parts.append(jnp.pad(part, ((0, 0), (0, grad_qkv.shape[1] - array.shape[1]))))
        return jnp.concatenate(parts)

    terms = [loop_part(0)] + [swap(loop_part(f), "depth", f) for f in depth_flips[1:]]
    near_sum = add_low(near_kept[0], near_got[0])
    far_sum = add_low(far_kept[0], far_got[0])
    result = mixed + (outcome[0].astype(F32) + outcome[1].astype(F32))
    result_low = result.astype(BF)
    near_sum, far_sum = add_low(near_sum, near_one), add_low(far_sum, far_one)
    far_sum = swap(far_sum, "rows", team)
    result_low, grad_qkv, grad_out, near_sum, far_sum, terms = tie(
        result_low, grad_qkv, grad_out, near_sum, far_sum, terms
    )

    dealt, grad_down_weight = home_pass(
        near_sum, far_sum, side_near, side_got, piece, width, slab // team
    )
    homeward = jnp.concatenate(
        [result_low.reshape(slots, seq_dev, width), grad_inputs.reshape(slots, seq_dev, width)],
        axis=1,
    )

    homeward, dealt = tie(homeward, dealt)
    homeward = turn(homeward)
    dealt = deal(dealt)
    row_place = jnp.arange(rows, dtype=jnp.int32)

    def to_owner(packed):
        return lax.psum_scatter(packed, "rows", scatter_dimension=0, tiled=True)

    qkv_rows = grad_qkv.shape[0] // loops
    rest_grads_of = [
        ((terms[0].shape[0] - qkv_rows) // rows, width),
        (grad_out.shape[0] // rows, rank),
        (rank // rows, width),
        (width // rows, rank),
        (width // rows, rank),
        (rank // rows, width),
    ]
    rest_sum = grads_pass(
        lambda *refs: rest_grads_kernel(qkv_rows, *refs),
        row_place,
        rows,
        rest_grads_of,
        [
            *terms,
            grad_out,
            full_out_enter,
            full_out_leave,
            grad_gateup,
            leave_full,
            grad_down,
            enter_full,
        ],
    )
    rest_sum = to_owner(rest_sum)
    attn_grads_of = attn_grads_shapes(rows, qkv_rows, grad_qkv, full_qkv_enter, full_leave, bands)
    attn_sum = grads_pass(
        lambda *refs: attn_grads_kernel(qkv_rows, bands, *refs),
        row_place,
        rows,
        attn_grads_of,
        [*terms, grad_qkv, full_qkv_enter, full_leave],
    )
    attn_sum = to_owner(attn_sum)
    homeward, dealt = tie(homeward, dealt)
    returned = lax.all_to_all(
        pick(homeward[:, seq_dev:], seq_here ^ levels),
        "depth",
        split_axis=0,
        concat_axis=0,
        tiled=True,
    )

    grad_tokens = pick(returned, mine)
    activations = pick(homeward[:, :seq_dev], seq_here ^ levels)
    own_out, *rest_grads = unpack_pass(
        rest_sum, rest_grads_of, F32, [[0], [1], [2], [3, 4], [5]]
    )
    own_qkv, *attn_grads = unpack_pass(
        attn_sum, attn_grads_of, F32, [[0], [1, 2, 3], [4], [5, 6]]
    )
    grad_gateup_leave, grad_gateup_weight, *grad_down_enter = join_pass(
        dealt, lines, slab // team, piece, padded, rank
    )
    if together:
        grad_down_enter = grad_down_enter[0]
    else:
        grad_down_in = through(grad_down, full_down_leave).astype(BF)
        grad_down_in = grad_down_in.reshape(loops, 2, 1, padded, rank)[:, :, :, :piece]
        spaced = jnp.zeros((loops, 2, team, piece, rank), BF)
        spaced = lax.dynamic_update_slice(spaced, grad_down_in, (0, 0, seat, 0, 0))
        grad_down_enter = lax.psum_scatter(
            spaced.reshape(hidden_units, rank), "rows", scatter_dimension=0, tiled=True
        ).astype(F32)

    block_pos = place * seq_dev + jnp.arange(seq_dev, dtype=jnp.int32)
    valid = block_pos[None, :] < sizes_here[:, None]
    counts_here = jnp.sum(
        ((exit_depth[None] == levels[:, None, None]) & valid[None]).astype(F32), axis=(1, 2)
    )
    given = inputs.astype(F32)
    cross = jnp.sum(given * result, axis=-1)
    own_sq = jnp.sum(given * given, axis=-1)
    out_sq = jnp.sum(result * result, axis=-1)
    cosines = cross * lax.rsqrt(own_sq * out_sq + 1e-06)
    cosine_here = jnp.sum(jnp.where(positions < size_here, cosines, 0.0))
    tallies = jnp.concatenate([counts_here, cosine_here[None]])
    gain_grads = jnp.concatenate([grad_gain_first, grad_gain_second])
    gain_grads = gain_grads.reshape(2, loops * rows, gain_size).transpose(1, 0, 2)
    small = jnp.concatenate(
        [
            jnp.broadcast_to(tallies[None], (loops * rows, loops + 1)),
            gain_grads.reshape(loops * rows, 2 * gain_size),
        ],
        axis=1,
    )
    small = jnp.pad(small, ((0, 0), (0, 127 - loops - 2 * gain_size)))
    small = lax.all_to_all(small, ("depth", "rows"), split_axis=0, concat_axis=0, tiled=True)
    small = jnp.sum(small, axis=0)
    tallies = small[: loops + 1]
    gain_grads = small[loops + 1 : loops + 1 + 2 * gain_size].reshape(2, gain_size)
    exit_counts = tallies[:loops].astype(jnp.int32)
    confidence = tallies[loops] / jnp.sum(lengths).astype(F32)

    return (
        activations,
        grad_tokens,
        exit_counts,
        confidence,
        gain_grads[0],
        gain_grads[1],
        own_qkv,
        own_out,
        grad_gateup_weight,
        grad_down_weight,
        attn_grads[0][None],
        attn_grads[1][None],
        attn_grads[2][None],
        rest_grads[0][None],
        rest_grads[1][None],
        rest_grads[2][None],
        grad_gateup_leave[None],
        grad_down_enter[None],
        rest_grads[3][None],
    )


def solution(mesh):
    split = P("depth", "rows", None)
    flat = P(("depth", "rows"))
    tall = P(("depth", "rows"), None)
    return jax.shard_map(
        per_device,
        mesh=mesh,
        in_specs=(split, split, P("depth", "rows"), P(), P(), flat, flat)
        + (tall,) * 4
        + (split,) * 9,
        out_specs=(split, split, P(), P(), flat, flat) + (tall,) * 4 + (split,) * 9,
        check_vma=False,
    )
```
